128 devices in a mesh: gx: 8 (over z_hi, y), gy: 4 (over z_lo, core), gz: 4 (over x).
Axes of the slice: x: 4, y: 4, z: 4 (z_hi: 2, z_lo: 2; z = z_hi * 2 + z_lo), core: 2. Of those that a mesh axis runs over, the one named last changes fastest.
Arguments:
- positions: float32 [16, 8, 8, 3, 64], P('gx', 'gy', 'gz'), may hold values from 0 to 8
- velocity: float32 [16, 8, 8, 3, 64], P('gx', 'gy', 'gz'), may hold values from -6 to 6
- atom_embed: bfloat16 [16, 8, 8, 64, 256], P('gx', 'gy', 'gz'), may hold values from -6 to 6
- embed_proj: bfloat16 [256, 256], replicated, may hold values from -0.375 to 0.375
- radial_weight: bfloat16 [8, 256], replicated, may hold values from -2 to 2
- latent_bias: float32 [256], replicated, may hold values from -3 to 3
- energy_weight: bfloat16 [256], replicated, may hold values from -0.375 to 0.375
- block_list: int32 [128, 2, 32], P(('gx', 'gy', 'gz')), may hold values from 0 to 13, as said below
- block_count: int32 [128], P(('gx', 'gy', 'gz')), may hold values from 8 to 32, as said below
- move_slot: int32 [128, 128], P(('gx', 'gy', 'gz')), may hold values from 0 to 511, as said below
- move_dest: int32 [16384, 1], P(('gx', 'gy', 'gz')), may hold values from 0 to 127; in each aligned block of 128 rows (0 to 127, 128 to 255, ...) at most 2 rows name the same one
Outputs:
- forces: float32 [16, 8, 8, 3, 64], P('gx', 'gy', 'gz')
- arrived_motion: float32 [16384, 2, 6], P(('gx', 'gy', 'gz'))
- arrived_embed: bfloat16 [16384, 2, 256], P(('gx', 'gy', 'gz'))
The draws below stay inside these ranges and needn't reach their ends.
Inputs may be any that keep to these rules, and one draw needn't show every extreme that they name: `block_list`: row 0 names a local cell below 8, row 1 an offset code below 14; no (cell, code) pair repeats within one device's list. `block_count`: some device has all 32 blocks live. `move_slot`: the slots of one device are distinct. `move_dest`: among the rows of one device at most 2 name the same owner.
All inputs are finite; a program needn't handle non-finite values.
Results may differ from the reference program's by a relative error of at most 0.0095.
Values may be sent and summed in bfloat16 or wider, within the bound.
A program may use at most 64 MiB of HBM per device.

```python
import math
import jax
import jax.numpy as jnp
import numpy as np
from jax import lax

LAT = 256
NB = 8
CELL_ATOMS = 64
MOVE_CAP = 2
CX = 2
CY = 2
CZ = 2
BLOCKS = 32
MOVE_ROWS = 128
NXC = 16
NYC = 8
NZC = 8
N_GX = 8
N_GY = 4
N_GZ = 4
DEVICES = 128


def draw_block_list(key, part):
    key = jax.random.fold_in(key, 11)
    candidates = 14 * CX * CY * CZ
    keys = jax.random.split(key, DEVICES)
    chosen = jax.vmap(lambda single: jax.random.permutation(single, candidates)[:BLOCKS])(keys)
    return jnp.stack([chosen // 14, chosen % 14], axis=1).astype(jnp.int32)


def draw_block_count(key, part):
    key = jax.random.fold_in(key, 12)
    first_key, second_key = jax.random.split(key)
    counts = jax.random.randint(first_key, (DEVICES,), BLOCKS // 4, BLOCKS + 1)
    busiest = jax.random.randint(second_key, (), 0, DEVICES)
    counts = counts.at[busiest].set(BLOCKS).at[(busiest + 1) % DEVICES].set(BLOCKS // 4)
    return counts.astype(jnp.int32)


def draw_move_slot(key, part):
    key = jax.random.fold_in(key, 13)
    keys = jax.random.split(key, DEVICES)
    chosen = jax.vmap(lambda single: jax.random.permutation(single, CX * CY * CZ * CELL_ATOMS)[:MOVE_ROWS])(keys)
    return chosen.astype(jnp.int32)


def block_levels(key, extent, shards, smallest, largest):
    factor_of = 1.0
    for axis_at, shards_of in shards:
        draws = jax.random.uniform(jax.random.fold_in(jax.random.fold_in(key, 6), axis_at), (shards_of,), jnp.float32, smallest / len(shards), largest / len(shards))
        factor_of = factor_of * jnp.repeat(jnp.exp(draws), extent[axis_at] // shards_of).reshape((-1,) + (1,) * (len(extent) - 1 - axis_at))
    return factor_of


def deal_out(rng, own, number, rows, amount, top, reach, slope):
    order = jax.random.permutation(rng, amount)
    packed, usual = shares(amount, rows * top, reach, slope, True), shares(amount, rows * top, reach, slope, False)
    places = jnp.arange(amount)

    def named(sizes, turn):
        used = int((sizes > 0).sum())
        fixed = max(1, used // 4)
        passed = fixed + (places - fixed + turn * (used - fixed)) % max(1, amount - fixed)
        return jnp.zeros((amount,), jnp.int32).at[order[jnp.where(places < fixed, places, passed)]].set(jnp.asarray(sizes, jnp.int32))

    sizes = jnp.where(number % 4 == 0, named(packed, number // 4), named(usual, number - number // 4 - 1))
    mixed = jax.random.permutation(jax.random.fold_in(own, 3), amount)
    donor, taker = mixed[0:amount // 2 * 2:2], mixed[1:amount // 2 * 2:2]
    slack = jnp.minimum(sizes[donor] - 1, reach - sizes[taker]) // 2
    slack = jnp.where((donor == order[0]) | (taker == order[0]) | (sizes[taker] == 0), 0, jnp.maximum(slack, 0))
    passed = jax.random.randint(jax.random.fold_in(own, 4), (amount // 2,), 0, 1 << 20) % (slack + 1)
    sizes = sizes.at[donor].add(-passed).at[taker].add(passed)
    members = jnp.searchsorted(jnp.cumsum(sizes), jnp.arange(rows * top), side="right").astype(jnp.int32)
    table = members.reshape(top, rows).T
    table = table[jax.random.permutation(jax.random.fold_in(own, 1), rows)]
    turn = jax.random.randint(jax.random.fold_in(own, 2), (rows, 1), 0, top)
    return jnp.take_along_axis(table, (jnp.arange(top)[None, :] + turn) % top, axis=1)


def shares(number_of, total, bound, skew, full):
    portions = [(1 << 20) // math.isqrt(standing ** skew) + 1 for standing in range(1, number_of + 1)]
    largest = bound if full else min(bound, max(-(-total // number_of), total * portions[0] // sum(portions)))
    least = 1 if total - largest >= number_of - 1 else 0
    holding, rest = [largest] + [least] * (number_of - 1), total - largest - least * (number_of - 1)
    while rest > 0:
        movable = [i for i in range(1, number_of) if holding[i] < largest] or [i for i in range(1, number_of) if holding[i] < bound]
        whole, left = sum([portions[i] for i in movable]), rest
        for i in movable:
            addition = min(bound - holding[i], max(1, left * portions[i] // whole), rest)
            holding[i] = holding[i] + addition
            rest = rest - addition
    return np.array(holding)


def bell_draw(stream_key, extent, deviation, most, cuts=(), kind=jnp.bfloat16):
    gain = block_levels(stream_key, extent, cuts, -0.22, 0.18) if cuts else 1.0
    entries = jax.random.normal(stream_key, extent, jnp.float32) * deviation * gain
    return jnp.minimum(jnp.maximum(entries, -most), most).astype(kind)


def setup_inputs(seed: int = 0) -> dict:
    arg_keys = jax.random.split(jax.random.key(seed), 12)
    positions = jnp.clip(8.0 * jax.random.uniform(arg_keys[0], (NXC, NYC, NZC, 3, CELL_ATOMS), jnp.float32) ** block_levels(arg_keys[0], (NXC, NYC, NZC, 3, CELL_ATOMS), ((0, 8), (1, 4), (2, 4)), -0.2, 0.2), 0.0, 8.0)
    velocity = bell_draw(arg_keys[1], (NXC, NYC, NZC, 3, CELL_ATOMS), 1.0, 6.0, ((0, 8), (1, 4), (2, 4)), jnp.float32)
    atom_embed = bell_draw(arg_keys[2], (NXC, NYC, NZC, CELL_ATOMS, LAT), 1.0, 6.0, ((0, 8), (1, 4), (2, 4)))
    embed_proj = bell_draw(arg_keys[3], (LAT, LAT), LAT ** -0.5, 0.375)
    radial_weight = bell_draw(arg_keys[4], (NB, LAT), NB ** -0.5, 2.0)
    latent_bias = bell_draw(arg_keys[5], (LAT,), 0.5, 3.0, (), jnp.float32)
    energy_weight = bell_draw(arg_keys[6], (LAT,), LAT ** -0.5, 0.375)
    block_list = draw_block_list(jax.random.fold_in(arg_keys[11], 71), 0)
    block_count = draw_block_count(jax.random.fold_in(arg_keys[11], 71), 0)
    move_slot = draw_move_slot(jax.random.fold_in(arg_keys[11], 71), 0)
    move_dest_keys = jax.random.split(jax.random.fold_in(arg_keys[10], 1), (DEVICES * MOVE_ROWS) // MOVE_ROWS)
    move_dest_turns = jax.random.permutation(jax.random.fold_in(arg_keys[10], 3), (DEVICES * MOVE_ROWS) // MOVE_ROWS)
    move_dest = jax.vmap(lambda own, number: deal_out(jax.random.fold_in(arg_keys[10], 2), own, number, MOVE_ROWS, DEVICES, 1, MOVE_CAP, 2))(move_dest_keys, move_dest_turns).reshape((DEVICES * MOVE_ROWS, 1))
    return {"positions": positions, "velocity": velocity, "atom_embed": atom_embed, "embed_proj": embed_proj, "radial_weight": radial_weight, "latent_bias": latent_bias, "energy_weight": energy_weight, "block_list": block_list, "block_count": block_count, "move_slot": move_slot, "move_dest": move_dest}


CELL_EDGE = 8.0
CUTOFF = 6.0
SOFTEN = 0.25
STEP = 0.5
OFFSET_TABLE = np.array([[0, 0, 0], [1, 0, 0], [0, 1, 0], [0, 0, 1], [1, 1, 0], [1, 0, 1], [0, 1, 1], [1, 1, 1], [1, 1, -1], [1, -1, 1], [-1, 1, 1], [1, -1, 0], [1, 0, -1], [0, 1, -1]], dtype=np.int32)

def block_energy(coords_a, coords_b, latent_a, latent_b, shifts, offset_code, weights, radial_weight, latent_bias, energy_weight):
    separation = coords_b[:, :, None, :] + shifts[:, :, None, None] - coords_a[:, :, :, None]
    scaled_dist = jnp.sqrt(lax.optimization_barrier(jnp.sum(separation * separation, axis=1)) + SOFTEN) / CUTOFF
    envelope = jnp.where(scaled_dist < 1.0, jnp.square(1.0 - scaled_dist * scaled_dist), 0.0)
    orders = jnp.arange(1, radial_weight.shape[0] + 1).astype(jnp.float32)
    radial_basis = jnp.sin(jnp.pi * scaled_dist[..., None] * orders).astype(jnp.bfloat16)
    preact = jnp.einsum('gijn,nl->gijl', radial_basis, radial_weight, preferred_element_type=jnp.float32)
    preact = preact + latent_a.astype(jnp.float32)[:, :, None, :] + latent_b.astype(jnp.float32)[:, None, :, :] + latent_bias
    hidden = jax.nn.silu(preact).astype(jnp.bfloat16)
    pair_energy = jnp.einsum('gijl,l->gij', hidden, energy_weight, preferred_element_type=jnp.float32) * envelope
    slot_count = coords_a.shape[2]
    upper_mask = (jnp.arange(slot_count)[:, None] < jnp.arange(slot_count)[None, :]).astype(jnp.float32)
    keep_mask = jnp.where((offset_code == 0)[:, None, None], upper_mask, 1.0) * weights[:, None, None]
    return jnp.sum(pair_energy * keep_mask)

def reference(positions, velocity, atom_embed, embed_proj, radial_weight, latent_bias, energy_weight, block_list, block_count, move_slot, move_dest):
    size_x, size_y, size_z = (positions.shape[0], positions.shape[1], positions.shape[2])
    cell_atoms = positions.shape[4]
    latent_width = atom_embed.shape[4]
    cell_total = size_x * size_y * size_z
    latent = jnp.dot(atom_embed.reshape(-1, latent_width), embed_proj, preferred_element_type=jnp.float32).astype(jnp.bfloat16)
    latent = latent.reshape(cell_total, cell_atoms, latent_width)
    flat_coords = positions.reshape(cell_total, 3, cell_atoms)
    device = jnp.arange(DEVICES).astype(jnp.int32)
    home_x = device // (N_GY * N_GZ)
    home_y = device // N_GZ % N_GY
    home_z = device % N_GZ
    owned_cell = block_list[:, 0, :]
    offset_code = block_list[:, 1, :]
    offsets = jnp.asarray(OFFSET_TABLE)[offset_code]
    first_x = home_x[:, None] * CX + owned_cell // (CY * CZ)
    first_y = home_y[:, None] * CY + owned_cell // CZ % CY
    first_z = home_z[:, None] * CZ + owned_cell % CZ
    second_x = (first_x + offsets[..., 0]) % size_x
    second_y = (first_y + offsets[..., 1]) % size_y
    second_z = (first_z + offsets[..., 2]) % size_z
    first_cell = ((first_x * size_y + first_y) * size_z + first_z).astype(jnp.int32)
    second_cell = ((second_x * size_y + second_y) * size_z + second_z).astype(jnp.int32)
    weights = (jnp.arange(BLOCKS)[None, :] < block_count[:, None]).astype(jnp.float32)
    shifts = offsets.astype(jnp.float32) * CELL_EDGE
    groups = DEVICES * BLOCKS // 8

    def visit_group(force_sum, items):
        pick_first, pick_second, pick_code, pick_weight, pick_shift = items
        grad_a, grad_b = jax.grad(block_energy, argnums=(0, 1))(flat_coords[pick_first], flat_coords[pick_second], latent[pick_first], latent[pick_second], pick_shift, pick_code, pick_weight, radial_weight, latent_bias, energy_weight)
        force_sum = force_sum.at[pick_first].add(-grad_a).at[pick_second].add(-grad_b)
        return (force_sum, None)
    scanned = lax.scan(visit_group, jnp.zeros((cell_total, 3, cell_atoms), jnp.float32), (first_cell.reshape(groups, 8), second_cell.reshape(groups, 8), offset_code.reshape(groups, 8), weights.reshape(groups, 8), shifts.reshape(groups, 8, 3)))
    forces = scanned[0].reshape(positions.shape)
    new_velocity = velocity + STEP * forces
    new_position = positions + STEP * new_velocity
    motion = jnp.concatenate([new_position, new_velocity], axis=3)
    motion = motion.reshape(N_GX, CX, N_GY, CY, N_GZ, CZ, 6, cell_atoms)
    motion = motion.transpose(0, 2, 4, 1, 3, 5, 7, 6).reshape(DEVICES, CX * CY * CZ * cell_atoms, 6)
    embeds = atom_embed.reshape(N_GX, CX, N_GY, CY, N_GZ, CZ, cell_atoms, latent_width)
    embeds = embeds.transpose(0, 2, 4, 1, 3, 5, 6, 7).reshape(DEVICES, CX * CY * CZ * cell_atoms, latent_width)
    moving_motion = jnp.take_along_axis(motion, move_slot[:, :, None], axis=1)
    moving_embed = jnp.take_along_axis(embeds, move_slot[:, :, None], axis=1)
    target = move_dest.reshape(DEVICES, MOVE_ROWS)
    row_index = jnp.arange(MOVE_ROWS)
    earlier = (target[:, :, None] == target[:, None, :]) & (row_index[None, None, :] < row_index[None, :, None])
    ranking = lax.optimization_barrier(jnp.sum(earlier.astype(jnp.int32), axis=2)).astype(jnp.int32)
    source = jnp.broadcast_to(device[:, None], target.shape)
    arrived_motion = jnp.zeros((DEVICES, DEVICES, MOVE_CAP, 6), jnp.float32).at[target, source, ranking].set(moving_motion)
    arrived_embed = jnp.zeros((DEVICES, DEVICES, MOVE_CAP, latent_width), jnp.bfloat16).at[target, source, ranking].set(moving_embed)
    return (forces, arrived_motion.reshape(DEVICES * DEVICES, MOVE_CAP, 6), arrived_embed.reshape(DEVICES * DEVICES, MOVE_CAP, latent_width))
```

```python
import functools
import jax
import jax.numpy as jnp
import numpy as np
from jax import lax
from jax.sharding import PartitionSpec as P
from jax.experimental import pallas as pl
from jax.experimental.pallas import tpu as pltpu

F32, BF16 = jnp.float32, jnp.bfloat16
OFFSETS = np.array([[0,0,0],[1,0,0],[0,1,0],[0,0,1],[1,1,0],[1,0,1],[0,1,1],[1,1,1],[1,1,-1],[1,-1,1],[-1,1,1],[1,-1,0],[1,0,-1],[0,1,-1]], np.int32)
LANES = 128
GROUP = 4
MAXCH = 32 * 32

def dot(a, b):
    return jnp.dot(a, b, preferred_element_type=F32)

def dot_nt(a, b):
    return lax.dot_general(a, b, (((1,), (1,)), ((), ())), preferred_element_type=F32)

def iota(shape, dim):
    return lax.broadcasted_iota(jnp.int32, shape, dim)

def sinpi_cospi(theta):
    m = jnp.round(theta)
    f = theta - m
    z = f * f
    sn = f * (3.14159265 + z * (-5.16771278 + z * (2.55016404 + z * (-0.599264529 + z * (0.0821458866 + z * -0.00737043094)))))
    cs = 1.0 + z * (-4.93480220 + z * (4.05871213 + z * (-1.33526277 + z * (0.235330630 + z * (-0.0258068913 + z * 0.00192957431)))))
    sign = 1.0 - 2.0 * (m - 2.0 * jnp.floor(0.5 * m))
    return sn * sign, cs * sign

def pair_kernel(blk, cnt, delta, pos, emb, projt, rb, w2, shift, out, g1, g2, rc, re, wt, acc, tab_b, tab_k, tot):
    live = cnt[0]
    def cells(b):
        a, code = blk[0, b], blk[1, b]
        first = ((a // 4 + 1) * 4 + (a // 2) % 2 + 1) * 4 + a % 2 + 1
        return first, first + delta[code], code
    jl = iota((64, 64), 1)
    il = iota((64, 64), 0)
    upper = jnp.where(il < jl, 1.0, 0.0)
    upper_b = upper.astype(BF16)
    lower_b = jnp.where(jl < il, 1.0, 0.0).astype(BF16)
    ones_b = jnp.ones((64, LANES), BF16)
    lane = iota((64, LANES), 1)

    def prepare(b):
        ca, cb, code = cells(b)
        pa, pb = pos[ca], pos[cb]
        sh = shift[code]
        pbs = pb + sh[:, :64]
        pat = jnp.transpose(pa)
        d2 = None
        for c in range(3):
            df = pbs[c:c + 1, :] - pat[:, c:c + 1]
            d2 = df * df if d2 is None else d2 + df * df
        keep = jnp.logical_and(d2 + 0.25 < 36.001, jnp.logical_or(code != 0, il < jl))
        keep = jnp.where(jnp.logical_and(keep, b < live), 1.0, 0.0)
        keep_b = keep.astype(BF16)
        counts = dot(keep_b, ones_b)
        prefix = dot(keep_b, upper_b)
        start = dot(lower_b, counts.astype(BF16))
        end = start + counts
        rc[b] = start
        re[b] = end
        local = jnp.where(keep > 0.5, prefix, 255.0)
        hi = jnp.floor(start * (1.0 / 64.0)) * 64.0
        side = jnp.where(lane == 64, hi, jnp.where(lane == 65, start - hi, 0.0))
        z = jnp.concatenate([local, side[:, 64:]], axis=1)
        zt = jnp.transpose(z)[:72]
        ah = pa.astype(BF16).astype(F32)
        bh = pb.astype(BF16).astype(F32)
        g1[b] = jnp.concatenate([zt, ah, pa - ah, jnp.zeros((8, 64), F32)], axis=0).astype(BF16)
        g2[b] = jnp.concatenate([bh, pb - bh], axis=0).astype(BF16)
        wt[b] = (dot_nt(projt[...], jnp.concatenate([emb[ca], emb[cb]], axis=0)).astype(BF16) * 0.5).astype(BF16)
        tot[b] = jnp.sum(keep).astype(jnp.int32)

    UNR = 4
    def prep_group(g, c):
        for u in range(UNR):
            prepare(g * UNR + u)
        return c
    lax.fori_loop(0, (live + UNR - 1) // UNR, prep_group, 0)

    def fill_block(b, n):
        chunks = (tot[b] + LANES - 1) // LANES
        def put(t, n):
            tab_b[n] = b
            tab_k[n] = t * LANES
            return n + 1
        return lax.fori_loop(0, chunks, put, n)
    n = lax.fori_loop(0, live, fill_block, 0)
    for u in range(GROUP):
        tab_b[n + u] = 0
        tab_k[n + u] = 1 << 20

    acc[...] = jnp.zeros_like(acc)
    kl = iota((1, LANES), 1)
    sub = iota((8, LANES), 0)
    order = (sub + 1).astype(F32)
    ones_rows = jnp.where(sub < 3, 1.0, 0.0)
    halves = iota((8, LANES), 1) < 64

    def chunk_group(g, c):
        R = range(GROUP)
        ids = [g * GROUP + u for u in R]
        bs = [tab_b[x] for x in ids]
        ks = [(kl + tab_k[x]).astype(F32) for x in ids]
        oh_i = []
        for u in R:
            hit = jnp.logical_and(ks[u] >= rc[bs[u]], ks[u] < re[bs[u]])
            oh_i.append(jnp.where(hit, 1.0, 0.0).astype(BF16))
        got = [dot(g1[bs[u]], oh_i[u]) for u in R]
        oh_j = []
        for u in R:
            want = ks[u] - got[u][64:65] - got[u][65:66]
            oh_j.append(jnp.where(got[u][:64] == want, 1.0, 0.0).astype(BF16))
        gotb = [dot(g2[bs[u]], oh_j[u]) for u in R]
        info = []
        xs = []
        for u in R:
            ca, cb, code = cells(bs[u])
            sep = (gotb[u][:8] + gotb[u][8:] + shift[code]) - (got[u][72:80] + got[u][80:88])
            sq = sep * sep
            d2 = sq[0:1] + sq[1:2] + sq[2:3]
            s = jnp.sqrt(jnp.broadcast_to(d2, (8, LANES)) + 0.25) * (1.0 / 6.0)
            sn, cs = sinpi_cospi(order * s)
            e = jnp.where(s < 1.0, 1.0 - s * s, 0.0)
            info.append((ca, cb, sep, s, e, cs * order))
            x2 = jnp.concatenate([sn, ones_rows], axis=0).astype(BF16)
            xs.append(jnp.concatenate([oh_i[u], oh_j[u], x2, jnp.zeros((112, LANES), BF16)], axis=0))
        qs = [dot(jnp.concatenate([wt[bs[u]], rb[...]], axis=1), xs[u]) for u in R]
        hd = []
        for u in R:
            q = qs[u]
            t = jnp.tanh(q)
            h = q + q * t
            d = (1.0 + t) + h * (1.0 - t)
            hd.append(jnp.concatenate([h.astype(BF16), d.astype(BF16)], axis=0))
        rs = []
        for u in range(0, GROUP, 2):
            both = dot(w2[...], jnp.concatenate([hd[u], hd[u + 1]], axis=1))
            rs += [both[:, :LANES], both[:, LANES:]]
        fs = []
        for u in R:
            ca, cb, sep, s, e, cn = info[u]
            r = rs[u]
            terms = r[:8] * cn * (np.pi * e * e) + r[8:] * (-4.0 * s * e)
            ct = jnp.sum(terms, axis=0, keepdims=True)
            f = sep * (ct / (36.0 * s))
            fh = f.astype(BF16).astype(F32)
            fs.append(jnp.concatenate([fh, f - fh], axis=0).astype(BF16))
        for u in R:
            ca, cb = info[u][:2]
            both = dot_nt(fs[u], xs[u][:128])
            part = both[:8] + both[8:]
            acc[ca] += jnp.where(halves, part, 0.0)
            acc[cb] += jnp.where(halves, 0.0, part)
        return c
    lax.fori_loop(0, (n + GROUP - 1) // GROUP, chunk_group, 0)
    out[...] = acc[:, :, :64] - acc[:, :, 64:]

def pair_forces(block_list, block_count, pos8, emb, embed_proj, radial_weight, latent_bias, energy_weight):
    n_cells = pos8.shape[0]
    rw = radial_weight.astype(F32)
    half = 0.5 * latent_bias
    b1 = half.astype(BF16)
    b2 = (half - b1.astype(F32)).astype(BF16)
    b3 = (half - b1.astype(F32) - b2.astype(F32)).astype(BF16)
    rb = jnp.concatenate([(0.5 * rw).astype(BF16), jnp.stack([b1, b2, b3]), jnp.zeros((117, 256), BF16)], axis=0).T
    ew = energy_weight.astype(F32)
    z8 = jnp.zeros((8, 256), F32)
    w2 = jnp.concatenate([
        jnp.concatenate([z8, ew[None], z8[:7]], axis=0),
        jnp.concatenate([0.5 * rw * ew[None], z8], axis=0)], axis=1).astype(BF16)
    delta = jnp.asarray((OFFSETS[:, 0] * 4 + OFFSETS[:, 1]) * 4 + OFFSETS[:, 2])
    shift = jnp.asarray(np.broadcast_to(np.pad(8.0 * OFFSETS, ((0, 0), (0, 5)))[:, :, None], (14, 8, 128)).astype(np.float32))
    smem = pl.BlockSpec(memory_space=pltpu.SMEM)
    vmem = pl.BlockSpec(memory_space=pltpu.VMEM)
    return pl.pallas_call(
        pair_kernel,
        out_shape=jax.ShapeDtypeStruct((n_cells, 8, 64), F32),
        in_specs=[smem] * 3 + [vmem] * 6,
        out_specs=vmem,
        scratch_shapes=[
            pltpu.VMEM((32, 96, 64), BF16),
            pltpu.VMEM((32, 16, 64), BF16),
            pltpu.VMEM((32, 64, LANES), F32),
            pltpu.VMEM((32, 64, LANES), F32),
            pltpu.VMEM((32, 256, 128), BF16),
            pltpu.VMEM((n_cells, 8, LANES), F32),
            pltpu.SMEM((MAXCH + GROUP,), jnp.int32),
            pltpu.SMEM((MAXCH + GROUP,), jnp.int32),
            pltpu.SMEM((32,), jnp.int32),
        ],
        compiler_params=pltpu.CompilerParams(vmem_limit_bytes=48 * 1024 * 1024),
    )(block_list, block_count, delta, pos8, emb, embed_proj.T, rb, w2, shift)

MOVE_CAP = 2
STEP = 0.5


def padded(value, sides, width):
    for axis, dim in sides:
        size, length = (lax.axis_size(axis), value.shape[dim])
        up = [(i, (i + 1) % size) for i in range(size)]
        down = [(j, i) for i, j in up]
        last = lax.slice_in_dim(value, length - width, length, axis=dim)
        initial = lax.slice_in_dim(value, 0, width, axis=dim)
        before = lax.ppermute(last, axis, up)
        after = lax.ppermute(initial, axis, down)
        value = jnp.concatenate([before, value, after], axis=dim)
    return value


def fold_rim(gathered, axis_dim, span):
    core_part = lax.slice_in_dim(gathered, 2, span + 2, axis=axis_dim)
    lower_rim = lax.slice_in_dim(gathered, 0, 1, axis=axis_dim)
    upper_rim = lax.slice_in_dim(gathered, span + 3, span + 4, axis=axis_dim)
    low_pad = [(0, 0)] * gathered.ndim
    high_pad = [(0, 0)] * gathered.ndim
    low_pad[axis_dim] = (0, span - 1)
    high_pad[axis_dim] = (span - 1, 0)
    return core_part + jnp.pad(lower_rim, low_pad) + jnp.pad(upper_rim, high_pad)


def per_device(
    positions,
    velocity,
    atom_embed,
    embed_proj,
    radial_weight,
    latent_bias,
    energy_weight,
    block_list,
    block_count,
    move_slot,
    move_dest,
):
    span_x, span_y, span_z = (positions.shape[0], positions.shape[1], positions.shape[2])
    cell_atoms = positions.shape[4]
    latent_width = atom_embed.shape[4]
    padded_coords = padded(positions, (("gx", 0), ("gy", 1), ("gz", 2)), 1)
    arriving = padded(atom_embed, (("gx", 0), ("gy", 1), ("gz", 2)), 1)
    cells = 4 * 4 * 4
    pos8 = jnp.pad(padded_coords.reshape(cells, 3, cell_atoms), ((0, 0), (0, 5), (0, 0)))
    force_sum = pair_forces(block_list[0], block_count, pos8, arriving.reshape(cells, cell_atoms, latent_width), embed_proj, radial_weight, latent_bias, energy_weight)
    padded_force = force_sum[:, :3].reshape(span_x + 2, span_y + 2, span_z + 2, 3, cell_atoms)
    gathered = padded(
        padded_force.astype(jnp.bfloat16), (("gx", 0), ("gy", 1), ("gz", 2)), 1
    ).astype(padded_force.dtype)
    forces = fold_rim(fold_rim(fold_rim(gathered, 0, span_x), 1, span_y), 2, span_z)
    new_velocity = velocity + STEP * forces
    new_position = positions + STEP * new_velocity
    motion = jnp.concatenate([new_position, new_velocity], axis=3).reshape(-1, 6, cell_atoms)
    slot_list = move_slot[0]
    moving_motion = motion[slot_list // cell_atoms, :, slot_list % cell_atoms]
    moving_embed = atom_embed.reshape(-1, latent_width)[slot_list].astype(jnp.float32)
    target = move_dest[:, 0]
    device_total = lax.axis_size(("gx", "gy", "gz"))
    row_index = jnp.arange(target.shape[0])
    earlier = (target[:, None] == target[None, :]) & (row_index[None, :] < row_index[:, None])
    ranking = jnp.sum(earlier.astype(jnp.int32), axis=1)
    place_index = target * MOVE_CAP + ranking
    send_motion = (
        jnp.zeros((device_total * MOVE_CAP, 6), jnp.float32)
        .at[place_index]
        .set(moving_motion)
        .reshape(device_total, MOVE_CAP, 6)
    )
    send_embed = (
        jnp.zeros((device_total * MOVE_CAP, latent_width), jnp.float32)
        .at[place_index]
        .set(moving_embed)
        .reshape(device_total, MOVE_CAP, latent_width)
    )
    got_embed, got_motion = (
        lax.all_to_all(
            send_embed.astype(jnp.bfloat16),
            ("gx", "gy", "gz"),
            split_axis=0,
            concat_axis=0,
            tiled=True,
        ).astype(send_embed.dtype),
        lax.all_to_all(
            send_motion.astype(jnp.bfloat16),
            ("gx", "gy", "gz"),
            split_axis=0,
            concat_axis=0,
            tiled=True,
        ).astype(send_motion.dtype),
    )
    return (forces, got_motion, got_embed.astype(jnp.bfloat16))


def solution(mesh):
    placed = (
        P("gx", "gy", "gz", None, None),
        P("gx", "gy", "gz", None, None),
        P("gx", "gy", "gz", None, None),
        P(),
        P(),
        P(),
        P(),
        P(("gx", "gy", "gz"), None, None),
        P(("gx", "gy", "gz")),
        P(("gx", "gy", "gz"), None),
        P(("gx", "gy", "gz"), None),
    )
    return jax.shard_map(
        per_device,
        mesh=mesh,
        in_specs=placed,
        out_specs=(
            P("gx", "gy", "gz", None, None),
            P(("gx", "gy", "gz"), None, None),
            P(("gx", "gy", "gz"), None, None),
        ),
        check_vma=False,
    )
```

```python
import functools

import jax
import jax.numpy as jnp
import numpy as np
from jax import lax
from jax.experimental import pallas as pl
from jax.experimental.pallas import tpu as pltpu
from jax.sharding import PartitionSpec as P

F32, BF16 = jnp.float32, jnp.bfloat16
MESH = pl.DeviceIdType.MESH
OFFSETS = np.array([[0, 0, 0], [1, 0, 0], [0, 1, 0], [0, 0, 1], [1, 1, 0], [1, 0, 1], [0, 1, 1], [1, 1, 1], [1, 1, -1], [1, -1, 1], [-1, 1, 1], [1, -1, 0], [1, 0, -1], [0, 1, -1]], np.int32)
LANES = 128
GROUP = 4
MAXCH = 32 * 32
SIZES = (8, 4, 4)


def ghost_boxes():
    need = {}
    for a in np.ndindex(2, 2, 2):
        for o in OFFSETS:
            b = [int(x) for x in np.array(a) + o]
            s = tuple(-1 if x < 0 else (1 if x > 1 else 0) for x in b)
            if any(s):
                need.setdefault(s, []).append([x - 2 * y for x, y in zip(b, s)])
    boxes = []
    for s in sorted(need, key=lambda s: (-len(set(map(tuple, need[s]))), s)):
        own = [(min(c[d] for c in need[s]), max(c[d] for c in need[s]) + 1) for d in range(3)]
        boxes.append((s, own, [(lo + 2 * s[d] + 1, hi + 2 * s[d] + 1) for d, (lo, hi) in enumerate(own)]))
    return boxes


BOXES = ghost_boxes()
N_BOX = len(BOXES)


def box(ref, ranges):
    return ref.at[tuple(pl.ds(lo, hi - lo) for lo, hi in ranges)]


def dot(a, b):
    return jnp.dot(a, b, preferred_element_type=F32)


def dot_nt(a, b):
    return lax.dot_general(a, b, (((1,), (1,)), ((), ())), preferred_element_type=F32)


def iota(shape, dim):
    return lax.broadcasted_iota(jnp.int32, shape, dim)


def position():
    return tuple(lax.axis_index(a) for a in ("gx", "gy", "gz"))


def shifted(me, s, sign):
    return tuple(lax.rem(m + sign * d + n, n) if d else m for m, d, n in zip(me, s, SIZES))


def enter(me, toward):
    barrier = pltpu.get_barrier_semaphore()
    for s, _, _ in BOXES:
        pl.semaphore_signal(barrier, inc=1, device_id=shifted(me, s, toward), device_id_type=MESH)
    for k in range(1, 16):
        pl.semaphore_signal(barrier, inc=1, device_id=plane_partner(me, k)[0], device_id_type=MESH)
    for k in range(1, 8):
        pl.semaphore_signal(barrier, inc=1, device_id=line_partner(me, k)[0], device_id_type=MESH)
    pl.semaphore_wait(barrier, N_BOX + 15 + 7)


def plane_partner(me, k):
    at = lax.rem(me[1] * 4 + me[2] + k, 16)
    return (me[0], at // 4, lax.rem(at, 4)), at


def line_partner(me, k):
    at = lax.rem(me[0] + k, 8)
    return (at, me[1], me[2]), at


def exchange(me, partner, count, rows, src, dst, send_sem, recv_sem):
    copies = []
    mine = me[0] if count == 8 else me[1] * 4 + me[2]
    here = pl.ds(pl.multiple_of(mine * rows, rows), rows)
    for k in range(1, count):
        device, at = partner(me, k)
        copy = pltpu.make_async_remote_copy(
            src_ref=src.at[pl.ds(pl.multiple_of(at * rows, rows), rows)],
            dst_ref=dst.at[here],
            send_sem=send_sem.at[k],
            recv_sem=recv_sem.at[k],
            device_id=device,
            device_id_type=MESH,
        )
        copy.start()
        copies.append(copy)
    dst[here] = src[here]
    return copies


def wait_all(copies):
    for copy in copies:
        copy.wait()


def placement(dest, ranks_apart):
    dest_f = dest.astype(F32)
    col = jnp.broadcast_to(dest_f, (128, LANES))
    row = jnp.transpose(col)
    earlier = jnp.logical_and(col == row, iota((128, 128), 1) < iota((128, 128), 0))
    rank = jnp.sum(jnp.where(earlier, 1.0, 0.0), axis=1, keepdims=True)
    gx = jnp.floor(dest_f * (1.0 / 16.0))
    order = (dest_f - 16.0 * gx) * 8.0 + gx
    place = order + 128.0 * rank if ranks_apart else 2.0 * order + rank
    lanes = iota((128, 256), 1).astype(F32)
    return jnp.where(lanes == place, 1.0, 0.0).astype(BF16)


def halo_kernel(pos, emb, slot, dest, gpos, gemb, arrived, emb_v, send1, recv1, send2, recv2, es, er, ps, pr, loc, s1, r1, s2, r2):
    me = position()
    own = [(1, 3)] * 3
    local = [
        pltpu.make_async_copy(emb, emb_v, loc.at[0]),
        pltpu.make_async_copy(emb, box(gemb, own), loc.at[1]),
        pltpu.make_async_copy(pos, box(gpos, own), loc.at[2]),
    ]
    for copy in local:
        copy.start()
    enter(me, 1)
    halo = []
    for i, (s, src, dst) in enumerate(BOXES):
        device = shifted(me, s, -1)
        for a, b, x, y in ((pos, gpos, ps, pr), (emb, gemb, es, er)):
            copy = pltpu.make_async_remote_copy(src_ref=box(a, src), dst_ref=box(b, dst), send_sem=x.at[i], recv_sem=y.at[i], device_id=device, device_id_type=MESH)
            copy.start()
            halo.append(copy)
    where = placement(dest[...], False)
    slots = slot[...]
    pick = jnp.where(iota((512, 128), 0) == slots, 1.0, 0.0).astype(BF16)
    place = lax.dot_general(where, pick, (((0,), (1,)), ((), ())), preferred_element_type=F32).astype(BF16)
    local[0].wait()
    rows = emb_v[...].reshape(512, 256)
    send1[...] = dot(place, rows).astype(BF16)
    wait_all(exchange(me, plane_partner, 16, 16, send1, recv1, s1, r1))
    out = iota((256, 256), 0)
    want = ((out // 2) % 16) * 16 + (out // 32) * 2 + out % 2
    perm = jnp.where(iota((256, 256), 1) == want, 1.0, 0.0).astype(BF16)
    send2[...] = dot(perm, recv1[...]).astype(BF16)
    wait_all(exchange(me, line_partner, 8, 32, send2, recv2, s2, r2))
    arrived[...] = recv2[...]
    local[1].wait()
    local[2].wait()
    wait_all(halo)


def return_kernel(fsum, pos, vel, slot, dest, forces, arrived, landed, mot, send1, recv1, send2, recv2, fs, fr, s1, r1, s2, r2):
    me = position()
    enter(me, -1)
    back = []
    for i, (s, own, ghost) in enumerate(BOXES):
        copy = pltpu.make_async_remote_copy(src_ref=box(fsum, ghost), dst_ref=box(landed.at[i], own), send_sem=fs.at[i], recv_sem=fr.at[i], device_id=shifted(me, s, 1), device_id_type=MESH)
        copy.start()
        back.append(copy)
    where = placement(dest[...], True)
    pick = jnp.where(iota((512, 128), 0) == slot[...], 1.0, 0.0).astype(BF16)
    place = dot(pick, where).astype(BF16)
    out = iota((128, 128), 0)
    perm = jnp.where(iota((128, 128), 1) == (out % 16) * 8 + out // 16, 1.0, 0.0).astype(BF16)
    mot[...] = jnp.zeros_like(mot)
    wait_all(back)
    for c in np.ndindex(2, 2, 2):
        total = fsum[c[0] + 1, c[1] + 1, c[2] + 1]
        for i, (s, own, ghost) in enumerate(BOXES):
            if all(lo <= x < hi for x, (lo, hi) in zip(c, own)):
                total = total + landed[i, c[0], c[1], c[2]]
        forces[c[0], c[1], c[2]] = total
        new_velocity = vel[c[0], c[1], c[2]] + 0.5 * total[:3]
        new_position = pos[c[0], c[1], c[2]] + 0.5 * new_velocity
        at = (c[0] * 4 + c[1] * 2 + c[2]) * 64
        mot[0:3, at:at + 64] = new_position
        mot[8:11, at:at + 64] = new_velocity
    rows = dot(mot[...].astype(BF16), place)
    tall = jnp.concatenate([rows[:, :128], rows[:, 128:], jnp.zeros((96, 128), F32)], axis=0)
    send1[...] = jnp.transpose(tall)
    wait_all(exchange(me, plane_partner, 16, 8, send1, recv1, s1, r1))
    send2[...] = dot(perm, recv1[...].astype(BF16))
    wait_all(exchange(me, line_partner, 8, 16, send2, recv2, s2, r2))
    arrived[...] = recv2[...]


def sinpi_cospi(theta):
    m = jnp.round(theta)
    f = theta - m
    z = f * f
    sn = f * (3.14159265 + z * (-5.16771278 + z * (2.55016404 + z * (-0.599264529 + z * (0.0821458866 + z * -0.00737043094)))))
    cs = 1.0 + z * (-4.93480220 + z * (4.05871213 + z * (-1.33526277 + z * (0.235330630 + z * (-0.0258068913 + z * 0.00192957431)))))
    sign = 1.0 - 2.0 * (m - 2.0 * jnp.floor(0.5 * m))
    return sn * sign, cs * sign


def pair_kernel(blk, cnt, delta, gpos, gemb, proj, rw, bias, ew, shift, out, pos, g1, g2, rc, re, wt, projt, rb, w2, acc, tab_b, tab_k, tot):
    live = cnt[0]

    def cells(b):
        a, code = blk[0, 0, b], blk[0, 1, b]
        first = ((a // 4 + 1) * 4 + (a // 2) % 2 + 1) * 4 + a % 2 + 1
        return first, first + delta[code], code

    jl = iota((64, 64), 1)
    il = iota((64, 64), 0)
    upper_b = jnp.where(il < jl, 1.0, 0.0).astype(BF16)
    lower_b = jnp.where(jl < il, 1.0, 0.0).astype(BF16)
    ones_b = jnp.ones((64, LANES), BF16)
    lane = iota((64, LANES), 1)

    pos[...] = jnp.zeros_like(pos)
    pos[:, 0:3, :] = gpos[...].reshape(64, 3, 64)
    projt[...] = jnp.transpose(proj[...])
    half = 0.5 * bias[...]
    b1 = half.astype(BF16).astype(F32)
    b2 = (half - b1).astype(BF16).astype(F32)
    row8 = iota((8, 256), 0)
    biases = jnp.where(row8 == 0, b1, jnp.where(row8 == 1, b2, jnp.where(row8 == 2, half - b1 - b2, 0.0)))
    rwf = rw[...].astype(F32)
    ewf = ew[...].astype(F32)
    rb[...] = jnp.transpose(jnp.concatenate([0.5 * rwf, biases, jnp.zeros((112, 256), F32)], axis=0)).astype(BF16)
    z8 = jnp.zeros((8, 256), F32)
    w2[:, :256] = jnp.concatenate([z8, jnp.where(row8 == 0, ewf, 0.0)], axis=0).astype(BF16)
    w2[:, 256:] = jnp.concatenate([0.5 * rwf * ewf, z8], axis=0).astype(BF16)

    def prepare(b):
        ca, cb, code = cells(b)
        pa, pb = pos[ca], pos[cb]
        pbs = pb + shift[code][:, :64]
        pat = jnp.transpose(pa)
        d2 = None
        for c in range(3):
            df = pbs[c:c + 1, :] - pat[:, c:c + 1]
            d2 = df * df if d2 is None else d2 + df * df
        keep = jnp.logical_and(d2 + 0.25 < 36.001, jnp.logical_or(code != 0, il < jl))
        keep = jnp.where(jnp.logical_and(keep, b < live), 1.0, 0.0)
        keep_b = keep.astype(BF16)
        counts = dot(keep_b, ones_b)
        prefix = dot(keep_b, upper_b)
        start = dot(lower_b, counts.astype(BF16))
        rc[b] = start
        re[b] = start + counts
        local = jnp.where(keep > 0.5, prefix, 255.0)
        hi = jnp.floor(start * (1.0 / 64.0)) * 64.0
        side = jnp.where(lane == 64, hi, jnp.where(lane == 65, start - hi, 0.0))
        zt = jnp.transpose(jnp.concatenate([local, side[:, 64:]], axis=1))[:72]
        ah = pa.astype(BF16).astype(F32)
        bh = pb.astype(BF16).astype(F32)
        g1[b] = jnp.concatenate([zt, ah, pa - ah, jnp.zeros((8, 64), F32)], axis=0).astype(BF16)
        g2[b] = jnp.concatenate([bh, pb - bh], axis=0).astype(BF16)
        both = jnp.concatenate([gemb[ca], gemb[cb]], axis=0)
        wt[b] = (dot_nt(projt[...], both).astype(BF16) * 0.5).astype(BF16)
        tot[b] = jnp.sum(keep).astype(jnp.int32)

    unroll = 4

    def prep_group(g, c):
        for u in range(unroll):
            prepare(g * unroll + u)
        return c

    lax.fori_loop(0, (live + unroll - 1) // unroll, prep_group, 0)

    def fill_block(b, n):
        def put(t, n):
            tab_b[n] = b
            tab_k[n] = t * LANES
            return n + 1

        return lax.fori_loop(0, (tot[b] + LANES - 1) // LANES, put, n)

    n = lax.fori_loop(0, live, fill_block, 0)
    for u in range(GROUP):
        tab_b[n + u] = 0
        tab_k[n + u] = 1 << 20

    acc[...] = jnp.zeros_like(acc)
    kl = iota((1, LANES), 1)
    sub = iota((8, LANES), 0)
    order = (sub + 1).astype(F32)
    ones_rows = jnp.where(sub < 3, 1.0, 0.0)
    halves = iota((8, LANES), 1) < 64

    def chunk_group(g, c):
        R = range(GROUP)
        ids = [g * GROUP + u for u in R]
        bs = [tab_b[x] for x in ids]
        ks = [(kl + tab_k[x]).astype(F32) for x in ids]
        oh_i = []
        for u in R:
            hit = jnp.logical_and(ks[u] >= rc[bs[u]], ks[u] < re[bs[u]])
            oh_i.append(jnp.where(hit, 1.0, 0.0).astype(BF16))
        got = [dot(g1[bs[u]], oh_i[u]) for u in R]
        oh_j = []
        for u in R:
            want = ks[u] - got[u][64:65] - got[u][65:66]
            oh_j.append(jnp.where(got[u][:64] == want, 1.0, 0.0).astype(BF16))
        gotb = [dot(g2[bs[u]], oh_j[u]) for u in R]
        info = []
        xs = []
        for u in R:
            ca, cb, code = cells(bs[u])
            sep = (gotb[u][:8] + gotb[u][8:] + shift[code]) - (got[u][72:80] + got[u][80:88])
            sq = sep * sep
            d2 = sq[0:1] + sq[1:2] + sq[2:3]
            s = jnp.sqrt(jnp.broadcast_to(d2, (8, LANES)) + 0.25) * (1.0 / 6.0)
            sn, cs = sinpi_cospi(order * s)
            e = jnp.where(s < 1.0, 1.0 - s * s, 0.0)
            info.append((ca, cb, sep, s, e, cs * order))
            x2 = jnp.concatenate([sn, ones_rows], axis=0).astype(BF16)
            xs.append(jnp.concatenate([oh_i[u], oh_j[u], x2, jnp.zeros((112, LANES), BF16)], axis=0))
        qs = [dot(jnp.concatenate([wt[bs[u]], rb[...]], axis=1), xs[u]) for u in R]
        hd = []
        for u in R:
            q = qs[u]
            t = jnp.tanh(q)
            h = q + q * t
            d = (1.0 + t) + h * (1.0 - t)
            hd.append(jnp.concatenate([h.astype(BF16), d.astype(BF16)], axis=0))
        rs = []
        for u in range(0, GROUP, 2):
            both = dot(w2[...], jnp.concatenate([hd[u], hd[u + 1]], axis=1))
            rs += [both[:, :LANES], both[:, LANES:]]
        fs = []
        for u in R:
            ca, cb, sep, s, e, cn = info[u]
            r = rs[u]
            terms = r[:8] * cn * (np.pi * e * e) + r[8:] * (-4.0 * s * e)
            ct = jnp.sum(terms, axis=0, keepdims=True)
            f = sep * (ct / (36.0 * s))
            fh = f.astype(BF16).astype(F32)
            fs.append(jnp.concatenate([fh, f - fh], axis=0).astype(BF16))
        for u in R:
            ca, cb = info[u][:2]
            both = dot_nt(fs[u], xs[u][:128])
            part = both[:8] + both[8:]
            acc[ca] += jnp.where(halves, part, 0.0)
            acc[cb] += jnp.where(halves, 0.0, part)
        return c

    lax.fori_loop(0, (n + GROUP - 1) // GROUP, chunk_group, 0)
    out[...] = (acc[:, :, :64] - acc[:, :, 64:]).reshape(4, 4, 4, 8, 64)


def pair_forces(block_list, block_count, gpos, gemb, embed_proj, radial_weight, latent_bias, energy_weight):
    delta = jnp.asarray((OFFSETS[:, 0] * 4 + OFFSETS[:, 1]) * 4 + OFFSETS[:, 2])
    shift = jnp.asarray(np.broadcast_to(np.pad(8.0 * OFFSETS, ((0, 0), (0, 5)))[:, :, None], (14, 8, 128)).astype(np.float32))
    smem = pl.BlockSpec(memory_space=pltpu.SMEM)
    vmem = pl.BlockSpec(memory_space=pltpu.VMEM)
    return pl.pallas_call(
        pair_kernel,
        out_shape=jax.ShapeDtypeStruct((4, 4, 4, 8, 64), F32),
        in_specs=[smem] * 3 + [vmem] * 7,
        out_specs=vmem,
        scratch_shapes=[
            pltpu.VMEM((64, 8, 64), F32),
            pltpu.VMEM((32, 96, 64), BF16),
            pltpu.VMEM((32, 16, 64), BF16),
            pltpu.VMEM((32, 64, LANES), F32),
            pltpu.VMEM((32, 64, LANES), F32),
            pltpu.VMEM((32, 256, 128), BF16),
            pltpu.VMEM((256, 256), BF16),
            pltpu.VMEM((256, 128), BF16),
            pltpu.VMEM((16, 512), BF16),
            pltpu.VMEM((64, 8, LANES), F32),
            pltpu.SMEM((MAXCH + GROUP,), jnp.int32),
            pltpu.SMEM((MAXCH + GROUP,), jnp.int32),
            pltpu.SMEM((32,), jnp.int32),
        ],
        compiler_params=pltpu.CompilerParams(vmem_limit_bytes=48 * 1024 * 1024),
        name="pairs",
    )(block_list, block_count, delta, gpos, gemb.reshape(64, 64, 256), embed_proj, radial_weight, latent_bias.reshape(1, 256), energy_weight.reshape(1, 256), shift)


def per_device(positions, velocity, atom_embed, embed_proj, radial_weight, latent_bias, energy_weight, block_list, block_count, move_slot, move_dest):
    any_, vmem, smem = (pl.BlockSpec(memory_space=m) for m in (pl.ANY, pltpu.VMEM, pltpu.SMEM))
    dma = pltpu.SemaphoreType.DMA
    gpos, gemb, got_embed = pl.pallas_call(
        halo_kernel,
        out_shape=(jax.ShapeDtypeStruct((4, 4, 4, 3, 64), F32), jax.ShapeDtypeStruct((4, 4, 4, 64, 256), BF16), jax.ShapeDtypeStruct((256, 256), BF16)),
        in_specs=[any_, any_, vmem, vmem],
        out_specs=(any_, any_, vmem),
        scratch_shapes=[pltpu.VMEM((2, 2, 2, 64, 256), BF16)] + [pltpu.VMEM((256, 256), BF16)] * 4
        + [dma((N_BOX,))] * 4 + [dma((3,))] + [dma((16,))] * 2 + [dma((8,))] * 2,
        compiler_params=pltpu.CompilerParams(collective_id=0, has_side_effects=True, vmem_limit_bytes=32 * 1024 * 1024),
        name="halo",
    )(positions, atom_embed, move_slot, move_dest)
    fsum = pair_forces(block_list, block_count, gpos, gemb, embed_proj, radial_weight, latent_bias, energy_weight)
    forces, moved = pl.pallas_call(
        return_kernel,
        out_shape=(jax.ShapeDtypeStruct((2, 2, 2, 8, 64), F32), jax.ShapeDtypeStruct((128, LANES), F32)),
        in_specs=[vmem] * 5,
        out_specs=(vmem, vmem),
        scratch_shapes=[pltpu.VMEM((N_BOX, 2, 2, 2, 8, 64), F32), pltpu.VMEM((16, 512), F32)] + [pltpu.VMEM((128, LANES), F32)] * 4
        + [dma((N_BOX,))] * 2 + [dma((16,))] * 2 + [dma((8,))] * 2,
        compiler_params=pltpu.CompilerParams(collective_id=1, has_side_effects=True, vmem_limit_bytes=32 * 1024 * 1024),
        name="give_back",
    )(fsum, positions, velocity, move_slot, move_dest)
    motion = moved[:, :32].reshape(128, 2, 2, 8)[..., :3].reshape(128, 2, 6)
    return forces[..., :3, :], motion, got_embed.reshape(128, 2, 256)


def solution(mesh):
    placed = (
        P("gx", "gy", "gz", None, None),
        P("gx", "gy", "gz", None, None),
        P("gx", "gy", "gz", None, None),
        P(),
        P(),
        P(),
        P(),
        P(("gx", "gy", "gz"), None, None),
        P(("gx", "gy", "gz")),
        P(("gx", "gy", "gz"), None),
        P(("gx", "gy", "gz"), None),
    )
    return jax.shard_map(
        per_device,
        mesh=mesh,
        in_specs=placed,
        out_specs=(
            P("gx", "gy", "gz", None, None),
            P(("gx", "gy", "gz"), None, None),
            P(("gx", "gy", "gz"), None, None),
        ),
        check_vma=False,
    )
```

```python
import functools

import jax
import jax.numpy as jnp
import numpy as np
from jax import lax
from jax.experimental import pallas as pl
from jax.experimental.pallas import tpu as pltpu
from jax.sharding import PartitionSpec as P

F32, BF16 = jnp.float32, jnp.bfloat16
MESH = pl.DeviceIdType.MESH
OFFSETS = np.array([[0, 0, 0], [1, 0, 0], [0, 1, 0], [0, 0, 1], [1, 1, 0], [1, 0, 1], [0, 1, 1], [1, 1, 1], [1, 1, -1], [1, -1, 1], [-1, 1, 1], [1, -1, 0], [1, 0, -1], [0, 1, -1]], np.int32)
LANES = 128
GROUP = 12
MAXCH = 32 * 32
SIZES = (8, 4, 4)


def ghost_boxes():
    need = {}
    for a in np.ndindex(2, 2, 2):
        for o in OFFSETS:
            b = [int(x) for x in np.array(a) + o]
            s = tuple(-1 if x < 0 else (1 if x > 1 else 0) for x in b)
            if any(s):
                need.setdefault(s, []).append([x - 2 * y for x, y in zip(b, s)])
    boxes = []
    for s in sorted(need, key=lambda s: (-len(set(map(tuple, need[s]))), s)):
        own = [(min(c[d] for c in need[s]), max(c[d] for c in need[s]) + 1) for d in range(3)]
        boxes.append((s, own, [(lo + 2 * s[d] + 1, hi + 2 * s[d] + 1) for d, (lo, hi) in enumerate(own)]))
    return boxes


BOXES = ghost_boxes()
N_BOX = len(BOXES)


def box(ref, ranges):
    return ref.at[tuple(pl.ds(lo, hi - lo) for lo, hi in ranges)]


def dot(a, b):
    return jnp.dot(a, b, preferred_element_type=F32)


def dot_nt(a, b):
    return lax.dot_general(a, b, (((1,), (1,)), ((), ())), preferred_element_type=F32)


def iota(shape, dim):
    return lax.broadcasted_iota(jnp.int32, shape, dim)


def position():
    return tuple(lax.axis_index(a) for a in ("gx", "gy", "gz"))


def shifted(me, s, sign):
    return tuple(lax.rem(m + sign * d + n, n) if d else m for m, d, n in zip(me, s, SIZES))


def greet(me, toward, line):
    barrier = pltpu.get_barrier_semaphore()
    for s, _, _ in BOXES:
        pl.semaphore_signal(barrier, inc=1, device_id=shifted(me, s, toward), device_id_type=MESH)
    for k in range(1, 16):
        pl.semaphore_signal(barrier, inc=1, device_id=plane_partner(me, k)[0], device_id_type=MESH)
    for k in range(1, 8 if line else 1):
        pl.semaphore_signal(barrier, inc=1, device_id=line_partner(me, k)[0], device_id_type=MESH)
    return N_BOX + 15 + (7 if line else 0)


def plane_partner(me, k):
    at = lax.rem(me[1] * 4 + me[2] + k, 16)
    return (me[0], at // 4, lax.rem(at, 4)), at


def line_partner(me, k):
    at = lax.rem(me[0] + k, 8)
    return (at, me[1], me[2]), at


def exchange(me, partner, count, rows, src, dst, send_sem, recv_sem):
    copies = []
    mine = me[0] if count == 8 else me[1] * 4 + me[2]
    here = pl.ds(pl.multiple_of(mine * rows, rows), rows)
    for k in range(1, count):
        device, at = partner(me, k)
        copy = pltpu.make_async_remote_copy(
            src_ref=src.at[pl.ds(pl.multiple_of(at * rows, rows), rows)],
            dst_ref=dst.at[here],
            send_sem=send_sem.at[k],
            recv_sem=recv_sem.at[k],
            device_id=device,
            device_id_type=MESH,
        )
        copy.start()
        copies.append(copy)
    dst[here] = src[here]
    return copies


def wait_all(copies):
    for copy in copies:
        copy.wait()


def placement(dest, ranks_apart):
    dest_f = dest.astype(F32)
    row = jnp.broadcast_to(dest_f, (128, LANES))
    col = jnp.transpose(row)
    earlier = jnp.logical_and(col == row, iota((128, 128), 1) < iota((128, 128), 0))
    rank = jnp.sum(jnp.where(earlier, 1.0, 0.0), axis=1, keepdims=True)
    dest_c = col[:, :1]
    gx = jnp.floor(dest_c * (1.0 / 16.0))
    order = (dest_c - 16.0 * gx) * 8.0 + gx
    place = order + 128.0 * rank if ranks_apart else 2.0 * order + rank
    lanes = iota((128, 256), 1).astype(F32)
    return jnp.where(lanes == place, 1.0, 0.0).astype(BF16)


def offset_of(code):
    out = []
    for d in range(3):
        v = 0
        for c, o in enumerate(OFFSETS):
            if o[d]:
                v = v + jnp.where(code == c, int(o[d]), 0)
        out.append(v)
    return out


def shift_rows(code, lanes):
    x, y, z = [(8 * v).astype(F32) for v in offset_of(code)]
    row = iota((8, lanes), 0)
    return jnp.where(row == 0, x, jnp.where(row == 1, y, jnp.where(row == 2, z, 0.0)))


def pair_cells(blk, b):
    a, code = blk[0, 0, b], blk[0, 1, b]
    x, y, z = offset_of(code)
    first = ((a // 4 + 1) * 4 + (a // 2) % 2 + 1) * 4 + a % 2 + 1
    return first, first + (x * 4 + y) * 4 + z, code


def halo_kernel(pos_in, emb, slot, dest, blk_in, proj, rw, bias, ew, cnt, gemb, held, g1, g2, rc, projt, rb, w2, blk, tot,
                pos, pos_v, emb_v, slot_v, dest_v, proj_v, rw_v, bias_v, ew_v, send1, recv1, loc, es, er, ps, pr, s1, r1):
    me = position()
    barrier = pltpu.get_barrier_semaphore()
    pos[...] = jnp.zeros_like(pos)
    partners = greet(me, 1, False)
    own = [(1, 3)] * 3
    local = []
    for i, (x, y) in enumerate(((pos_in, pos_v), (emb, emb_v), (slot, slot_v), (dest, dest_v), (blk_in, blk), (proj, proj_v), (rw, rw_v), (bias, bias_v), (ew, ew_v), (emb, box(gemb, own)))):
        local.append(pltpu.make_async_copy(x, y, loc.at[i]))
        local[-1].start()
    local[0].wait()
    for c in np.ndindex(2, 2, 2):
        pos[c[0] + 1, c[1] + 1, c[2] + 1, 0:3] = pos_v[c[0], c[1], :, c[2], :]
    pl.semaphore_wait(barrier, partners)
    halo = []
    for a, b, x, y in ((pos, pos, ps, pr), (emb, gemb, es, er)):
        copies = []
        for i, (s, src, dst) in enumerate(BOXES):
            start = box(a, [(lo + 1, hi + 1) for lo, hi in src]) if a is pos else box(a, src)
            copies.append(pltpu.make_async_remote_copy(src_ref=start, dst_ref=box(b, dst), send_sem=x.at[i], recv_sem=y.at[i], device_id=shifted(me, s, -1), device_id_type=MESH))
            copies[-1].start()
        halo.append(copies)
    for copy in local[1:]:
        copy.wait()
    where = placement(dest_v[...], False)
    pick = jnp.where(iota((512, 128), 0) == slot_v[...], 1.0, 0.0).astype(BF16)
    place = lax.dot_general(where, pick, (((0,), (1,)), ((), ())), preferred_element_type=F32).astype(BF16)
    send1[...] = dot(place, emb_v[...].reshape(512, 256)).astype(BF16)
    rows = exchange(me, plane_partner, 16, 16, send1, recv1, s1, r1)
    projt[...] = jnp.transpose(proj_v[...])
    half = 0.5 * bias_v[...]
    b1 = half.astype(BF16).astype(F32)
    b2 = (half - b1).astype(BF16).astype(F32)
    row8 = iota((8, 256), 0)
    biases = jnp.where(row8 == 0, b1, jnp.where(row8 == 1, b2, jnp.where(row8 == 2, half - b1 - b2, 0.0)))
    rwf = rw_v[...].astype(F32)
    ewf = ew_v[...].astype(F32).reshape(1, 256)
    rb[...] = jnp.transpose(jnp.concatenate([0.5 * rwf, biases, jnp.zeros((112, 256), F32)], axis=0)).astype(BF16)
    z8 = jnp.zeros((8, 256), F32)
    w2[:, :256] = jnp.concatenate([z8, jnp.where(row8 == 0, ewf, 0.0)], axis=0).astype(BF16)
    w2[:, 256:] = jnp.concatenate([0.5 * rwf * ewf, z8], axis=0).astype(BF16)

    jl = iota((64, 64), 1)
    il = iota((64, 64), 0)
    upper_b = jnp.where(il < jl, 1.0, 0.0).astype(BF16)
    lower_b = jnp.where(jl < il, 1.0, 0.0).astype(BF16)
    ones_b = jnp.ones((64, LANES), BF16)
    lane = iota((64, LANES), 1)

    def pos_at(c):
        return pos[c // 16, c // 4 % 4, c % 4]

    def prepare(b):
        ca, cb, code = pair_cells(blk, b)
        pa, pb = pos_at(ca), pos_at(cb)
        pbs = pb + shift_rows(code, 64)
        pat = jnp.transpose(pa)
        d2 = None
        for c in range(3):
            df = pbs[c:c + 1, :] - pat[:, c:c + 1]
            d2 = df * df if d2 is None else d2 + df * df
        keep = jnp.logical_and(d2 + 0.25 < 36.001, jnp.logical_or(code != 0, il < jl))
        keep = jnp.where(jnp.logical_and(keep, b < cnt[0]), 1.0, 0.0)
        keep_b = keep.astype(BF16)
        counts = dot(keep_b, ones_b)
        prefix = dot(keep_b, upper_b)
        start = dot(lower_b, counts.astype(BF16))
        rc[b, 0:64] = start
        rc[b, 64:72] = jnp.broadcast_to(start[63:64] + counts[63:64], (8, LANES))
        local = jnp.where(keep > 0.5, prefix, 255.0)
        hi = jnp.floor(start * (1.0 / 64.0)) * 64.0
        side = jnp.where(lane == 64, hi, jnp.where(lane == 65, start - hi, 0.0))
        zt = jnp.transpose(jnp.concatenate([local, side[:, 64:]], axis=1))[:72]
        ah = pa.astype(BF16).astype(F32)
        bh = pb.astype(BF16).astype(F32)
        g1[b] = jnp.concatenate([zt, ah, pa - ah, jnp.zeros((8, 64), F32)], axis=0).astype(BF16)
        g2[b] = jnp.concatenate([bh, pb - bh], axis=0).astype(BF16)
        tot[b] = jnp.sum(keep).astype(jnp.int32)
    wait_all(halo[0])

    def prep_group(g, c):
        for u in range(4):
            prepare(g * 4 + u)
        return c

    lax.fori_loop(0, 8, prep_group, 0)
    wait_all(rows)
    held[...] = recv1[...]
    wait_all(halo[1])


def sinpi_cospi(theta):
    m = jnp.round(theta)
    f = theta - m
    z = f * f
    sn = f * (3.14159265 + z * (-5.16771278 + z * (2.55016404 + z * (-0.599264529 + z * (0.0821458866 + z * -0.00737043094)))))
    cs = 1.0 + z * (-4.93480220 + z * (4.05871213 + z * (-1.33526277 + z * (0.235330630 + z * (-0.0258068913 + z * 0.00192957431)))))
    sign = 1.0 - 2.0 * (m - 2.0 * jnp.floor(0.5 * m))
    return sn * sign, cs * sign


def pair_kernel(blk, cnt, tot, gemb, g1, g2, rc, projt, rb, w2, out, wt, acc, tab_b, tab_k):
    def project(g, c):
        for u in range(4):
            ca, cb, _ = pair_cells(blk, g * 4 + u)
            both = jnp.concatenate([gemb[ca], gemb[cb]], axis=0)
            wt[g * 4 + u] = (dot_nt(projt[...], both).astype(BF16) * 0.5).astype(BF16)
        return c

    lax.fori_loop(0, (cnt[0] + 3) // 4, project, 0)

    def fill_block(b, n):
        def put(t, n):
            tab_b[n] = b
            tab_k[n] = t * LANES
            return n + 1

        return lax.fori_loop(0, (tot[b] + LANES - 1) // LANES, put, n)

    n = lax.fori_loop(0, cnt[0], fill_block, 0)
    for u in range(GROUP):
        tab_b[n + u] = 0
        tab_k[n + u] = 1 << 20

    acc[...] = jnp.zeros_like(acc)
    kl = iota((1, LANES), 1)
    sub = iota((8, LANES), 0)
    order = (sub + 1).astype(F32)
    ones_rows = jnp.where(sub < 3, 1.0, 0.0)
    halves = iota((8, LANES), 1) < 64

    def chunk_group(g, c):
        R = range(GROUP)
        ids = [g * GROUP + u for u in R]
        bs = [tab_b[x] for x in ids]
        ks = [(kl + tab_k[x]).astype(F32) for x in ids]
        oh_i = []
        for u in R:
            hit = jnp.logical_and(ks[u] >= rc[bs[u], 0:64], ks[u] < rc[bs[u], 1:65])
            oh_i.append(jnp.where(hit, 1.0, 0.0).astype(BF16))
        got = [dot(g1[bs[u]], oh_i[u]) for u in R]
        oh_j = []
        for u in R:
            want = ks[u] - got[u][64:65] - got[u][65:66]
            oh_j.append(jnp.where(got[u][:64] == want, 1.0, 0.0).astype(BF16))
        gotb = [dot(g2[bs[u]], oh_j[u]) for u in R]
        info = []
        xs = []
        for u in R:
            ca, cb, code = pair_cells(blk, bs[u])
            sep = (gotb[u][:8] + gotb[u][8:] + shift_rows(code, LANES)) - (got[u][72:80] + got[u][80:88])
            sq = sep * sep
            d2 = sq[0:1] + sq[1:2] + sq[2:3]
            s = jnp.sqrt(jnp.broadcast_to(d2, (8, LANES)) + 0.25) * (1.0 / 6.0)
            sn, cs = sinpi_cospi(order * s)
            e = jnp.where(s < 1.0, 1.0 - s * s, 0.0)
            info.append((ca, cb, sep, s, e, cs * order))
            x2 = jnp.concatenate([sn, ones_rows], axis=0).astype(BF16)
            xs.append(jnp.concatenate([oh_i[u], oh_j[u], x2, jnp.zeros((112, LANES), BF16)], axis=0))
        qs = [dot(jnp.concatenate([wt[bs[u]], rb[...]], axis=1), xs[u]) for u in R]
        hd = []
        for u in R:
            q = qs[u]
            t = jnp.tanh(q)
            h = q + q * t
            d = (1.0 + t) + h * (1.0 - t)
            hd.append(jnp.concatenate([h.astype(BF16), d.astype(BF16)], axis=0))
        rs = []
        for u in range(0, GROUP, 2):
            both = dot(w2[...], jnp.concatenate([hd[u], hd[u + 1]], axis=1))
            rs += [both[:, :LANES], both[:, LANES:]]
        fs = []
        for u in R:
            ca, cb, sep, s, e, cn = info[u]
            r = rs[u]
            terms = r[:8] * cn * (np.pi * e * e) + r[8:] * (-4.0 * s * e)
            ct = jnp.sum(terms, axis=0, keepdims=True)
            f = sep * (ct / (36.0 * s))
            fh = f.astype(BF16).astype(F32)
            fs.append(jnp.concatenate([fh, f - fh], axis=0).astype(BF16))
        for u in R:
            ca, cb = info[u][:2]
            both = dot_nt(fs[u], xs[u][:128])
            part = both[:8] + both[8:]
            acc[ca] += jnp.where(halves, part, 0.0)
            acc[cb] += jnp.where(halves, 0.0, part)
        return c

    lax.fori_loop(0, (n + GROUP - 1) // GROUP, chunk_group, 0)
    out[...] = (acc[:, :, :64] - acc[:, :, 64:]).reshape(4, 4, 4, 8, 64)


def return_kernel(fsum, pos_in, vel_in, slot, dest, held, forces, moved, embeds, pos_v, vel_v, slot_v, dest_v, landed, mot, send1, recv1, send2, recv2, esend, erecv, loc, fs, fr, s1, r1, s2, r2, s3, r3):
    me = position()
    barrier = pltpu.get_barrier_semaphore()
    partners = greet(me, -1, True)
    local = []
    for i, (x, y) in enumerate(((pos_in, pos_v), (vel_in, vel_v), (slot, slot_v), (dest, dest_v))):
        local.append(pltpu.make_async_copy(x, y, loc.at[i]))
        local[-1].start()
    mot[...] = jnp.zeros_like(mot)
    out = iota((256, 256), 0)
    want = ((out // 2) % 16) * 16 + (out // 32) * 2 + out % 2
    perm2 = jnp.where(iota((256, 256), 1) == want, 1.0, 0.0).astype(BF16)
    esend[...] = dot(perm2, held[...]).astype(BF16)
    out = iota((128, 128), 0)
    perm = jnp.where(iota((128, 128), 1) == (out % 16) * 8 + out // 16, 1.0, 0.0).astype(BF16)
    pl.semaphore_wait(barrier, partners)
    back = []
    for i, (s, own, ghost) in enumerate(BOXES):
        copy = pltpu.make_async_remote_copy(src_ref=box(fsum, ghost), dst_ref=box(landed.at[i], own), send_sem=fs.at[i], recv_sem=fr.at[i], device_id=shifted(me, s, 1), device_id_type=MESH)
        copy.start()
        back.append(copy)
    rows_sent = exchange(me, line_partner, 8, 32, esend, erecv, s3, r3)
    wait_all(local)
    where = placement(dest_v[...], True)
    pick = jnp.where(iota((512, 128), 0) == slot_v[...], 1.0, 0.0).astype(BF16)
    place = dot(pick, where).astype(BF16)
    wait_all(back)
    for c in np.ndindex(2, 2, 2):
        total = fsum[c[0] + 1, c[1] + 1, c[2] + 1]
        for i, (s, own, ghost) in enumerate(BOXES):
            if all(lo <= x < hi for x, (lo, hi) in zip(c, own)):
                total = total + landed[i, c[0], c[1], c[2]]
        forces[c[0], c[1], c[2]] = total
        new_velocity = vel_v[c[0], c[1], :, c[2], :] + 0.5 * total[:3]
        new_position = pos_v[c[0], c[1], :, c[2], :] + 0.5 * new_velocity
        at = (c[0] * 4 + c[1] * 2 + c[2]) * 64
        mot[0:3, at:at + 64] = new_position
        mot[8:11, at:at + 64] = new_velocity
    rows = dot(mot[...].astype(BF16), place)
    tall = jnp.concatenate([rows[:, :128], rows[:, 128:], jnp.zeros((96, 128), F32)], axis=0)
    send1[...] = jnp.transpose(tall)
    wait_all(exchange(me, plane_partner, 16, 8, send1, recv1, s1, r1))
    send2[...] = dot(perm, recv1[...].astype(BF16))
    last = exchange(me, line_partner, 8, 16, send2, recv2, s2, r2)
    wait_all(rows_sent)
    embeds[...] = erecv[...]
    wait_all(last)
    moved[...] = jnp.transpose(recv2[...])[:32]


def finish_kernel(forces, moved, embeds, forces_out, motion_out, embeds_out):
    for c in np.ndindex(2, 2, 2):
        forces_out[c[0], c[1], :, c[2], :] = forces[c[0], c[1], c[2]][:3]
    for v in range(6):
        for h in range(2):
            at = 16 * h + 8 * (v // 3) + v % 3
            motion_out[v, h:h + 1, :] = moved[at:at + 1, :]
    embeds_out[...] = embeds[...].reshape(128, 2, 256)


def per_device(positions, velocity, atom_embed, embed_proj, radial_weight, latent_bias, energy_weight, block_list, block_count, move_slot, move_dest):
    any_, vmem, smem, hbm = (pl.BlockSpec(memory_space=m) for m in (pl.ANY, pltpu.VMEM, pltpu.SMEM, pltpu.HBM))
    dma = pltpu.SemaphoreType.DMA
    array = jax.ShapeDtypeStruct
    pos_rows, vel_rows = (x.transpose(0, 1, 3, 2, 4) for x in (positions, velocity))
    dest_row = move_dest.reshape(1, 128)
    spaces = pltpu.VMEM((2, 2, 3, 2, 64), F32)
    gemb, held, g1, g2, rc, projt, rb, w2, blk, tot = pl.pallas_call(
        halo_kernel,
        out_shape=(
            array((4, 4, 4, 64, 256), BF16),
            array((256, 256), BF16),
            array((32, 96, 64), BF16),
            array((32, 16, 64), BF16),
            array((32, 72, LANES), F32),
            array((256, 256), BF16),
            array((256, 128), BF16),
            array((16, 512), BF16),
            array((1, 2, 32), jnp.int32),
            array((32,), jnp.int32),
        ),
        in_specs=[hbm] * 9 + [smem],
        out_specs=(any_,) + (vmem,) * 7 + (smem,) * 2,
        scratch_shapes=[
            pltpu.VMEM((4, 4, 4, 8, 64), F32),
            spaces,
            pltpu.VMEM((2, 2, 2, 64, 256), BF16),
            pltpu.VMEM((1, 128), jnp.int32),
            pltpu.VMEM((1, 128), jnp.int32),
            pltpu.VMEM((256, 256), BF16),
            pltpu.VMEM((8, 256), BF16),
            pltpu.VMEM((1, 256), F32),
            pltpu.VMEM((256,), BF16),
            pltpu.VMEM((256, 256), BF16),
            pltpu.VMEM((256, 256), BF16),
        ]
        + [dma((10,))] + [dma((N_BOX,))] * 4 + [dma((16,))] * 2,
        compiler_params=pltpu.CompilerParams(collective_id=0, has_side_effects=True, vmem_limit_bytes=16 * 1024 * 1024),
        name="halo",
    )(*(pltpu.with_memory_space_constraint(x, pltpu.HBM) for x in (pos_rows, atom_embed, move_slot, dest_row, block_list, embed_proj, radial_weight, latent_bias.reshape(1, 256), energy_weight)), block_count)
    fsum = pl.pallas_call(
        pair_kernel,
        out_shape=array((4, 4, 4, 8, 64), F32),
        in_specs=[smem] * 3 + [vmem] * 7,
        out_specs=vmem,
        scratch_shapes=[
            pltpu.VMEM((32, 256, 128), BF16),
            pltpu.VMEM((64, 8, LANES), F32),
            pltpu.SMEM((MAXCH + GROUP,), jnp.int32),
            pltpu.SMEM((MAXCH + GROUP,), jnp.int32),
        ],
        compiler_params=pltpu.CompilerParams(vmem_limit_bytes=24 * 1024 * 1024),
        name="pairs",
    )(blk, block_count, tot, gemb.reshape(64, 64, 256), g1, g2, rc, projt, rb, w2)
    raw = pl.pallas_call(
        return_kernel,
        out_shape=(array((2, 2, 2, 8, 64), F32), array((32, LANES), F32), array((256, 256), BF16)),
        in_specs=[vmem] + [hbm] * 4 + [vmem],
        out_specs=(vmem,) * 3,
        scratch_shapes=[spaces, spaces, pltpu.VMEM((1, 128), jnp.int32), pltpu.VMEM((1, 128), jnp.int32)]
        + [pltpu.VMEM((N_BOX, 2, 2, 2, 8, 64), F32), pltpu.VMEM((16, 512), F32)]
        + [pltpu.VMEM((128, LANES), F32)] * 4
        + [pltpu.VMEM((256, 256), BF16)] * 2
        + [dma((4,))] + [dma((N_BOX,))] * 2 + [dma((16,))] * 2 + [dma((8,))] * 4,
        compiler_params=pltpu.CompilerParams(collective_id=1, has_side_effects=True, vmem_limit_bytes=16 * 1024 * 1024),
        name="give_back",
    )(fsum, *(pltpu.with_memory_space_constraint(x, pltpu.HBM) for x in (pos_rows, vel_rows, move_slot, dest_row)), held)
    forces, motion, embeds = pl.pallas_call(
        finish_kernel,
        out_shape=(array((2, 2, 3, 2, 64), F32), array((6, 2, 128), F32), array((128, 2, 256), BF16)),
        in_specs=[vmem] * 3,
        out_specs=(vmem,) * 3,
        name="finish",
    )(*raw)
    return forces.transpose(0, 1, 3, 2, 4), motion.transpose(2, 1, 0), embeds


def solution(mesh):
    placed = (
        P("gx", "gy", "gz", None, None),
        P("gx", "gy", "gz", None, None),
        P("gx", "gy", "gz", None, None),
        P(),
        P(),
        P(),
        P(),
        P(("gx", "gy", "gz"), None, None),
        P(("gx", "gy", "gz")),
        P(("gx", "gy", "gz"), None),
        P(("gx", "gy", "gz"), None),
    )
    return jax.shard_map(
        per_device,
        mesh=mesh,
        in_specs=placed,
        out_specs=(
            P("gx", "gy", "gz", None, None),
            P(("gx", "gy", "gz"), None, None),
            P(("gx", "gy", "gz"), None, None),
        ),
        check_vma=False,
    )
```

```python
import functools

import jax
import jax.numpy as jnp
import numpy as np
from jax import lax
from jax.experimental import pallas as pl
from jax.experimental.pallas import tpu as pltpu
from jax.sharding import PartitionSpec as P

F32, BF16 = jnp.float32, jnp.bfloat16
MESH = pl.DeviceIdType.MESH
OFFSETS = np.array([[0, 0, 0], [1, 0, 0], [0, 1, 0], [0, 0, 1], [1, 1, 0], [1, 0, 1], [0, 1, 1], [1, 1, 1], [1, 1, -1], [1, -1, 1], [-1, 1, 1], [1, -1, 0], [1, 0, -1], [0, 1, -1]], np.int32)
LANES = 128
GROUP = 12
CHUNK = 128
MAXCH = 32 * 32
SIZES = (8, 4, 4)


def ghost_boxes():
    need = {}
    for a in np.ndindex(2, 2, 2):
        for o in OFFSETS:
            b = [int(x) for x in np.array(a) + o]
            s = tuple(-1 if x < 0 else (1 if x > 1 else 0) for x in b)
            if any(s):
                need.setdefault(s, []).append([x - 2 * y for x, y in zip(b, s)])
    boxes = []
    for s in sorted(need, key=lambda s: (-s[0], -len(set(map(tuple, need[s]))), s)):
        own = [(min(c[d] for c in need[s]), max(c[d] for c in need[s]) + 1) for d in range(3)]
        boxes.append((s, own, [(lo + 2 * s[d] + 1, hi + 2 * s[d] + 1) for d, (lo, hi) in enumerate(own)]))
    return boxes


BOXES = ghost_boxes()
N_BOX = len(BOXES)


def box(ref, ranges):
    return ref.at[tuple(pl.ds(lo, hi - lo) for lo, hi in ranges)]


def dot(a, b):
    return jnp.dot(a, b, preferred_element_type=F32)


def dot_nt(a, b):
    return lax.dot_general(a, b, (((1,), (1,)), ((), ())), preferred_element_type=F32)


def iota(shape, dim):
    return lax.broadcasted_iota(jnp.int32, shape, dim)


def position():
    return tuple(lax.axis_index(a) for a in ("gx", "gy", "gz"))


def shifted(me, s, sign):
    return tuple(lax.rem(m + sign * d + n, n) if d else m for m, d, n in zip(me, s, SIZES))


def greet(me, toward, line):
    barrier = pltpu.get_barrier_semaphore()
    for s, _, _ in BOXES:
        pl.semaphore_signal(barrier, inc=1, device_id=shifted(me, s, toward), device_id_type=MESH)
    for k in range(1, 16):
        pl.semaphore_signal(barrier, inc=1, device_id=plane_partner(me, k)[0], device_id_type=MESH)
    for k in range(1, 8 if line else 1):
        pl.semaphore_signal(barrier, inc=1, device_id=line_partner(me, k)[0], device_id_type=MESH)
    return N_BOX + 15 + (7 if line else 0)


def plane_partner(me, k):
    at = lax.rem(me[1] * 4 + me[2] + k, 16)
    return (me[0], at // 4, lax.rem(at, 4)), at


def line_partner(me, k):
    at = lax.rem(me[0] + k, 8)
    return (at, me[1], me[2]), at


def exchange(me, partner, count, rows, src, dst, send_sem, recv_sem):
    copies = []
    mine = me[0] if count == 8 else me[1] * 4 + me[2]
    here = pl.ds(pl.multiple_of(mine * rows, rows), rows)
    for k in range(1, count):
        device, at = partner(me, k)
        copy = pltpu.make_async_remote_copy(
            src_ref=src.at[pl.ds(pl.multiple_of(at * rows, rows), rows)],
            dst_ref=dst.at[here],
            send_sem=send_sem.at[k],
            recv_sem=recv_sem.at[k],
            device_id=device,
            device_id_type=MESH,
        )
        copy.start()
        copies.append(copy)
    dst[here] = src[here]
    return copies


def wait_all(copies):
    for copy in copies:
        copy.wait()


def placement(dest, ranks_apart):
    dest_f = dest.astype(F32)
    row = jnp.broadcast_to(dest_f, (128, LANES))
    col = jnp.transpose(row)
    earlier = jnp.logical_and(col == row, iota((128, 128), 1) < iota((128, 128), 0))
    rank = jnp.sum(jnp.where(earlier, 1.0, 0.0), axis=1, keepdims=True)
    dest_c = col[:, :1]
    gx = jnp.floor(dest_c * (1.0 / 16.0))
    order = (dest_c - 16.0 * gx) * 8.0 + gx
    place = order + 128.0 * rank if ranks_apart else 2.0 * order + rank
    lanes = iota((128, 256), 1).astype(F32)
    return jnp.where(lanes == place, 1.0, 0.0).astype(BF16)


def shift_rows(offset, lanes):
    x, y, z = [(8 * v).astype(F32) for v in offset]
    row = iota((8, lanes), 0)
    return jnp.where(row == 0, x, jnp.where(row == 1, y, jnp.where(row == 2, z, 0.0)))


def halo_kernel(pos_in, emb, slot, dest, blk_in, proj, rw, bias, ew, cnt, gemb, held, g1, g2, rc, projt, rb, w2, plan, tot,
                pos, pos_v, emb_v, slot_v, dest_v, proj_v, rw_v, bias_v, ew_v, send1, recv1, blk, offs, loc, es, er, ps, pr, s1, r1):
    me = position()
    barrier = pltpu.get_barrier_semaphore()
    pos[...] = jnp.zeros_like(pos)
    for c, o in enumerate(OFFSETS):
        for d in range(3):
            offs[d, c] = int(o[d])
    partners = greet(me, 1, False)
    own = [(1, 3)] * 3
    local = []
    for i, (x, y) in enumerate(((pos_in, pos_v), (emb, emb_v), (slot, slot_v), (dest, dest_v), (blk_in, blk), (proj, proj_v), (rw, rw_v), (bias, bias_v), (ew, ew_v), (emb, box(gemb, own)))):
        local.append(pltpu.make_async_copy(x, y, loc.at[i]))
        local[-1].start()
    local[0].wait()
    for c in np.ndindex(2, 2, 2):
        pos[c[0] + 1, c[1] + 1, c[2] + 1, 0:3, 0:64] = pos_v[c[0], c[1], :, c[2], :]
    pl.semaphore_wait(barrier, partners)
    halo = []
    for a, b, x, y in ((pos, pos, ps, pr), (emb, gemb, es, er)):
        copies = []
        for i, (s, src, dst) in enumerate(BOXES):
            start = box(a, [(lo + 1, hi + 1) for lo, hi in src]) if a is pos else box(a, src)
            copies.append(pltpu.make_async_remote_copy(src_ref=start, dst_ref=box(b, dst), send_sem=x.at[i], recv_sem=y.at[i], device_id=shifted(me, s, -1), device_id_type=MESH))
            copies[-1].start()
        halo.append(copies)
    for copy in local[1:]:
        copy.wait()
    where = placement(dest_v[...], False)
    pick = jnp.where(iota((512, 128), 0) == slot_v[...], 1.0, 0.0).astype(BF16)
    place = lax.dot_general(where, pick, (((0,), (1,)), ((), ())), preferred_element_type=F32).astype(BF16)
    send1[...] = dot(place, emb_v[...].reshape(512, 256)).astype(BF16)
    rows = exchange(me, plane_partner, 16, 16, send1, recv1, s1, r1)
    projt[...] = jnp.transpose(proj_v[...])
    half = 0.5 * bias_v[...]
    b1 = half.astype(BF16).astype(F32)
    b2 = (half - b1).astype(BF16).astype(F32)
    row8 = iota((8, 256), 0)
    biases = jnp.where(row8 == 0, b1, jnp.where(row8 == 1, b2, jnp.where(row8 == 2, half - b1 - b2, 0.0)))
    rwf = rw_v[...].astype(F32)
    ewf = ew_v[...].astype(F32).reshape(1, 256)
    rb[...] = jnp.transpose(jnp.concatenate([0.5 * rwf, biases, jnp.zeros((112, 256), F32)], axis=0)).astype(BF16)
    z8 = jnp.zeros((8, 256), F32)
    w2[:, :256] = jnp.concatenate([z8, jnp.where(row8 == 0, ewf, 0.0)], axis=0).astype(BF16)
    w2[:, 256:] = jnp.concatenate([0.5 * rwf * ewf, z8], axis=0).astype(BF16)

    jl = iota((64, 64), 1)
    il = iota((64, 64), 0)
    upper_b = jnp.where(il < jl, 1.0, 0.0).astype(BF16)
    lower_b = jnp.where(jl < il, 1.0, 0.0).astype(BF16)
    ones_b = jnp.ones((64, LANES), BF16)
    lane = iota((64, LANES), 1)

    def pos_at(c):
        return pos[c // 16, c // 4 % 4, c % 4][:, :64]

    def prepare(b):
        a, code = blk[0, 0, b], blk[0, 1, b]
        off = [offs[d, code] for d in range(3)]
        ca = ((a // 4 + 1) * 4 + (a // 2) % 2 + 1) * 4 + a % 2 + 1
        cb = ca + (off[0] * 4 + off[1]) * 4 + off[2]
        plan[0, b] = ca
        plan[1, b] = cb
        sh = shift_rows(off, 64)
        pa, pb = pos_at(ca), pos_at(cb)
        pbs = pb + sh
        pat = jnp.transpose(pa)
        d2 = None
        for c in range(3):
            df = pbs[c:c + 1, :] - pat[:, c:c + 1]
            d2 = df * df if d2 is None else d2 + df * df
        keep = jnp.logical_and(d2 + 0.25 < 36.001, jnp.logical_or(code != 0, il < jl))
        keep = jnp.where(jnp.logical_and(keep, b < cnt[0]), 1.0, 0.0)
        keep_b = keep.astype(BF16)
        counts = dot(keep_b, ones_b)
        prefix = dot(keep_b, upper_b)
        start = dot(lower_b, counts.astype(BF16))
        rc[b, 0:64] = start
        rc[b, 64:128] = start + counts
        local = jnp.where(keep > 0.5, prefix, 255.0)
        hi = jnp.floor(start * (1.0 / 64.0)) * 64.0
        side = jnp.where(lane == 64, hi, jnp.where(lane == 65, start - hi, 0.0))
        zt = jnp.transpose(jnp.concatenate([local, side[:, 64:]], axis=1))[:72]
        ah = pa.astype(BF16).astype(F32)
        bh = pb.astype(BF16).astype(F32)
        far = jnp.concatenate([sh, jnp.zeros_like(sh)], axis=0)
        g1[b] = jnp.concatenate([zt, ah, pa - ah, jnp.zeros((8, 64), F32)], axis=0).astype(BF16)
        g2[b] = jnp.concatenate([bh, pb - bh, far], axis=0).astype(BF16)
        tot[b] = jnp.sum(keep).astype(jnp.int32)
    wait_all(halo[0])

    def prep_group(g, c):
        for u in range(4):
            prepare(g * 4 + u)
        return c

    lax.fori_loop(0, 8, prep_group, 0)
    wait_all(rows)
    held[...] = recv1[...]
    wait_all(halo[1])


def sinpi_cospi(theta):
    m = jnp.round(theta)
    f = theta - m
    z = f * f
    sn = f * (3.14159265 + z * (-5.16771278 + z * (2.55016404 + z * (-0.599264529 + z * (0.0821458866 + z * -0.00737043094)))))
    cs = 1.0 + z * (-4.93480220 + z * (4.05871213 + z * (-1.33526277 + z * (0.235330630 + z * (-0.0258068913 + z * 0.00192957431)))))
    sign = 1.0 - 2.0 * (m - 2.0 * jnp.floor(0.5 * m))
    return sn * sign, cs * sign


def pair_kernel(plan, cnt, tot, gemb, g1, g2, rc, projt, rb, w2, out, wt, acc, tab_b, tab_k):
    def project(g, c):
        four = []
        for u in range(4):
            four += [gemb[plan[0, g * 4 + u]], gemb[plan[1, g * 4 + u]]]
        for u in (0, 2):
            both = (dot_nt(projt[...], jnp.concatenate(four[2 * u:2 * u + 4], axis=0)).astype(BF16) * 0.5).astype(BF16)
            wt[g * 4 + u] = both[:, :LANES]
            wt[g * 4 + u + 1] = both[:, LANES:]
        return c

    lax.fori_loop(0, (cnt[0] + 3) // 4, project, 0)

    def fill_block(b, n):
        def put(t, n):
            tab_b[n] = b
            tab_k[n] = t * CHUNK
            return n + 1

        return lax.fori_loop(0, (tot[b] + CHUNK - 1) // CHUNK, put, n)

    n = lax.fori_loop(0, cnt[0], fill_block, 0)
    for u in range(GROUP):
        tab_b[n + u] = 0
        tab_k[n + u] = 1 << 20

    acc[...] = jnp.zeros_like(acc)
    kl = iota((1, CHUNK), 1)
    sub = iota((8, CHUNK), 0)
    order = (sub + 1).astype(F32)
    ones_rows = jnp.where(sub < 3, 1.0, 0.0)
    halves = iota((8, LANES), 1) < 64

    def wide(x):
        return jnp.concatenate([x] * (CHUNK // LANES), axis=1)

    def chunk_group(g, c):
        R = range(GROUP)
        bs = [tab_b[g * GROUP + u] for u in R]
        ks = [(kl + tab_k[g * GROUP + u]).astype(F32) for u in R]
        oh_i = []
        for u in R:
            hit = jnp.logical_and(ks[u] >= wide(rc[bs[u], 0:64]), ks[u] < wide(rc[bs[u], 64:128]))
            oh_i.append(jnp.where(hit, 1.0, 0.0).astype(BF16))
        got = [dot(g1[bs[u]], oh_i[u]) for u in R]
        oh_j = []
        for u in R:
            want = ks[u] - got[u][64:65] - got[u][65:66]
            oh_j.append(jnp.where(got[u][:64] == want, 1.0, 0.0).astype(BF16))
        gotb = [dot(g2[bs[u]], oh_j[u]) for u in R]
        info = []
        xs = []
        for u in R:
            sep = (gotb[u][:8] + gotb[u][8:16] + gotb[u][16:24]) - (got[u][72:80] + got[u][80:88])
            sq = sep * sep
            d2 = sq[0:1] + sq[1:2] + sq[2:3]
            s = jnp.sqrt(jnp.broadcast_to(d2, (8, CHUNK)) + 0.25) * (1.0 / 6.0)
            sn, cs = sinpi_cospi(order * s)
            e = jnp.where(s < 1.0, 1.0 - s * s, 0.0)
            info.append((sep, s, e, cs * order))
            x2 = jnp.concatenate([sn, ones_rows], axis=0).astype(BF16)
            xs.append(jnp.concatenate([oh_i[u], oh_j[u], x2, jnp.zeros((112, CHUNK), BF16)], axis=0))
        qs = [dot(jnp.concatenate([wt[bs[u]], rb[...]], axis=1), xs[u]) for u in R]
        hd = []
        for u in R:
            q = qs[u]
            t = jnp.tanh(q)
            h = q + q * t
            d = (1.0 + t) + h * (1.0 - t)
            hd.append(jnp.concatenate([h.astype(BF16), d.astype(BF16)], axis=0))
        rs = []
        for u in range(0, GROUP, 2):
            both = dot(w2[...], jnp.concatenate([hd[u], hd[u + 1]], axis=1))
            rs += [both[:, :CHUNK], both[:, CHUNK:]]
        fs = []
        for u in R:
            sep, s, e, cn = info[u]
            terms = rs[u][:8] * cn * (np.pi * e * e) + rs[u][8:] * (-4.0 * s * e)
            ct = jnp.sum(terms, axis=0, keepdims=True)
            f = sep * (ct / (36.0 * s))
            fh = f.astype(BF16).astype(F32)
            fs.append(jnp.concatenate([fh, f - fh], axis=0).astype(BF16))
        for u in R:
            both = dot_nt(fs[u], xs[u][:128])
            part = both[:8] + both[8:]
            acc[plan[0, bs[u]]] += jnp.where(halves, part, 0.0)
            acc[plan[1, bs[u]]] += jnp.where(halves, 0.0, part)
        return c

    lax.fori_loop(0, (n + GROUP - 1) // GROUP, chunk_group, 0)
    out[...] = (acc[...] - jnp.roll(acc[...], 64, axis=2)).reshape(4, 4, 4, 8, LANES)


def return_kernel(fsum, pos_in, vel_in, slot, dest, held, forces, moved, embeds, pos_v, vel_v, slot_v, dest_v, landed, mot, send1, recv1, send2, recv2, esend, erecv, loc, fs, fr, s1, r1, s2, r2, s3, r3):
    me = position()
    barrier = pltpu.get_barrier_semaphore()
    partners = greet(me, -1, True)
    local = []
    for i, (x, y) in enumerate(((pos_in, pos_v), (vel_in, vel_v), (slot, slot_v), (dest, dest_v))):
        local.append(pltpu.make_async_copy(x, y, loc.at[i]))
        local[-1].start()
    mot[...] = jnp.zeros_like(mot)
    pl.semaphore_wait(barrier, partners)
    back = []
    for i, (s, own, ghost) in enumerate(BOXES):
        copy = pltpu.make_async_remote_copy(src_ref=box(fsum, ghost), dst_ref=box(landed.at[i], own), send_sem=fs.at[i], recv_sem=fr.at[i], device_id=shifted(me, s, 1), device_id_type=MESH)
        copy.start()
        back.append(copy)
    out = iota((256, 256), 0)
    want = ((out // 2) % 16) * 16 + (out // 32) * 2 + out % 2
    perm2 = jnp.where(iota((256, 256), 1) == want, 1.0, 0.0).astype(BF16)
    esend[...] = dot(perm2, held[...]).astype(BF16)
    out = iota((128, 128), 0)
    perm = jnp.where(iota((128, 128), 1) == (out % 16) * 8 + out // 16, 1.0, 0.0).astype(BF16)
    rows_sent = exchange(me, line_partner, 8, 32, esend, erecv, s3, r3)
    wait_all(local)
    where = placement(dest_v[...], True)
    pick = jnp.where(iota((512, 128), 0) == slot_v[...], 1.0, 0.0).astype(BF16)
    place = dot(pick, where).astype(BF16)
    wait_all(back)
    for c in np.ndindex(2, 2, 2):
        total = fsum[c[0] + 1, c[1] + 1, c[2] + 1]
        for i, (s, own, ghost) in enumerate(BOXES):
            if all(lo <= x < hi for x, (lo, hi) in zip(c, own)):
                total = total + landed[i, c[0], c[1], c[2]]
        forces[c[0], c[1], c[2]] = total
        new_velocity = vel_v[c[0], c[1], :, c[2], :] + 0.5 * total[:3, :64]
        new_position = pos_v[c[0], c[1], :, c[2], :] + 0.5 * new_velocity
        at = (c[0] * 4 + c[1] * 2 + c[2]) * 64
        mot[0:3, at:at + 64] = new_position
        mot[8:11, at:at + 64] = new_velocity
    rows = dot(mot[...].astype(BF16), place)
    tall = jnp.concatenate([rows[:, :128], rows[:, 128:], jnp.zeros((96, 128), F32)], axis=0)
    send1[...] = jnp.transpose(tall)
    wait_all(exchange(me, plane_partner, 16, 8, send1, recv1, s1, r1))
    send2[...] = dot(perm, recv1[...].astype(BF16))
    last = exchange(me, line_partner, 8, 16, send2, recv2, s2, r2)
    wait_all(rows_sent)
    embeds[...] = erecv[...]
    wait_all(last)
    moved[...] = jnp.transpose(recv2[...])[:32]


def finish_kernel(forces, moved, embeds, forces_out, motion_out, embeds_out):
    for c in np.ndindex(2, 2, 2):
        forces_out[c[0], c[1], :, c[2], :] = forces[c[0], c[1], c[2]][:3, :64]
    for v in range(6):
        for h in range(2):
            at = 16 * h + 8 * (v // 3) + v % 3
            motion_out[v, h:h + 1, :] = moved[at:at + 1, :]
    embeds_out[...] = embeds[...].reshape(128, 2, 256)


def per_device(positions, velocity, atom_embed, embed_proj, radial_weight, latent_bias, energy_weight, block_list, block_count, move_slot, move_dest):
    any_, vmem, smem, hbm = (pl.BlockSpec(memory_space=m) for m in (pl.ANY, pltpu.VMEM, pltpu.SMEM, pltpu.HBM))
    dma = pltpu.SemaphoreType.DMA
    array = jax.ShapeDtypeStruct
    pos_rows, vel_rows = (x.transpose(0, 1, 3, 2, 4) for x in (positions, velocity))
    dest_row = move_dest.reshape(1, 128)
    spaces = pltpu.VMEM((2, 2, 3, 2, 64), F32)
    gemb, held, g1, g2, rc, projt, rb, w2, plan, tot = pl.pallas_call(
        halo_kernel,
        out_shape=(
            array((4, 4, 4, 64, 256), BF16),
            array((256, 256), BF16),
            array((32, 96, 64), BF16),
            array((32, 32, 64), BF16),
            array((32, 128, LANES), F32),
            array((256, 256), BF16),
            array((256, 128), BF16),
            array((16, 512), BF16),
            array((2, 32), jnp.int32),
            array((32,), jnp.int32),
        ),
        in_specs=[hbm] * 9 + [smem],
        out_specs=(any_,) + (vmem,) * 7 + (smem,) * 2,
        scratch_shapes=[
            pltpu.VMEM((4, 4, 4, 8, LANES), F32),
            spaces,
            pltpu.VMEM((2, 2, 2, 64, 256), BF16),
            pltpu.VMEM((1, 128), jnp.int32),
            pltpu.VMEM((1, 128), jnp.int32),
            pltpu.VMEM((256, 256), BF16),
            pltpu.VMEM((8, 256), BF16),
            pltpu.VMEM((1, 256), F32),
            pltpu.VMEM((256,), BF16),
            pltpu.VMEM((256, 256), BF16),
            pltpu.VMEM((256, 256), BF16),
            pltpu.SMEM((1, 2, 32), jnp.int32),
            pltpu.SMEM((3, 16), jnp.int32),
        ]
        + [dma((10,))] + [dma((N_BOX,))] * 4 + [dma((16,))] * 2,
        compiler_params=pltpu.CompilerParams(collective_id=0, has_side_effects=True, vmem_limit_bytes=16 * 1024 * 1024),
        name="halo",
    )(*(pltpu.with_memory_space_constraint(x, pltpu.HBM) for x in (pos_rows, atom_embed, move_slot, dest_row, block_list, embed_proj, radial_weight, latent_bias.reshape(1, 256), energy_weight)), block_count)
    fsum = pl.pallas_call(
        pair_kernel,
        out_shape=array((4, 4, 4, 8, LANES), F32),
        in_specs=[smem] * 3 + [vmem] * 7,
        out_specs=vmem,
        scratch_shapes=[
            pltpu.VMEM((32, 256, 128), BF16),
            pltpu.VMEM((64, 8, LANES), F32),
            pltpu.SMEM((MAXCH + GROUP,), jnp.int32),
            pltpu.SMEM((MAXCH + GROUP,), jnp.int32),
        ],
        compiler_params=pltpu.CompilerParams(vmem_limit_bytes=24 * 1024 * 1024),
        name="pairs",
    )(plan, block_count, tot, gemb.reshape(64, 64, 256), g1, g2, rc, projt, rb, w2)
    raw = pl.pallas_call(
        return_kernel,
        out_shape=(array((2, 2, 2, 8, LANES), F32), array((32, LANES), F32), array((256, 256), BF16)),
        in_specs=[vmem] + [hbm] * 4 + [vmem],
        out_specs=(vmem,) * 3,
        scratch_shapes=[spaces, spaces, pltpu.VMEM((1, 128), jnp.int32), pltpu.VMEM((1, 128), jnp.int32)]
        + [pltpu.VMEM((N_BOX, 2, 2, 2, 8, LANES), F32), pltpu.VMEM((16, 512), F32)]
        + [pltpu.VMEM((128, LANES), F32)] * 4
        + [pltpu.VMEM((256, 256), BF16)] * 2
        + [dma((4,))] + [dma((N_BOX,))] * 2 + [dma((16,))] * 2 + [dma((8,))] * 4,
        compiler_params=pltpu.CompilerParams(collective_id=1, has_side_effects=True, vmem_limit_bytes=16 * 1024 * 1024),
        name="give_back",
    )(fsum, *(pltpu.with_memory_space_constraint(x, pltpu.HBM) for x in (pos_rows, vel_rows, move_slot, dest_row)), held)
    forces, motion, embeds = pl.pallas_call(
        finish_kernel,
        out_shape=(array((2, 2, 3, 2, 64), F32), array((6, 2, 128), F32), array((128, 2, 256), BF16)),
        in_specs=[vmem] * 3,
        out_specs=(vmem,) * 3,
        compiler_params=pltpu.CompilerParams(vmem_limit_bytes=8 * 1024 * 1024),
        name="finish",
    )(*raw)
    return forces.transpose(0, 1, 3, 2, 4), motion.transpose(2, 1, 0), embeds


def solution(mesh):
    placed = (
        P("gx", "gy", "gz", None, None),
        P("gx", "gy", "gz", None, None),
        P("gx", "gy", "gz", None, None),
        P(),
        P(),
        P(),
        P(),
        P(("gx", "gy", "gz"), None, None),
        P(("gx", "gy", "gz")),
        P(("gx", "gy", "gz"), None),
        P(("gx", "gy", "gz"), None),
    )
    return jax.shard_map(
        per_device,
        mesh=mesh,
        in_specs=placed,
        out_specs=(
            P("gx", "gy", "gz", None, None),
            P(("gx", "gy", "gz"), None, None),
            P(("gx", "gy", "gz"), None, None),
        ),
        check_vma=False,
    )
```

```python
import functools

import jax
import jax.numpy as jnp
import numpy as np
from jax import lax
from jax.experimental import pallas as pl
from jax.experimental.pallas import tpu as pltpu
from jax.sharding import PartitionSpec as P

F32, BF16 = jnp.float32, jnp.bfloat16
MESH = pl.DeviceIdType.MESH
OFFSETS = np.array([[0, 0, 0], [1, 0, 0], [0, 1, 0], [0, 0, 1], [1, 1, 0], [1, 0, 1], [0, 1, 1], [1, 1, 1], [1, 1, -1], [1, -1, 1], [-1, 1, 1], [1, -1, 0], [1, 0, -1], [0, 1, -1]], np.int32)
LANES = 128
GROUP = 12
CHUNK = 128
MAXCH = 32 * 32
SIZES = (8, 4, 4)


def ghost_boxes():
    need = {}
    for a in np.ndindex(2, 2, 2):
        for o in OFFSETS:
            b = [int(x) for x in np.array(a) + o]
            s = tuple(-1 if x < 0 else (1 if x > 1 else 0) for x in b)
            if any(s):
                need.setdefault(s, []).append([x - 2 * y for x, y in zip(b, s)])
    boxes = []
    for s in sorted(need, key=lambda s: (-s[0], -len(set(map(tuple, need[s]))), s)):
        own = [(min(c[d] for c in need[s]), max(c[d] for c in need[s]) + 1) for d in range(3)]
        boxes.append((s, own, [(lo + 2 * s[d] + 1, hi + 2 * s[d] + 1) for d, (lo, hi) in enumerate(own)]))
    return boxes


BOXES = ghost_boxes()
N_BOX = len(BOXES)


def box(ref, ranges):
    return ref.at[tuple(pl.ds(lo, hi - lo) for lo, hi in ranges)]


def dot(a, b):
    return jnp.dot(a, b, preferred_element_type=F32)


def dot_nt(a, b):
    return lax.dot_general(a, b, (((1,), (1,)), ((), ())), preferred_element_type=F32)


def iota(shape, dim):
    return lax.broadcasted_iota(jnp.int32, shape, dim)


def position():
    return tuple(lax.axis_index(a) for a in ("gx", "gy", "gz"))


def shifted(me, s, sign):
    return tuple(lax.rem(m + sign * d + n, n) if d else m for m, d, n in zip(me, s, SIZES))


def greet(me, toward, line):
    barrier = pltpu.get_barrier_semaphore()
    for s, _, _ in BOXES:
        pl.semaphore_signal(barrier, inc=1, device_id=shifted(me, s, toward), device_id_type=MESH)
    for k in range(1, 16):
        pl.semaphore_signal(barrier, inc=1, device_id=plane_partner(me, k)[0], device_id_type=MESH)
    for k in range(1, 8 if line else 1):
        pl.semaphore_signal(barrier, inc=1, device_id=line_partner(me, k)[0], device_id_type=MESH)
    return N_BOX + 15 + (7 if line else 0)


def plane_partner(me, k):
    at = lax.rem(me[1] * 4 + me[2] + k, 16)
    return (me[0], at // 4, lax.rem(at, 4)), at


def line_partner(me, k):
    at = lax.rem(me[0] + k, 8)
    return (at, me[1], me[2]), at


def exchange(me, partner, count, rows, src, dst, send_sem, recv_sem):
    copies = []
    mine = me[0] if count == 8 else me[1] * 4 + me[2]
    here = pl.ds(pl.multiple_of(mine * rows, rows), rows)
    for k in range(1, count):
        device, at = partner(me, k)
        copy = pltpu.make_async_remote_copy(
            src_ref=src.at[pl.ds(pl.multiple_of(at * rows, rows), rows)],
            dst_ref=dst.at[here],
            send_sem=send_sem.at[k],
            recv_sem=recv_sem.at[k],
            device_id=device,
            device_id_type=MESH,
        )
        copy.start()
        copies.append(copy)
    dst[here] = src[here]
    return copies


def wait_all(copies):
    for copy in copies:
        copy.wait()


def leaving(dest, slot):
    dest_f = dest.astype(F32)
    row = jnp.broadcast_to(dest_f, (128, LANES))
    col = jnp.transpose(row)
    earlier = jnp.logical_and(col == row, iota((128, 128), 0) < iota((128, 128), 1))
    rank = jnp.sum(jnp.where(earlier, 1.0, 0.0), axis=0, keepdims=True)
    gx = jnp.floor(dest_f * (1.0 / 16.0))
    place = 2.0 * ((dest_f - 16.0 * gx) * 8.0 + gx) + rank
    sub = iota((8, LANES), 0)
    return jnp.where(sub == 0, slot.astype(F32), jnp.where(sub == 1, place, 0.0))


def places_of(rows):
    return jnp.where(iota((256, LANES), 0).astype(F32) == rows[1:2], 1.0, 0.0).astype(BF16)


def slots_of(rows, cells):
    at = iota((64, LANES), 0)
    hits = [(at + (c[0] * 4 + c[1] * 2 + c[2]) * 64).astype(F32) == rows[0:1] for c in cells]
    return jnp.where(jnp.concatenate(hits, axis=0), 1.0, 0.0).astype(BF16)


def cells_in(own):
    return [c for c in np.ndindex(2, 2, 2) if all(lo <= x < hi for x, (lo, hi) in zip(c, own))]


OWNERS = [((0, 0, 0), cells_in([(0, 2)] * 3))] + [(s, cells_in(own)) for s, own, _ in BOXES]
N_ROWS = 64 * sum(len(cells) for _, cells in OWNERS)


def turned(x, s):
    lane = iota(x.shape, 1)
    if s[0]:
        x = pltpu.roll(x, (16 * s[0]) % 128, 1)
    for size, step, at in ((s[1], 4, lane // 4 % 4), (s[2], 1, lane % 4)):
        if size:
            x = jnp.where(at == (0 if size > 0 else 3), pltpu.roll(x, (-3 * step * size) % 128, 1), pltpu.roll(x, (step * size) % 128, 1))
    return x


def shift_rows(offset, lanes):
    x, y, z = [(8 * v).astype(F32) for v in offset]
    row = iota((8, lanes), 0)
    return jnp.where(row == 0, x, jnp.where(row == 1, y, jnp.where(row == 2, z, 0.0)))


def halo_kernel(pos_in, emb, slot, dest, blk_in, proj, rw, bias, ew, cnt, gemb, held, g1, g2, rc, projt, rb, w2, places, plan, tot,
                pos, pos_v, emb_v, slot_v, dest_v, proj_v, rw_v, bias_v, ew_v, send1, recv1, mine, lists, blk, offs, loc, es, er, ps, pr, ls, lr, s1, r1):
    me = position()
    barrier = pltpu.get_barrier_semaphore()
    pos[...] = jnp.zeros_like(pos)
    for c, o in enumerate(OFFSETS):
        for d in range(3):
            offs[d, c] = int(o[d])
    partners = greet(me, 1, False)
    own = [(1, 3)] * 3
    local = []
    for i, (x, y) in enumerate(((pos_in, pos_v), (emb, emb_v), (slot, slot_v), (dest, dest_v), (blk_in, blk), (proj, proj_v), (rw, rw_v), (bias, bias_v), (ew, ew_v), (emb, box(gemb, own)))):
        local.append(pltpu.make_async_copy(x, y, loc.at[i]))
        local[-1].start()
    local[0].wait()
    for c in np.ndindex(2, 2, 2):
        pos[c[0] + 1, c[1] + 1, c[2] + 1, 0:3, 0:64] = pos_v[c[0], c[1], :, c[2], :]
    pl.semaphore_wait(barrier, partners)
    halo = []
    for a, b, x, y in ((pos, pos, ps, pr), (emb, gemb, es, er)):
        copies = []
        for i, (s, src, dst) in enumerate(BOXES):
            start = box(a, [(lo + 1, hi + 1) for lo, hi in src]) if a is pos else box(a, src)
            copies.append(pltpu.make_async_remote_copy(src_ref=start, dst_ref=box(b, dst), send_sem=x.at[i], recv_sem=y.at[i], device_id=shifted(me, s, -1), device_id_type=MESH))
            copies[-1].start()
        halo.append(copies)
    for copy in local[1:]:
        copy.wait()
    rows_out = leaving(dest_v[...], slot_v[...])
    mine[...] = rows_out
    copies = []
    for i, (s, src, dst) in enumerate(BOXES):
        copies.append(pltpu.make_async_remote_copy(src_ref=mine, dst_ref=lists.at[i], send_sem=ls.at[i], recv_sem=lr.at[i], device_id=shifted(me, s, -1), device_id_type=MESH))
        copies[-1].start()
    halo.append(copies)
    place = dot_nt(places_of(rows_out), slots_of(rows_out, OWNERS[0][1])).astype(BF16)
    send1[...] = dot(place, emb_v[...].reshape(512, 256)).astype(BF16)
    rows = exchange(me, plane_partner, 16, 16, send1, recv1, s1, r1)
    projt[...] = jnp.transpose(proj_v[...])
    half = 0.5 * bias_v[...]
    b1 = half.astype(BF16).astype(F32)
    b2 = (half - b1).astype(BF16).astype(F32)
    row8 = iota((8, 256), 0)
    biases = jnp.where(row8 == 0, b1, jnp.where(row8 == 1, b2, jnp.where(row8 == 2, half - b1 - b2, 0.0)))
    rwf = rw_v[...].astype(F32)
    ewf = ew_v[...].astype(F32).reshape(1, 256)
    rb[...] = jnp.transpose(jnp.concatenate([0.5 * rwf, biases, jnp.zeros((112, 256), F32)], axis=0)).astype(BF16)
    z8 = jnp.zeros((8, 256), F32)
    w2[:, :256] = jnp.concatenate([z8, jnp.where(row8 == 0, ewf, 0.0)], axis=0).astype(BF16)
    w2[:, 256:] = jnp.concatenate([0.5 * rwf * ewf, z8], axis=0).astype(BF16)

    jl = iota((64, 64), 1)
    il = iota((64, 64), 0)
    upper_b = jnp.where(il < jl, 1.0, 0.0).astype(BF16)
    lower_b = jnp.where(jl < il, 1.0, 0.0).astype(BF16)
    ones_b = jnp.ones((64, LANES), BF16)
    lane = iota((64, LANES), 1)

    def pos_at(c):
        return pos[c // 16, c // 4 % 4, c % 4][:, :64]

    def prepare(b):
        a, code = blk[0, 0, b], blk[0, 1, b]
        off = [offs[d, code] for d in range(3)]
        ca = ((a // 4 + 1) * 4 + (a // 2) % 2 + 1) * 4 + a % 2 + 1
        cb = ca + (off[0] * 4 + off[1]) * 4 + off[2]
        plan[0, b] = ca
        plan[1, b] = cb
        sh = shift_rows(off, 64)
        pa, pb = pos_at(ca), pos_at(cb)
        pbs = pb + sh
        pat = jnp.transpose(pa)
        d2 = None
        for c in range(3):
            df = pbs[c:c + 1, :] - pat[:, c:c + 1]
            d2 = df * df if d2 is None else d2 + df * df
        keep = jnp.logical_and(d2 + 0.25 < 36.001, jnp.logical_or(code != 0, il < jl))
        keep = jnp.where(jnp.logical_and(keep, b < cnt[0]), 1.0, 0.0)
        keep_b = keep.astype(BF16)
        counts = dot(keep_b, ones_b)
        prefix = dot(keep_b, upper_b)
        start = dot(lower_b, counts.astype(BF16))
        rc[b, 0:64] = start
        rc[b, 64:128] = start + counts
        local = jnp.where(keep > 0.5, prefix, 255.0)
        hi = jnp.floor(start * (1.0 / 64.0)) * 64.0
        side = jnp.where(lane == 64, hi, jnp.where(lane == 65, start - hi, 0.0))
        zt = jnp.transpose(jnp.concatenate([local, side[:, 64:]], axis=1))[:72]
        ah = pa.astype(BF16).astype(F32)
        bh = pb.astype(BF16).astype(F32)
        far = jnp.concatenate([sh, jnp.zeros_like(sh)], axis=0)
        g1[b] = jnp.concatenate([zt, ah, pa - ah, jnp.zeros((8, 64), F32)], axis=0).astype(BF16)
        g2[b] = jnp.concatenate([bh, pb - bh, far], axis=0).astype(BF16)
        tot[b] = jnp.sum(keep).astype(jnp.int32)
    wait_all(halo[0])

    def prep_group(g, c):
        for u in range(4):
            prepare(g * 4 + u)
        return c

    lax.fori_loop(0, 8, prep_group, 0)
    wait_all(halo[2])
    at = 0
    for i, (s, owned) in enumerate(OWNERS):
        rows_out = lists[i - 1] if i else mine[...]
        size = 64 * len(owned)
        places[at:at + size] = dot_nt(slots_of(rows_out, owned), places_of(rows_out)).astype(BF16)
        at += size
    wait_all(rows)
    held[...] = recv1[...]
    wait_all(halo[1])


def sinpi_cospi(theta):
    m = jnp.round(theta)
    f = theta - m
    z = f * f
    sn = f * (3.14159265 + z * (-5.16771278 + z * (2.55016404 + z * (-0.599264529 + z * (0.0821458866 + z * -0.00737043094)))))
    cs = 1.0 + z * (-4.93480220 + z * (4.05871213 + z * (-1.33526277 + z * (0.235330630 + z * (-0.0258068913 + z * 0.00192957431)))))
    sign = 1.0 - 2.0 * (m - 2.0 * jnp.floor(0.5 * m))
    return sn * sign, cs * sign


def pair_kernel(plan, cnt, tot, gemb, g1, g2, rc, projt, rb, w2, out, wt, acc, tab_b, tab_k):
    def project(g, c):
        four = []
        for u in range(4):
            four += [gemb[plan[0, g * 4 + u]], gemb[plan[1, g * 4 + u]]]
        for u in (0, 2):
            both = (dot_nt(projt[...], jnp.concatenate(four[2 * u:2 * u + 4], axis=0)).astype(BF16) * 0.5).astype(BF16)
            wt[g * 4 + u] = both[:, :LANES]
            wt[g * 4 + u + 1] = both[:, LANES:]
        return c

    lax.fori_loop(0, (cnt[0] + 3) // 4, project, 0)

    def fill_block(b, n):
        def put(t, n):
            tab_b[n] = b
            tab_k[n] = t * CHUNK
            return n + 1

        return lax.fori_loop(0, (tot[b] + CHUNK - 1) // CHUNK, put, n)

    n = lax.fori_loop(0, cnt[0], fill_block, 0)
    for u in range(GROUP):
        tab_b[n + u] = 0
        tab_k[n + u] = 1 << 20

    acc[...] = jnp.zeros_like(acc)
    kl = iota((1, CHUNK), 1)
    sub = iota((8, CHUNK), 0)
    order = (sub + 1).astype(F32)
    ones_rows = jnp.where(sub < 3, 1.0, 0.0)
    halves = iota((8, LANES), 1) < 64

    def wide(x):
        return jnp.concatenate([x] * (CHUNK // LANES), axis=1)

    def chunk_group(g, c):
        R = range(GROUP)
        bs = [tab_b[g * GROUP + u] for u in R]
        ks = [(kl + tab_k[g * GROUP + u]).astype(F32) for u in R]
        oh_i = []
        for u in R:
            hit = jnp.logical_and(ks[u] >= wide(rc[bs[u], 0:64]), ks[u] < wide(rc[bs[u], 64:128]))
            oh_i.append(jnp.where(hit, 1.0, 0.0).astype(BF16))
        got = [dot(g1[bs[u]], oh_i[u]) for u in R]
        oh_j = []
        for u in R:
            want = ks[u] - got[u][64:65] - got[u][65:66]
            oh_j.append(jnp.where(got[u][:64] == want, 1.0, 0.0).astype(BF16))
        gotb = [dot(g2[bs[u]], oh_j[u]) for u in R]
        info = []
        xs = []
        for u in R:
            sep = (gotb[u][:8] + gotb[u][8:16] + gotb[u][16:24]) - (got[u][72:80] + got[u][80:88])
            sq = sep * sep
            d2 = sq[0:1] + sq[1:2] + sq[2:3]
            s = jnp.sqrt(jnp.broadcast_to(d2, (8, CHUNK)) + 0.25) * (1.0 / 6.0)
            sn, cs = sinpi_cospi(order * s)
            e = jnp.where(s < 1.0, 1.0 - s * s, 0.0)
            info.append((sep, s, e, cs * order))
            x2 = jnp.concatenate([sn, ones_rows], axis=0).astype(BF16)
            xs.append(jnp.concatenate([oh_i[u], oh_j[u], x2, jnp.zeros((112, CHUNK), BF16)], axis=0))
        qs = [dot(jnp.concatenate([wt[bs[u]], rb[...]], axis=1), xs[u]) for u in R]
        hd = []
        for u in R:
            q = qs[u]
            t = jnp.tanh(q)
            h = q + q * t
            d = (1.0 + t) + h * (1.0 - t)
            hd.append(jnp.concatenate([h.astype(BF16), d.astype(BF16)], axis=0))
        rs = []
        for u in range(0, GROUP, 2):
            both = dot(w2[...], jnp.concatenate([hd[u], hd[u + 1]], axis=1))
            rs += [both[:, :CHUNK], both[:, CHUNK:]]
        fs = []
        for u in R:
            sep, s, e, cn = info[u]
            terms = rs[u][:8] * cn * (np.pi * e * e) + rs[u][8:] * (-4.0 * s * e)
            ct = jnp.sum(terms, axis=0, keepdims=True)
            f = sep * (ct / (36.0 * s))
            fh = f.astype(BF16).astype(F32)
            fs.append(jnp.concatenate([fh, f - fh], axis=0).astype(BF16))
        for u in R:
            both = dot_nt(fs[u], xs[u][:128])
            part = both[:8] + both[8:]
            acc[plan[0, bs[u]]] += jnp.where(halves, part, 0.0)
            acc[plan[1, bs[u]]] += jnp.where(halves, 0.0, part)
        return c

    lax.fori_loop(0, (n + GROUP - 1) // GROUP, chunk_group, 0)
    out[...] = (acc[...] - jnp.roll(acc[...], 64, axis=2)).reshape(4, 4, 4, 8, LANES)


def return_kernel(fsum, pos_in, vel_in, held, places, forces, moved, embeds, pos_v, vel_v, landed, lhs, send1, recv1, send2, recv2, esend, erecv, loc, fs, fr, s1, r1, s2, r2, s3, r3):
    me = position()
    barrier = pltpu.get_barrier_semaphore()
    partners = greet(me, -1, True)
    local = []
    for i, (x, y) in enumerate(((pos_in, pos_v), (vel_in, vel_v))):
        local.append(pltpu.make_async_copy(x, y, loc.at[i]))
        local[-1].start()
    lhs[...] = jnp.zeros_like(lhs)
    at = 0
    for i, (s, owned) in enumerate(OWNERS):
        for c in owned:
            part = fsum[tuple(x + 2 * d + 1 for x, d in zip(c, s))]
            if i % 2:
                part = pltpu.roll(part, 4, 0)
            lhs[8 * (i // 2):8 * (i // 2) + 8, at:at + 64] = part[:, :64]
            at += 64
    wait_all(local)
    for j, c in enumerate(OWNERS[0][1]):
        velocity = vel_v[c[0], c[1], :, c[2], :]
        lhs[80:83, 64 * j:64 * j + 64] = pos_v[c[0], c[1], :, c[2], :] + 0.5 * velocity
        lhs[84:87, 64 * j:64 * j + 64] = velocity
    rows = dot(lhs[...].astype(BF16), places[...])
    send1[...] = jnp.transpose(jnp.concatenate([rows, jnp.zeros((32, 256), F32)], axis=0)).astype(BF16)
    pl.semaphore_wait(barrier, partners)
    first = exchange(me, plane_partner, 16, 16, send1, recv1, s1, r1)
    back = []
    for i, (s, own, ghost) in enumerate(BOXES):
        copy = pltpu.make_async_remote_copy(src_ref=box(fsum, ghost), dst_ref=box(landed.at[i], own), send_sem=fs.at[i], recv_sem=fr.at[i], device_id=shifted(me, s, 1), device_id_type=MESH)
        copy.start()
        back.append(copy)
    out = iota((256, 256), 0)
    source = iota((256, 256), 1)
    want = ((out // 2) % 16) * 16 + (out // 32) * 2 + out % 2
    perm2 = jnp.where(source == want, 1.0, 0.0).astype(BF16)
    esend[...] = dot(perm2, held[...]).astype(BF16)
    rows_sent = exchange(me, line_partner, 8, 32, esend, erecv, s3, r3)
    want = (out % 16) * 16 + (out // 32) * 2 + (out // 16) % 2
    perm = jnp.where(source == want, 1.0, 0.0).astype(BF16)
    wait_all(first)
    send2[...] = dot(perm, recv1[...]).astype(BF16)
    last = exchange(me, line_partner, 8, 32, send2, recv2, s2, r2)
    wait_all(back)
    for c in np.ndindex(2, 2, 2):
        total = fsum[c[0] + 1, c[1] + 1, c[2] + 1]
        for i, (s, own, ghost) in enumerate(BOXES):
            if all(lo <= x < hi for x, (lo, hi) in zip(c, own)):
                total = total + landed[i, c[0], c[1], c[2]]
        forces[c[0], c[1], c[2]] = total
    wait_all(rows_sent)
    embeds[...] = erecv[...]
    wait_all(last)
    for h in range(2):
        by_source = jnp.concatenate([recv2[32 * g + 16 * h:32 * g + 16 * h + 16] for g in range(8)], axis=0)
        by_source = jnp.transpose(by_source.astype(F32))
        sums = [None, None]
        for i, (s, _) in enumerate(OWNERS):
            part = turned(by_source[8 * (i // 2):8 * (i // 2) + 8], s)
            sums[i % 2] = part if sums[i % 2] is None else sums[i % 2] + part
        total = sums[0] + pltpu.roll(sums[1], 4, 0)
        base = by_source[80:88]
        moved[16 * h:16 * h + 8] = base + 0.25 * total
        moved[16 * h + 8:16 * h + 16] = pltpu.roll(base, 4, 0) + 0.5 * total


def finish_kernel(forces, moved, embeds, forces_out, motion_out, embeds_out):
    for c in np.ndindex(2, 2, 2):
        forces_out[c[0], c[1], :, c[2], :] = forces[c[0], c[1], c[2]][:3, :64]
    for v in range(6):
        for h in range(2):
            at = 16 * h + 8 * (v // 3) + v % 3
            motion_out[v, h:h + 1, :] = moved[at:at + 1, :]
    embeds_out[...] = embeds[...].reshape(128, 2, 256)


def per_device(positions, velocity, atom_embed, embed_proj, radial_weight, latent_bias, energy_weight, block_list, block_count, move_slot, move_dest):
    any_, vmem, smem, hbm = (pl.BlockSpec(memory_space=m) for m in (pl.ANY, pltpu.VMEM, pltpu.SMEM, pltpu.HBM))
    dma = pltpu.SemaphoreType.DMA
    array = jax.ShapeDtypeStruct
    pos_rows, vel_rows = (x.transpose(0, 1, 3, 2, 4) for x in (positions, velocity))
    dest_row = move_dest.reshape(1, 128)
    spaces = pltpu.VMEM((2, 2, 3, 2, 64), F32)
    gemb, held, g1, g2, rc, projt, rb, w2, places, plan, tot = pl.pallas_call(
        halo_kernel,
        out_shape=(
            array((4, 4, 4, 64, 256), BF16),
            array((256, 256), BF16),
            array((32, 96, 64), BF16),
            array((32, 32, 64), BF16),
            array((32, 128, LANES), F32),
            array((256, 256), BF16),
            array((256, 128), BF16),
            array((16, 512), BF16),
            array((N_ROWS, 256), BF16),
            array((2, 32), jnp.int32),
            array((32,), jnp.int32),
        ),
        in_specs=[hbm] * 9 + [smem],
        out_specs=(any_,) + (vmem,) * 8 + (smem,) * 2,
        scratch_shapes=[
            pltpu.VMEM((4, 4, 4, 8, LANES), F32),
            spaces,
            pltpu.VMEM((2, 2, 2, 64, 256), BF16),
            pltpu.VMEM((1, 128), jnp.int32),
            pltpu.VMEM((1, 128), jnp.int32),
            pltpu.VMEM((256, 256), BF16),
            pltpu.VMEM((8, 256), BF16),
            pltpu.VMEM((1, 256), F32),
            pltpu.VMEM((256,), BF16),
            pltpu.VMEM((256, 256), BF16),
            pltpu.VMEM((256, 256), BF16),
            pltpu.VMEM((8, LANES), F32),
            pltpu.VMEM((N_BOX, 8, LANES), F32),
            pltpu.SMEM((1, 2, 32), jnp.int32),
            pltpu.SMEM((3, 16), jnp.int32),
        ]
        + [dma((10,))] + [dma((N_BOX,))] * 6 + [dma((16,))] * 2,
        compiler_params=pltpu.CompilerParams(collective_id=0, has_side_effects=True, vmem_limit_bytes=16 * 1024 * 1024),
        name="halo",
    )(*(pltpu.with_memory_space_constraint(x, pltpu.HBM) for x in (pos_rows, atom_embed, move_slot, dest_row, block_list, embed_proj, radial_weight, latent_bias.reshape(1, 256), energy_weight)), block_count)
    fsum = pl.pallas_call(
        pair_kernel,
        out_shape=array((4, 4, 4, 8, LANES), F32),
        in_specs=[smem] * 3 + [vmem] * 7,
        out_specs=vmem,
        scratch_shapes=[
            pltpu.VMEM((32, 256, 128), BF16),
            pltpu.VMEM((64, 8, LANES), F32),
            pltpu.SMEM((MAXCH + GROUP,), jnp.int32),
            pltpu.SMEM((MAXCH + GROUP,), jnp.int32),
        ],
        compiler_params=pltpu.CompilerParams(vmem_limit_bytes=24 * 1024 * 1024),
        name="pairs",
    )(plan, block_count, tot, gemb.reshape(64, 64, 256), g1, g2, rc, projt, rb, w2)
    raw = pl.pallas_call(
        return_kernel,
        out_shape=(array((2, 2, 2, 8, LANES), F32), array((32, LANES), F32), array((256, 256), BF16)),
        in_specs=[vmem] + [hbm] * 2 + [vmem] * 2,
        out_specs=(vmem,) * 3,
        scratch_shapes=[spaces, spaces, pltpu.VMEM((N_BOX, 2, 2, 2, 8, LANES), F32), pltpu.VMEM((96, N_ROWS), F32)]
        + [pltpu.VMEM((256, LANES), BF16)] * 4
        + [pltpu.VMEM((256, 256), BF16)] * 2
        + [dma((2,))] + [dma((N_BOX,))] * 2 + [dma((16,))] * 2 + [dma((8,))] * 4,
        compiler_params=pltpu.CompilerParams(collective_id=1, has_side_effects=True, vmem_limit_bytes=16 * 1024 * 1024),
        name="give_back",
    )(fsum, *(pltpu.with_memory_space_constraint(x, pltpu.HBM) for x in (pos_rows, vel_rows)), held, places)
    forces, motion, embeds = pl.pallas_call(
        finish_kernel,
        out_shape=(array((2, 2, 3, 2, 64), F32), array((6, 2, 128), F32), array((128, 2, 256), BF16)),
        in_specs=[vmem] * 3,
        out_specs=(vmem,) * 3,
        compiler_params=pltpu.CompilerParams(vmem_limit_bytes=8 * 1024 * 1024),
        name="finish",
    )(*raw)
    return forces.transpose(0, 1, 3, 2, 4), motion.transpose(2, 1, 0), embeds


def solution(mesh):
    placed = (
        P("gx", "gy", "gz", None, None),
        P("gx", "gy", "gz", None, None),
        P("gx", "gy", "gz", None, None),
        P(),
        P(),
        P(),
        P(),
        P(("gx", "gy", "gz"), None, None),
        P(("gx", "gy", "gz")),
        P(("gx", "gy", "gz"), None),
        P(("gx", "gy", "gz"), None),
    )
    return jax.shard_map(
        per_device,
        mesh=mesh,
        in_specs=placed,
        out_specs=(
            P("gx", "gy", "gz", None, None),
            P(("gx", "gy", "gz"), None, None),
            P(("gx", "gy", "gz"), None, None),
        ),
        check_vma=False,
    )
```

```python
import functools

import jax
import jax.numpy as jnp
import numpy as np
from jax import lax
from jax.experimental import pallas as pl
from jax.experimental.pallas import tpu as pltpu
from jax.sharding import PartitionSpec as P

F32, BF16 = jnp.float32, jnp.bfloat16
MESH = pl.DeviceIdType.MESH
OFFSETS = np.array([[0, 0, 0], [1, 0, 0], [0, 1, 0], [0, 0, 1], [1, 1, 0], [1, 0, 1], [0, 1, 1], [1, 1, 1], [1, 1, -1], [1, -1, 1], [-1, 1, 1], [1, -1, 0], [1, 0, -1], [0, 1, -1]], np.int32)
LANES = 128
GROUP = 12
CHUNK = 128
MAXCH = 32 * 32
SIZES = (8, 4, 4)


def ghost_boxes():
    need = {}
    for a in np.ndindex(2, 2, 2):
        for o in OFFSETS:
            b = [int(x) for x in np.array(a) + o]
            s = tuple(-1 if x < 0 else (1 if x > 1 else 0) for x in b)
            if any(s):
                need.setdefault(s, []).append([x - 2 * y for x, y in zip(b, s)])
    boxes = []
    for s in sorted(need, key=lambda s: (-s[0], -len(set(map(tuple, need[s]))), s)):
        own = [(min(c[d] for c in need[s]), max(c[d] for c in need[s]) + 1) for d in range(3)]
        boxes.append((s, own, [(lo + 2 * s[d] + 1, hi + 2 * s[d] + 1) for d, (lo, hi) in enumerate(own)]))
    return boxes


BOXES = ghost_boxes()
N_BOX = len(BOXES)


def box(ref, ranges):
    return ref.at[tuple(pl.ds(lo, hi - lo) for lo, hi in ranges)]


def dot(a, b):
    return jnp.dot(a, b, preferred_element_type=F32)


def dot_nt(a, b):
    return lax.dot_general(a, b, (((1,), (1,)), ((), ())), preferred_element_type=F32)


def iota(shape, dim):
    return lax.broadcasted_iota(jnp.int32, shape, dim)


def position():
    return tuple(lax.axis_index(a) for a in ("gx", "gy", "gz"))


def shifted(me, s, sign):
    return tuple(lax.rem(m + sign * d + n, n) if d else m for m, d, n in zip(me, s, SIZES))


def greet(me, toward, line):
    barrier = pltpu.get_barrier_semaphore()
    for s, _, _ in BOXES:
        pl.semaphore_signal(barrier, inc=1, device_id=shifted(me, s, toward), device_id_type=MESH)
    for k in range(1, 16):
        pl.semaphore_signal(barrier, inc=1, device_id=plane_partner(me, k)[0], device_id_type=MESH)
    for k in range(1, 8 if line else 1):
        pl.semaphore_signal(barrier, inc=1, device_id=line_partner(me, k)[0], device_id_type=MESH)
    return N_BOX + 15 + (7 if line else 0)


def plane_partner(me, k):
    at = lax.rem(me[1] * 4 + me[2] + k, 16)
    return (me[0], at // 4, lax.rem(at, 4)), at


def line_partner(me, k):
    at = lax.rem(me[0] + k, 8)
    return (at, me[1], me[2]), at


def exchange(me, partner, count, rows, src, dst, send_sem, recv_sem):
    copies = []
    mine = me[0] if count == 8 else me[1] * 4 + me[2]
    here = pl.ds(pl.multiple_of(mine * rows, rows), rows)
    for k in range(1, count):
        device, at = partner(me, k)
        copy = pltpu.make_async_remote_copy(
            src_ref=src.at[pl.ds(pl.multiple_of(at * rows, rows), rows)],
            dst_ref=dst.at[here],
            send_sem=send_sem.at[k],
            recv_sem=recv_sem.at[k],
            device_id=device,
            device_id_type=MESH,
        )
        copy.start()
        copies.append(copy)
    dst[here] = src[here]
    return copies


def wait_all(copies):
    for copy in copies:
        copy.wait()


def leaving(dest, slot):
    dest_f = dest.astype(F32)
    row = jnp.broadcast_to(dest_f, (128, LANES))
    col = jnp.transpose(row)
    earlier = jnp.logical_and(col == row, iota((128, 128), 0) < iota((128, 128), 1))
    rank = jnp.sum(jnp.where(earlier, 1.0, 0.0), axis=0, keepdims=True)
    gx = jnp.floor(dest_f * (1.0 / 16.0))
    place = 2.0 * ((dest_f - 16.0 * gx) * 8.0 + gx) + rank
    sub = iota((8, LANES), 0)
    return jnp.where(sub == 4, slot.astype(F32), jnp.where(sub == 5, place, 0.0))


def places_of(rows):
    return jnp.where(iota((256, LANES), 0).astype(F32) == rows[5:6], 1.0, 0.0).astype(BF16)


def slots_of(rows, cells):
    at = iota((64, LANES), 0)
    hits = [(at + (c[0] * 4 + c[1] * 2 + c[2]) * 64).astype(F32) == rows[4:5] for c in cells]
    return jnp.where(jnp.concatenate(hits, axis=0), 1.0, 0.0).astype(BF16)


def cells_in(own):
    return [c for c in np.ndindex(2, 2, 2) if all(lo <= x < hi for x, (lo, hi) in zip(c, own))]


OWNERS = [((0, 0, 0), cells_in([(0, 2)] * 3))] + [(s, cells_in(own)) for s, own, _ in BOXES]
N_ROWS = 64 * sum(len(cells) for _, cells in OWNERS)


def turned(x, s):
    lane = iota(x.shape, 1)
    if s[0]:
        x = pltpu.roll(x, (16 * s[0]) % 128, 1)
    for size, step, at in ((s[1], 4, lane // 4 % 4), (s[2], 1, lane % 4)):
        if size:
            x = jnp.where(at == (0 if size > 0 else 3), pltpu.roll(x, (-3 * step * size) % 128, 1), pltpu.roll(x, (step * size) % 128, 1))
    return x


def shift_rows(offset, lanes):
    x, y, z = [(8 * v).astype(F32) for v in offset]
    row = iota((8, lanes), 0)
    return jnp.where(row == 0, x, jnp.where(row == 1, y, jnp.where(row == 2, z, 0.0)))


def halo_kernel(pos_in, emb, slot, dest, blk_in, proj, rw, bias, ew, cnt, gemb, held, g1, g2, rc, projt, rb, w2, places, plan, tot,
                pos, pos_v, emb_v, slot_v, dest_v, proj_v, rw_v, bias_v, ew_v, send1, recv1, blk, offs, loc, es, er, ps, pr, s1, r1):
    me = position()
    barrier = pltpu.get_barrier_semaphore()
    pos[...] = jnp.zeros_like(pos)
    for c, o in enumerate(OFFSETS):
        for d in range(3):
            offs[d, c] = int(o[d])
    partners = greet(me, 1, False)
    own = [(1, 3)] * 3
    local = []
    for i, (x, y) in enumerate(((pos_in, pos_v), (slot, slot_v), (dest, dest_v), (emb, emb_v), (blk_in, blk), (proj, proj_v), (rw, rw_v), (bias, bias_v), (ew, ew_v), (emb, box(gemb, own)))):
        local.append(pltpu.make_async_copy(x, y, loc.at[i]))
        local[-1].start()
    for copy in local[:3]:
        copy.wait()
    rows_out = leaving(dest_v[...], slot_v[...])
    for c in np.ndindex(2, 2, 2):
        pos[c[0] + 1, c[1] + 1, c[2] + 1] = rows_out
        pos[c[0] + 1, c[1] + 1, c[2] + 1, 0:3, 0:64] = pos_v[c[0], c[1], :, c[2], :]
    pl.semaphore_wait(barrier, partners)
    halo = []
    for a, b, x, y in ((pos, pos, ps, pr), (emb, gemb, es, er)):
        copies = []
        for i, (s, src, dst) in enumerate(BOXES):
            start = box(a, [(lo + 1, hi + 1) for lo, hi in src]) if a is pos else box(a, src)
            copies.append(pltpu.make_async_remote_copy(src_ref=start, dst_ref=box(b, dst), send_sem=x.at[i], recv_sem=y.at[i], device_id=shifted(me, s, -1), device_id_type=MESH))
            copies[-1].start()
        halo.append(copies)
    for copy in local[3:]:
        copy.wait()
    place = dot_nt(places_of(rows_out), slots_of(rows_out, OWNERS[0][1])).astype(BF16)
    send1[...] = dot(place, emb_v[...].reshape(512, 256)).astype(BF16)
    rows = exchange(me, plane_partner, 16, 16, send1, recv1, s1, r1)
    projt[...] = jnp.transpose(proj_v[...])
    half = 0.5 * bias_v[...]
    b1 = half.astype(BF16).astype(F32)
    b2 = (half - b1).astype(BF16).astype(F32)
    row8 = iota((8, 256), 0)
    biases = jnp.where(row8 == 0, b1, jnp.where(row8 == 1, b2, jnp.where(row8 == 2, half - b1 - b2, 0.0)))
    rwf = rw_v[...].astype(F32)
    ewf = ew_v[...].astype(F32).reshape(1, 256)
    rb[...] = jnp.transpose(jnp.concatenate([0.5 * rwf, biases, jnp.zeros((112, 256), F32)], axis=0)).astype(BF16)
    z8 = jnp.zeros((8, 256), F32)
    w2[:, :256] = jnp.concatenate([z8, jnp.where(row8 == 0, ewf, 0.0)], axis=0).astype(BF16)
    w2[:, 256:] = jnp.concatenate([0.5 * rwf * ewf, z8], axis=0).astype(BF16)

    jl = iota((64, 64), 1)
    il = iota((64, 64), 0)
    upper_b = jnp.where(il < jl, 1.0, 0.0).astype(BF16)
    lower_b = jnp.where(jl < il, 1.0, 0.0).astype(BF16)
    ones_b = jnp.ones((64, LANES), BF16)
    lane = iota((64, LANES), 1)

    def pos_at(c):
        return jnp.where(iota((8, 64), 0) < 3, pos[c // 16, c // 4 % 4, c % 4][:, :64], 0.0)

    def prepare(b):
        a, code = blk[0, 0, b], blk[0, 1, b]
        off = [offs[d, code] for d in range(3)]
        ca = ((a // 4 + 1) * 4 + (a // 2) % 2 + 1) * 4 + a % 2 + 1
        cb = ca + (off[0] * 4 + off[1]) * 4 + off[2]
        plan[0, b] = ca
        plan[1, b] = cb
        sh = shift_rows(off, 64)
        pa, pb = pos_at(ca), pos_at(cb)
        pbs = pb + sh
        pat = jnp.transpose(pa)
        d2 = None
        for c in range(3):
            df = pbs[c:c + 1, :] - pat[:, c:c + 1]
            d2 = df * df if d2 is None else d2 + df * df
        keep = jnp.logical_and(d2 + 0.25 < 36.001, jnp.logical_or(code != 0, il < jl))
        keep = jnp.where(jnp.logical_and(keep, b < cnt[0]), 1.0, 0.0)
        keep_b = keep.astype(BF16)
        counts = dot(keep_b, ones_b)
        prefix = dot(keep_b, upper_b)
        start = dot(lower_b, counts.astype(BF16))
        rc[b, 0:64] = start
        rc[b, 64:128] = start + counts
        local = jnp.where(keep > 0.5, prefix, 255.0)
        hi = jnp.floor(start * (1.0 / 64.0)) * 64.0
        side = jnp.where(lane == 64, hi, jnp.where(lane == 65, start - hi, 0.0))
        zt = jnp.transpose(jnp.concatenate([local, side[:, 64:]], axis=1))[:72]
        ah = pa.astype(BF16).astype(F32)
        bh = pb.astype(BF16).astype(F32)
        far = jnp.concatenate([sh, jnp.zeros_like(sh)], axis=0)
        g1[b] = jnp.concatenate([zt, ah, pa - ah, jnp.zeros((8, 64), F32)], axis=0).astype(BF16)
        g2[b] = jnp.concatenate([bh, pb - bh, far], axis=0).astype(BF16)
        tot[b] = jnp.sum(keep).astype(jnp.int32)
    wait_all(halo[0])

    def prep_group(g, c):
        for u in range(8):
            prepare(g * 8 + u)
        return c

    lax.fori_loop(0, 4, prep_group, 0)
    at = 0
    for i, (s, owned) in enumerate(OWNERS):
        first = tuple(x + 2 * d + 1 for x, d in zip(owned[0], s))
        rows_out = pos[first]
        size = 64 * len(owned)
        places[at:at + size] = dot_nt(slots_of(rows_out, owned), places_of(rows_out)).astype(BF16)
        at += size
    wait_all(rows)
    held[...] = recv1[...]
    wait_all(halo[1])


def sinpi_cospi(theta):
    m = jnp.round(theta)
    f = theta - m
    z = f * f
    sn = f * (3.14159265 + z * (-5.16771278 + z * (2.55016404 + z * (-0.599264529 + z * (0.0821458866 + z * -0.00737043094)))))
    cs = 1.0 + z * (-4.93480220 + z * (4.05871213 + z * (-1.33526277 + z * (0.235330630 + z * (-0.0258068913 + z * 0.00192957431)))))
    sign = 1.0 - 2.0 * (m - 2.0 * jnp.floor(0.5 * m))
    return sn * sign, cs * sign


def pair_kernel(plan, cnt, tot, gemb, g1, g2, rc, projt, rb, w2, out, wt, acc, tab_b, tab_k):
    def project(g, c):
        four = []
        for u in range(4):
            four += [gemb[plan[0, g * 4 + u]], gemb[plan[1, g * 4 + u]]]
        for u in (0, 2):
            both = (dot_nt(projt[...], jnp.concatenate(four[2 * u:2 * u + 4], axis=0)).astype(BF16) * 0.5).astype(BF16)
            wt[g * 4 + u] = both[:, :LANES]
            wt[g * 4 + u + 1] = both[:, LANES:]
        return c

    lax.fori_loop(0, (cnt[0] + 3) // 4, project, 0)

    def fill_block(b, n):
        def put(t, n):
            tab_b[n] = b
            tab_k[n] = t * CHUNK
            return n + 1

        return lax.fori_loop(0, (tot[b] + CHUNK - 1) // CHUNK, put, n)

    n = lax.fori_loop(0, cnt[0], fill_block, 0)
    for u in range(GROUP):
        tab_b[n + u] = 0
        tab_k[n + u] = 1 << 20

    acc[...] = jnp.zeros_like(acc)
    kl = iota((1, CHUNK), 1)
    sub = iota((8, CHUNK), 0)
    order = (sub + 1).astype(F32)
    ones_rows = jnp.where(sub < 3, 1.0, 0.0)
    halves = iota((8, LANES), 1) < 64

    def wide(x):
        return jnp.concatenate([x] * (CHUNK // LANES), axis=1)

    def chunk_group(g, c):
        R = range(GROUP)
        bs = [tab_b[g * GROUP + u] for u in R]
        ks = [(kl + tab_k[g * GROUP + u]).astype(F32) for u in R]
        oh_i = []
        for u in R:
            hit = jnp.logical_and(ks[u] >= wide(rc[bs[u], 0:64]), ks[u] < wide(rc[bs[u], 64:128]))
            oh_i.append(jnp.where(hit, 1.0, 0.0).astype(BF16))
        got = [dot(g1[bs[u]], oh_i[u]) for u in R]
        oh_j = []
        for u in R:
            want = ks[u] - got[u][64:65] - got[u][65:66]
            oh_j.append(jnp.where(got[u][:64] == want, 1.0, 0.0).astype(BF16))
        gotb = [dot(g2[bs[u]], oh_j[u]) for u in R]
        info = []
        xs = []
        for u in R:
            sep = (gotb[u][:8] + gotb[u][8:16] + gotb[u][16:24]) - (got[u][72:80] + got[u][80:88])
            sq = sep * sep
            d2 = sq[0:1] + sq[1:2] + sq[2:3]
            s = jnp.sqrt(jnp.broadcast_to(d2, (8, CHUNK)) + 0.25) * (1.0 / 6.0)
            sn, cs = sinpi_cospi(order * s)
            e = jnp.where(s < 1.0, 1.0 - s * s, 0.0)
            info.append((sep, s, e, cs * order))
            x2 = jnp.concatenate([sn, ones_rows], axis=0).astype(BF16)
            xs.append(jnp.concatenate([oh_i[u], oh_j[u], x2, jnp.zeros((112, CHUNK), BF16)], axis=0))
        qs = [dot(jnp.concatenate([wt[bs[u]], rb[...]], axis=1), xs[u]) for u in R]
        hd = []
        for u in R:
            q = qs[u]
            t = jnp.tanh(q)
            h = q + q * t
            d = (1.0 + t) + h * (1.0 - t)
            hd.append(jnp.concatenate([h.astype(BF16), d.astype(BF16)], axis=0))
        rs = []
        for u in range(0, GROUP, 2):
            both = dot(w2[...], jnp.concatenate([hd[u], hd[u + 1]], axis=1))
            rs += [both[:, :CHUNK], both[:, CHUNK:]]
        fs = []
        for u in R:
            sep, s, e, cn = info[u]
            terms = rs[u][:8] * cn * (np.pi * e * e) + rs[u][8:] * (-4.0 * s * e)
            ct = jnp.sum(terms, axis=0, keepdims=True)
            f = sep * (ct / (36.0 * s))
            fh = f.astype(BF16).astype(F32)
            fs.append(jnp.concatenate([fh, f - fh], axis=0).astype(BF16))
        for u in R:
            both = dot_nt(fs[u], xs[u][:128])
            part = both[:8] + both[8:]
            acc[plan[0, bs[u]]] += jnp.where(halves, part, 0.0)
            acc[plan[1, bs[u]]] += jnp.where(halves, 0.0, part)
        return c

    lax.fori_loop(0, (n + GROUP - 1) // GROUP, chunk_group, 0)
    out[...] = (acc[...] - jnp.roll(acc[...], 64, axis=2)).reshape(4, 4, 4, 8, LANES)


def return_kernel(fsum, pos_in, vel_in, held, places, forces, moved, embeds, pos_v, vel_v, landed, lhs, send1, recv1, send2, recv2, esend, erecv, loc, fs, fr, s1, r1, s2, r2, s3, r3):
    me = position()
    barrier = pltpu.get_barrier_semaphore()
    partners = greet(me, -1, True)
    local = []
    for i, (x, y) in enumerate(((pos_in, pos_v), (vel_in, vel_v))):
        local.append(pltpu.make_async_copy(x, y, loc.at[i]))
        local[-1].start()
    lhs[...] = jnp.zeros_like(lhs)
    at = 0
    for i, (s, owned) in enumerate(OWNERS):
        for c in owned:
            part = fsum[tuple(x + 2 * d + 1 for x, d in zip(c, s))]
            if i % 2:
                part = pltpu.roll(part, 4, 0)
            lhs[8 * (i // 2):8 * (i // 2) + 8, at:at + 64] = part[:, :64]
            at += 64
    wait_all(local)
    for j, c in enumerate(OWNERS[0][1]):
        velocity = vel_v[c[0], c[1], :, c[2], :]
        lhs[80:83, 64 * j:64 * j + 64] = pos_v[c[0], c[1], :, c[2], :] + 0.5 * velocity
        lhs[84:87, 64 * j:64 * j + 64] = velocity
    rows = dot(lhs[...].astype(BF16), places[...])
    send1[...] = jnp.transpose(jnp.concatenate([rows, jnp.zeros((32, 256), F32)], axis=0)).astype(BF16)
    pl.semaphore_wait(barrier, partners)
    first = exchange(me, plane_partner, 16, 16, send1, recv1, s1, r1)
    back = []
    for i, (s, own, ghost) in enumerate(BOXES):
        copy = pltpu.make_async_remote_copy(src_ref=box(fsum, ghost), dst_ref=box(landed.at[i], own), send_sem=fs.at[i], recv_sem=fr.at[i], device_id=shifted(me, s, 1), device_id_type=MESH)
        copy.start()
        back.append(copy)
    out = iota((256, 256), 0)
    source = iota((256, 256), 1)
    want = ((out // 2) % 16) * 16 + (out // 32) * 2 + out % 2
    perm2 = jnp.where(source == want, 1.0, 0.0).astype(BF16)
    esend[...] = dot(perm2, held[...]).astype(BF16)
    rows_sent = exchange(me, line_partner, 8, 32, esend, erecv, s3, r3)
    want = (out % 16) * 16 + (out // 32) * 2 + (out // 16) % 2
    perm = jnp.where(source == want, 1.0, 0.0).astype(BF16)
    wait_all(first)
    send2[...] = dot(perm, recv1[...]).astype(BF16)
    last = exchange(me, line_partner, 8, 32, send2, recv2, s2, r2)
    wait_all(back)
    for c in np.ndindex(2, 2, 2):
        total = fsum[c[0] + 1, c[1] + 1, c[2] + 1]
        for i, (s, own, ghost) in enumerate(BOXES):
            if all(lo <= x < hi for x, (lo, hi) in zip(c, own)):
                total = total + landed[i, c[0], c[1], c[2]]
        forces[c[0], c[1], c[2]] = total
    wait_all(rows_sent)
    embeds[...] = erecv[...]
    wait_all(last)
    for h in range(2):
        by_source = jnp.concatenate([recv2[32 * g + 16 * h:32 * g + 16 * h + 16] for g in range(8)], axis=0)
        by_source = jnp.transpose(by_source.astype(F32))
        sums = [None, None]
        for i, (s, _) in enumerate(OWNERS):
            part = turned(by_source[8 * (i // 2):8 * (i // 2) + 8], s)
            sums[i % 2] = part if sums[i % 2] is None else sums[i % 2] + part
        total = sums[0] + pltpu.roll(sums[1], 4, 0)
        base = by_source[80:88]
        moved[16 * h:16 * h + 8] = base + 0.25 * total
        moved[16 * h + 8:16 * h + 16] = pltpu.roll(base, 4, 0) + 0.5 * total


def finish_kernel(forces, moved, embeds, forces_out, motion_out, embeds_out):
    for c in np.ndindex(2, 2, 2):
        forces_out[c[0], c[1], :, c[2], :] = forces[c[0], c[1], c[2]][:3, :64]
    for v in range(6):
        for h in range(2):
            at = 16 * h + 8 * (v // 3) + v % 3
            motion_out[v, h:h + 1, :] = moved[at:at + 1, :]
    embeds_out[...] = embeds[...].reshape(128, 2, 256)


def per_device(positions, velocity, atom_embed, embed_proj, radial_weight, latent_bias, energy_weight, block_list, block_count, move_slot, move_dest):
    any_, vmem, smem, hbm = (pl.BlockSpec(memory_space=m) for m in (pl.ANY, pltpu.VMEM, pltpu.SMEM, pltpu.HBM))
    dma = pltpu.SemaphoreType.DMA
    array = jax.ShapeDtypeStruct
    pos_rows, vel_rows = (x.transpose(0, 1, 3, 2, 4) for x in (positions, velocity))
    dest_row = move_dest.reshape(1, 128)
    spaces = pltpu.VMEM((2, 2, 3, 2, 64), F32)
    gemb, held, g1, g2, rc, projt, rb, w2, places, plan, tot = pl.pallas_call(
        halo_kernel,
        out_shape=(
            array((4, 4, 4, 64, 256), BF16),
            array((256, 256), BF16),
            array((32, 96, 64), BF16),
            array((32, 32, 64), BF16),
            array((32, 128, LANES), F32),
            array((256, 256), BF16),
            array((256, 128), BF16),
            array((16, 512), BF16),
            array((N_ROWS, 256), BF16),
            array((2, 32), jnp.int32),
            array((32,), jnp.int32),
        ),
        in_specs=[hbm] * 9 + [smem],
        out_specs=(any_,) + (vmem,) * 8 + (smem,) * 2,
        scratch_shapes=[
            pltpu.VMEM((4, 4, 4, 8, LANES), F32),
            spaces,
            pltpu.VMEM((2, 2, 2, 64, 256), BF16),
            pltpu.VMEM((1, 128), jnp.int32),
            pltpu.VMEM((1, 128), jnp.int32),
            pltpu.VMEM((256, 256), BF16),
            pltpu.VMEM((8, 256), BF16),
            pltpu.VMEM((1, 256), F32),
            pltpu.VMEM((256,), BF16),
            pltpu.VMEM((256, 256), BF16),
            pltpu.VMEM((256, 256), BF16),
            pltpu.SMEM((1, 2, 32), jnp.int32),
            pltpu.SMEM((3, 16), jnp.int32),
        ]
        + [dma((10,))] + [dma((N_BOX,))] * 4 + [dma((16,))] * 2,
        compiler_params=pltpu.CompilerParams(collective_id=0, has_side_effects=True, vmem_limit_bytes=16 * 1024 * 1024),
        name="halo",
    )(*(pltpu.with_memory_space_constraint(x, pltpu.HBM) for x in (pos_rows, atom_embed, move_slot, dest_row, block_list, embed_proj, radial_weight, latent_bias.reshape(1, 256), energy_weight)), block_count)
    fsum = pl.pallas_call(
        pair_kernel,
        out_shape=array((4, 4, 4, 8, LANES), F32),
        in_specs=[smem] * 3 + [vmem] * 7,
        out_specs=vmem,
        scratch_shapes=[
            pltpu.VMEM((32, 256, 128), BF16),
            pltpu.VMEM((64, 8, LANES), F32),
            pltpu.SMEM((MAXCH + GROUP,), jnp.int32),
            pltpu.SMEM((MAXCH + GROUP,), jnp.int32),
        ],
        compiler_params=pltpu.CompilerParams(vmem_limit_bytes=24 * 1024 * 1024),
        name="pairs",
    )(plan, block_count, tot, gemb.reshape(64, 64, 256), g1, g2, rc, projt, rb, w2)
    raw = pl.pallas_call(
        return_kernel,
        out_shape=(array((2, 2, 2, 8, LANES), F32), array((32, LANES), F32), array((256, 256), BF16)),
        in_specs=[vmem] + [hbm] * 2 + [vmem] * 2,
        out_specs=(vmem,) * 3,
        scratch_shapes=[spaces, spaces, pltpu.VMEM((N_BOX, 2, 2, 2, 8, LANES), F32), pltpu.VMEM((96, N_ROWS), F32)]
        + [pltpu.VMEM((256, LANES), BF16)] * 4
        + [pltpu.VMEM((256, 256), BF16)] * 2
        + [dma((2,))] + [dma((N_BOX,))] * 2 + [dma((16,))] * 2 + [dma((8,))] * 4,
        compiler_params=pltpu.CompilerParams(collective_id=1, has_side_effects=True, vmem_limit_bytes=16 * 1024 * 1024),
        name="give_back",
    )(fsum, *(pltpu.with_memory_space_constraint(x, pltpu.HBM) for x in (pos_rows, vel_rows)), held, places)
    forces, motion, embeds = pl.pallas_call(
        finish_kernel,
        out_shape=(array((2, 2, 3, 2, 64), F32), array((6, 2, 128), F32), array((128, 2, 256), BF16)),
        in_specs=[vmem] * 3,
        out_specs=(vmem,) * 3,
        compiler_params=pltpu.CompilerParams(vmem_limit_bytes=8 * 1024 * 1024),
        name="finish",
    )(*raw)
    return forces.transpose(0, 1, 3, 2, 4), motion.transpose(2, 1, 0), embeds


def solution(mesh):
    placed = (
        P("gx", "gy", "gz", None, None),
        P("gx", "gy", "gz", None, None),
        P("gx", "gy", "gz", None, None),
        P(),
        P(),
        P(),
        P(),
        P(("gx", "gy", "gz"), None, None),
        P(("gx", "gy", "gz")),
        P(("gx", "gy", "gz"), None),
        P(("gx", "gy", "gz"), None),
    )
    return jax.shard_map(
        per_device,
        mesh=mesh,
        in_specs=placed,
        out_specs=(
            P("gx", "gy", "gz", None, None),
            P(("gx", "gy", "gz"), None, None),
            P(("gx", "gy", "gz"), None, None),
        ),
        check_vma=False,
    )
```

```python
import functools

import jax
import jax.numpy as jnp
import numpy as np
from jax import lax
from jax.experimental import pallas as pl
from jax.experimental.pallas import tpu as pltpu
from jax.sharding import PartitionSpec as P

F32, BF16 = jnp.float32, jnp.bfloat16
MESH = pl.DeviceIdType.MESH
OFFSETS = np.array([[0, 0, 0], [1, 0, 0], [0, 1, 0], [0, 0, 1], [1, 1, 0], [1, 0, 1], [0, 1, 1], [1, 1, 1], [1, 1, -1], [1, -1, 1], [-1, 1, 1], [1, -1, 0], [1, 0, -1], [0, 1, -1]], np.int32)
LANES = 128
GROUP = 12
WIDE = 256
WIDE_GROUP = 6
MAXCH = 32 * 16
SIZES = (8, 4, 4)


def ghost_boxes():
    need = {}
    for a in np.ndindex(2, 2, 2):
        for o in OFFSETS:
            b = [int(x) for x in np.array(a) + o]
            s = tuple(-1 if x < 0 else (1 if x > 1 else 0) for x in b)
            if any(s):
                need.setdefault(s, []).append([x - 2 * y for x, y in zip(b, s)])
    boxes = []
    for s in sorted(need, key=lambda s: (-s[0], -len(set(map(tuple, need[s]))), s)):
        own = [(min(c[d] for c in need[s]), max(c[d] for c in need[s]) + 1) for d in range(3)]
        boxes.append((s, own, [(lo + 2 * s[d] + 1, hi + 2 * s[d] + 1) for d, (lo, hi) in enumerate(own)]))
    return boxes


BOXES = ghost_boxes()
N_BOX = len(BOXES)


def box(ref, ranges):
    return ref.at[tuple(pl.ds(lo, hi - lo) for lo, hi in ranges)]


def dot(a, b):
    return jnp.dot(a, b, preferred_element_type=F32)


def dot_nt(a, b):
    return lax.dot_general(a, b, (((1,), (1,)), ((), ())), preferred_element_type=F32)


def iota(shape, dim):
    return lax.broadcasted_iota(jnp.int32, shape, dim)


def position():
    return tuple(lax.axis_index(a) for a in ("gx", "gy", "gz"))


def shifted(me, s, sign):
    return tuple(lax.rem(m + sign * d + n, n) if d else m for m, d, n in zip(me, s, SIZES))


def greet(me, toward, line):
    barrier = pltpu.get_barrier_semaphore()
    for s, _, _ in BOXES:
        pl.semaphore_signal(barrier, inc=1, device_id=shifted(me, s, toward), device_id_type=MESH)
    for k in range(1, 16):
        pl.semaphore_signal(barrier, inc=1, device_id=plane_partner(me, k)[0], device_id_type=MESH)
    for k in range(1, 8 if line else 1):
        pl.semaphore_signal(barrier, inc=1, device_id=line_partner(me, k)[0], device_id_type=MESH)
    return N_BOX + 15 + (7 if line else 0)


def plane_partner(me, k):
    at = lax.rem(me[1] * 4 + me[2] + k, 16)
    return (me[0], at // 4, lax.rem(at, 4)), at


def line_partner(me, k):
    at = lax.rem(me[0] + k, 8)
    return (at, me[1], me[2]), at


def exchange(me, partner, count, rows, src, dst, send_sem, recv_sem):
    copies = []
    mine = me[0] if count == 8 else me[1] * 4 + me[2]
    here = pl.ds(pl.multiple_of(mine * rows, rows), rows)
    for k in range(1, count):
        device, at = partner(me, k)
        copy = pltpu.make_async_remote_copy(
            src_ref=src.at[pl.ds(pl.multiple_of(at * rows, rows), rows)],
            dst_ref=dst.at[here],
            send_sem=send_sem.at[k],
            recv_sem=recv_sem.at[k],
            device_id=device,
            device_id_type=MESH,
        )
        copy.start()
        copies.append(copy)
    dst[here] = src[here]
    return copies


def wait_all(copies):
    for copy in copies:
        copy.wait()


def leaving(dest, slot):
    dest_f = dest.astype(F32)
    row = jnp.broadcast_to(dest_f, (128, LANES))
    col = jnp.transpose(row)
    earlier = jnp.logical_and(col == row, iota((128, 128), 0) < iota((128, 128), 1))
    rank = jnp.sum(jnp.where(earlier, 1.0, 0.0), axis=0, keepdims=True)
    gx = jnp.floor(dest_f * (1.0 / 16.0))
    place = 2.0 * ((dest_f - 16.0 * gx) * 8.0 + gx) + rank
    sub = iota((8, LANES), 0)
    return jnp.where(sub == 4, slot.astype(F32), jnp.where(sub == 5, place, 0.0))


def places_of(rows):
    return jnp.where(iota((256, LANES), 0).astype(F32) == rows[5:6], 1.0, 0.0).astype(BF16)


def slots_of(rows, cells):
    at = iota((64, LANES), 0)
    hits = [(at + (c[0] * 4 + c[1] * 2 + c[2]) * 64).astype(F32) == rows[4:5] for c in cells]
    return jnp.where(jnp.concatenate(hits, axis=0), 1.0, 0.0).astype(BF16)


def cells_in(own):
    return [c for c in np.ndindex(2, 2, 2) if all(lo <= x < hi for x, (lo, hi) in zip(c, own))]


OWNERS = [((0, 0, 0), cells_in([(0, 2)] * 3))] + [(s, cells_in(own)) for s, own, _ in BOXES]
N_ROWS = 64 * sum(len(cells) for _, cells in OWNERS)


def turned(x, s):
    lane = iota(x.shape, 1)
    if s[0]:
        x = pltpu.roll(x, (16 * s[0]) % 128, 1)
    for size, step, at in ((s[1], 4, lane // 4 % 4), (s[2], 1, lane % 4)):
        if size:
            x = jnp.where(at == (0 if size > 0 else 3), pltpu.roll(x, (-3 * step * size) % 128, 1), pltpu.roll(x, (step * size) % 128, 1))
    return x


def shift_rows(offset, lanes):
    x, y, z = [(8 * v).astype(F32) for v in offset]
    row = iota((8, lanes), 0)
    return jnp.where(row == 0, x, jnp.where(row == 1, y, jnp.where(row == 2, z, 0.0)))


def halo_kernel(pos_in, emb, slot, dest, blk_in, proj, rw, bias, ew, cnt, gemb, held, g1, g2, rc, projt, rb, w2, places, plan, tot,
                pos, pos_v, emb_v, slot_v, dest_v, proj_v, rw_v, bias_v, ew_v, send1, recv1, blk, offs, loc, es, er, ps, pr, s1, r1):
    me = position()
    barrier = pltpu.get_barrier_semaphore()
    pos[...] = jnp.zeros_like(pos)
    for c, o in enumerate(OFFSETS):
        for d in range(3):
            offs[d, c] = int(o[d])
    partners = greet(me, 1, False)
    own = [(1, 3)] * 3
    local = []
    for i, (x, y) in enumerate(((pos_in, pos_v), (slot, slot_v), (dest, dest_v), (emb, emb_v), (blk_in, blk), (proj, proj_v), (rw, rw_v), (bias, bias_v), (ew, ew_v), (emb, box(gemb, own)))):
        local.append(pltpu.make_async_copy(x, y, loc.at[i]))
        local[-1].start()
    for copy in local[:3]:
        copy.wait()
    rows_out = leaving(dest_v[...], slot_v[...])
    for c in np.ndindex(2, 2, 2):
        pos[c[0] + 1, c[1] + 1, c[2] + 1] = rows_out
        pos[c[0] + 1, c[1] + 1, c[2] + 1, 0:3, 0:64] = pos_v[c[0], c[1], :, c[2], :]
    pl.semaphore_wait(barrier, partners)
    halo = []
    for a, b, x, y in ((pos, pos, ps, pr), (emb, gemb, es, er)):
        copies = []
        for i, (s, src, dst) in enumerate(BOXES):
            start = box(a, [(lo + 1, hi + 1) for lo, hi in src]) if a is pos else box(a, src)
            copies.append(pltpu.make_async_remote_copy(src_ref=start, dst_ref=box(b, dst), send_sem=x.at[i], recv_sem=y.at[i], device_id=shifted(me, s, -1), device_id_type=MESH))
            copies[-1].start()
        halo.append(copies)
    for copy in local[3:]:
        copy.wait()
    place = dot_nt(places_of(rows_out), slots_of(rows_out, OWNERS[0][1])).astype(BF16)
    send1[...] = dot(place, emb_v[...].reshape(512, 256)).astype(BF16)
    rows = exchange(me, plane_partner, 16, 16, send1, recv1, s1, r1)
    projt[...] = (0.5 * jnp.transpose(proj_v[...]).astype(F32)).astype(BF16)
    half = 0.5 * bias_v[...]
    b1 = half.astype(BF16).astype(F32)
    b2 = (half - b1).astype(BF16).astype(F32)
    row8 = iota((8, 256), 0)
    biases = jnp.where(row8 == 0, b1, jnp.where(row8 == 1, b2, jnp.where(row8 == 2, half - b1 - b2, 0.0)))
    rwf = rw_v[...].astype(F32)
    ewf = ew_v[...].astype(F32).reshape(1, 256)
    rb[...] = jnp.transpose(jnp.concatenate([0.5 * rwf, biases, jnp.zeros((112, 256), F32)], axis=0)).astype(BF16)
    z8 = jnp.zeros((8, 256), F32)
    w2[:, :256] = jnp.concatenate([z8, jnp.where(row8 == 0, ewf, 0.0)], axis=0).astype(BF16)
    w2[:, 256:] = jnp.concatenate([0.5 * rwf * ewf, z8], axis=0).astype(BF16)

    jl = iota((64, 64), 1)
    il = iota((64, 64), 0)
    upper_b = jnp.where(il < jl, 1.0, 0.0).astype(BF16)
    lower_b = jnp.where(jl < il, 1.0, 0.0).astype(BF16)
    ones_b = jnp.ones((64, LANES), BF16)
    lane = iota((64, LANES), 1)

    def pos_at(c):
        return jnp.where(iota((8, 64), 0) < 3, pos[c // 16, c // 4 % 4, c % 4][:, :64], 0.0)

    def prepare(b):
        a, code = blk[0, 0, b], blk[0, 1, b]
        off = [offs[d, code] for d in range(3)]
        ca = ((a // 4 + 1) * 4 + (a // 2) % 2 + 1) * 4 + a % 2 + 1
        cb = ca + (off[0] * 4 + off[1]) * 4 + off[2]
        plan[0, b] = ca
        plan[1, b] = cb
        sh = shift_rows(off, 64)
        pa, pb = pos_at(ca), pos_at(cb)
        pbs = pb + sh
        pat = jnp.transpose(pa)
        d2 = None
        for c in range(3):
            df = pbs[c:c + 1, :] - pat[:, c:c + 1]
            d2 = df * df if d2 is None else d2 + df * df
        keep = jnp.logical_and(d2 + 0.25 < 36.001, jnp.logical_or(code != 0, il < jl))
        keep = jnp.where(jnp.logical_and(keep, b < cnt[0]), 1.0, 0.0)
        keep_b = keep.astype(BF16)
        counts = dot(keep_b, ones_b)
        prefix = dot(keep_b, upper_b)
        start = dot(lower_b, counts.astype(BF16))
        rc[b, 0:64] = start
        rc[b, 64:128] = start + counts
        local = jnp.where(keep > 0.5, prefix, 255.0)
        hi = jnp.floor(start * (1.0 / 64.0)) * 64.0
        side = jnp.where(lane == 64, hi, jnp.where(lane == 65, start - hi, 0.0))
        zt = jnp.transpose(jnp.concatenate([local, side[:, 64:]], axis=1))[:72]
        ah = pa.astype(BF16).astype(F32)
        bh = pb.astype(BF16).astype(F32)
        far = jnp.concatenate([sh, jnp.zeros_like(sh)], axis=0)
        g1[b] = jnp.concatenate([zt, ah, pa - ah, jnp.zeros((8, 64), F32)], axis=0).astype(BF16)
        g2[b] = jnp.concatenate([bh, pb - bh, far], axis=0).astype(BF16)
        tot[b] = jnp.sum(keep).astype(jnp.int32)
    wait_all(halo[0])

    def prep_group(g, c):
        for u in range(8):
            prepare(g * 8 + u)
        return c

    lax.fori_loop(0, 4, prep_group, 0)
    at = 0
    for i, (s, owned) in enumerate(OWNERS):
        first = tuple(x + 2 * d + 1 for x, d in zip(owned[0], s))
        rows_out = pos[first]
        size = 64 * len(owned)
        places[at:at + size] = dot_nt(slots_of(rows_out, owned), places_of(rows_out)).astype(BF16)
        at += size
    wait_all(rows)
    held[...] = recv1[...]
    wait_all(halo[1])


def sinpi_cospi(theta):
    m = jnp.round(theta)
    f = theta - m
    z = f * f
    sn = f * (3.14159265 + z * (-5.16771278 + z * (2.55016404 + z * (-0.599264529 + z * (0.0821458866 + z * -0.00737043094)))))
    cs = 1.0 + z * (-4.93480220 + z * (4.05871213 + z * (-1.33526277 + z * (0.235330630 + z * (-0.0258068913 + z * 0.00192957431)))))
    sign = 1.0 - 2.0 * (m - 2.0 * jnp.floor(0.5 * m))
    return sn * sign, cs * sign


def pair_kernel(plan, cnt, tot, gemb, g1, g2, rc, projt, rb, w2, out, wt, acc, tab_b, tab_k, rest_b, rest_k):
    def project(g, c):
        for u in range(0, 8, 2):
            four = [gemb[plan[d, g * 8 + v]] for v in (u, u + 1) for d in range(2)]
            both = dot_nt(projt[...], jnp.concatenate(four, axis=0)).astype(BF16)
            wt[g * 8 + u] = both[:, :LANES]
            wt[g * 8 + u + 1] = both[:, LANES:]
        return c

    lax.fori_loop(0, (cnt[0] + 7) // 8, project, 0)

    def fill_block(b, c):
        n, m = c
        wide_chunks = (tot[b] + WIDE - LANES - 1) // WIDE

        def put(t, n):
            tab_b[n] = b
            tab_k[n] = t * WIDE
            return n + 1

        rest_b[m] = b
        rest_k[m] = wide_chunks * WIDE
        return lax.fori_loop(0, wide_chunks, put, n), m + jnp.where(tot[b] > wide_chunks * WIDE, 1, 0)

    n, m = lax.fori_loop(0, cnt[0], fill_block, (0, 0))
    for u in range(WIDE_GROUP):
        tab_b[n + u] = 0
        tab_k[n + u] = 1 << 20
    for u in range(GROUP):
        rest_b[m + u] = 0
        rest_k[m + u] = 1 << 20

    acc[...] = jnp.zeros_like(acc)
    halves = iota((8, LANES), 1) < 64

    def run(chunk, group, tab_b, tab_k, count):
        kl = iota((1, chunk), 1)
        sub = iota((8, chunk), 0)
        order = (sub + 1).astype(F32)
        ones_rows = jnp.where(sub < 3, 1.0, 0.0)

        def wide(x):
            return jnp.concatenate([x] * (chunk // LANES), axis=1)

        def chunk_group(g, c):
            R = range(group)
            bs = [tab_b[g * group + u] for u in R]
            ks = [(kl + tab_k[g * group + u]).astype(F32) for u in R]
            oh_i = []
            for u in R:
                hit = jnp.logical_and(ks[u] >= wide(rc[bs[u], 0:64]), ks[u] < wide(rc[bs[u], 64:128]))
                oh_i.append(jnp.where(hit, 1.0, 0.0).astype(BF16))
            got = [dot(g1[bs[u]], oh_i[u]) for u in R]
            oh_j = []
            for u in R:
                want = ks[u] - got[u][64:65] - got[u][65:66]
                oh_j.append(jnp.where(got[u][:64] == want, 1.0, 0.0).astype(BF16))
            gotb = [dot(g2[bs[u]], oh_j[u]) for u in R]
            info = []
            xs = []
            for u in R:
                sep = (gotb[u][:8] + gotb[u][8:16] + gotb[u][16:24]) - (got[u][72:80] + got[u][80:88])
                sq = sep * sep
                d2 = sq[0:1] + sq[1:2] + sq[2:3]
                s = jnp.sqrt(jnp.broadcast_to(d2, (8, chunk)) + 0.25) * (1.0 / 6.0)
                sn, cs = sinpi_cospi(order * s)
                e = jnp.where(s < 1.0, 1.0 - s * s, 0.0)
                info.append((sep, s, e, cs * order))
                x2 = jnp.concatenate([sn, ones_rows], axis=0).astype(BF16)
                xs.append(jnp.concatenate([oh_i[u], oh_j[u], x2, jnp.zeros((112, chunk), BF16)], axis=0))
            qs = [dot(jnp.concatenate([wt[bs[u]], rb[...]], axis=1), xs[u]) for u in R]
            hd = []
            for u in R:
                q = qs[u]
                t = jnp.tanh(q)
                h = q + q * t
                d = (1.0 + t) + h * (1.0 - t)
                hd.append(jnp.concatenate([h.astype(BF16), d.astype(BF16)], axis=0))
            rs = []
            for u in range(0, group, 2 if chunk == LANES else 1):
                both = dot(w2[...], jnp.concatenate(hd[u:u + 2], axis=1) if chunk == LANES else hd[u])
                rs += [both[:, :LANES], both[:, LANES:]] if chunk == LANES else [both]
            fs = []
            for u in R:
                sep, s, e, cn = info[u]
                terms = rs[u][:8] * cn * (np.pi * e * e) + rs[u][8:] * (-4.0 * s * e)
                ct = jnp.sum(terms, axis=0, keepdims=True)
                f = sep * (ct / (36.0 * s))
                fh = f.astype(BF16).astype(F32)
                fs.append(jnp.concatenate([fh, f - fh], axis=0).astype(BF16))
            for u in R:
                both = dot_nt(fs[u], xs[u][:128])
                part = both[:8] + both[8:]
                acc[plan[0, bs[u]]] += jnp.where(halves, part, 0.0)
                acc[plan[1, bs[u]]] += jnp.where(halves, 0.0, part)
            return c

        lax.fori_loop(0, (count + group - 1) // group, chunk_group, 0)

    run(WIDE, WIDE_GROUP, tab_b, tab_k, n)
    run(LANES, GROUP, rest_b, rest_k, m)
    out[...] = (acc[...] - jnp.roll(acc[...], 64, axis=2)).reshape(4, 4, 4, 8, LANES)


def return_kernel(fsum, pos_in, vel_in, held, places, forces, moved, embeds, pos_v, vel_v, landed, lhs, send1, recv1, send2, recv2, esend, erecv, loc, fs, fr, s1, r1, s2, r2, s3, r3):
    me = position()
    barrier = pltpu.get_barrier_semaphore()
    partners = greet(me, -1, True)
    local = []
    for i, (x, y) in enumerate(((pos_in, pos_v), (vel_in, vel_v))):
        local.append(pltpu.make_async_copy(x, y, loc.at[i]))
        local[-1].start()
    lhs[...] = jnp.zeros_like(lhs)
    at = 0
    for i, (s, owned) in enumerate(OWNERS):
        for c in owned:
            part = fsum[tuple(x + 2 * d + 1 for x, d in zip(c, s))]
            if i % 2:
                part = pltpu.roll(part, 4, 0)
            lhs[8 * (i // 2):8 * (i // 2) + 8, at:at + 64] = part[:, :64]
            at += 64
    wait_all(local)
    for j, c in enumerate(OWNERS[0][1]):
        velocity = vel_v[c[0], c[1], :, c[2], :]
        lhs[80:83, 64 * j:64 * j + 64] = pos_v[c[0], c[1], :, c[2], :] + 0.5 * velocity
        lhs[84:87, 64 * j:64 * j + 64] = velocity
    rows = dot(lhs[...].astype(BF16), places[...])
    send1[...] = jnp.transpose(jnp.concatenate([rows, jnp.zeros((32, 256), F32)], axis=0)).astype(BF16)
    pl.semaphore_wait(barrier, partners)
    first = exchange(me, plane_partner, 16, 16, send1, recv1, s1, r1)
    back = []
    for i, (s, own, ghost) in enumerate(BOXES):
        copy = pltpu.make_async_remote_copy(src_ref=box(fsum, ghost), dst_ref=box(landed.at[i], own), send_sem=fs.at[i], recv_sem=fr.at[i], device_id=shifted(me, s, 1), device_id_type=MESH)
        copy.start()
        back.append(copy)
    out = iota((256, 256), 0)
    source = iota((256, 256), 1)
    want = ((out // 2) % 16) * 16 + (out // 32) * 2 + out % 2
    perm2 = jnp.where(source == want, 1.0, 0.0).astype(BF16)
    esend[...] = dot(perm2, held[...]).astype(BF16)
    rows_sent = exchange(me, line_partner, 8, 32, esend, erecv, s3, r3)
    want = (out % 16) * 16 + (out // 32) * 2 + (out // 16) % 2
    perm = jnp.where(source == want, 1.0, 0.0).astype(BF16)
    wait_all(first)
    send2[...] = dot(perm, recv1[...]).astype(BF16)
    last = exchange(me, line_partner, 8, 32, send2, recv2, s2, r2)
    wait_all(back)
    for c in np.ndindex(2, 2, 2):
        total = fsum[c[0] + 1, c[1] + 1, c[2] + 1]
        for i, (s, own, ghost) in enumerate(BOXES):
            if all(lo <= x < hi for x, (lo, hi) in zip(c, own)):
                total = total + landed[i, c[0], c[1], c[2]]
        forces[c[0], c[1], c[2]] = total
    wait_all(rows_sent)
    embeds[...] = erecv[...]
    wait_all(last)
    for h in range(2):
        by_source = jnp.concatenate([recv2[32 * g + 16 * h:32 * g + 16 * h + 16] for g in range(8)], axis=0)
        by_source = jnp.transpose(by_source.astype(F32))
        sums = [None, None]
        for i, (s, _) in enumerate(OWNERS):
            part = turned(by_source[8 * (i // 2):8 * (i // 2) + 8], s)
            sums[i % 2] = part if sums[i % 2] is None else sums[i % 2] + part
        total = sums[0] + pltpu.roll(sums[1], 4, 0)
        base = by_source[80:88]
        moved[16 * h:16 * h + 8] = base + 0.25 * total
        moved[16 * h + 8:16 * h + 16] = pltpu.roll(base, 4, 0) + 0.5 * total


def finish_kernel(forces, moved, embeds, forces_out, motion_out, embeds_out):
    for c in np.ndindex(2, 2, 2):
        forces_out[c[0], c[1], :, c[2], :] = forces[c[0], c[1], c[2]][:3, :64]
    for v in range(6):
        for h in range(2):
            at = 16 * h + 8 * (v // 3) + v % 3
            motion_out[v, h:h + 1, :] = moved[at:at + 1, :]
    embeds_out[...] = embeds[...].reshape(128, 2, 256)


def per_device(positions, velocity, atom_embed, embed_proj, radial_weight, latent_bias, energy_weight, block_list, block_count, move_slot, move_dest):
    any_, vmem, smem, hbm = (pl.BlockSpec(memory_space=m) for m in (pl.ANY, pltpu.VMEM, pltpu.SMEM, pltpu.HBM))
    dma = pltpu.SemaphoreType.DMA
    array = jax.ShapeDtypeStruct
    pos_rows, vel_rows = (x.transpose(0, 1, 3, 2, 4) for x in (positions, velocity))
    dest_row = move_dest.reshape(1, 128)
    spaces = pltpu.VMEM((2, 2, 3, 2, 64), F32)
    gemb, held, g1, g2, rc, projt, rb, w2, places, plan, tot = pl.pallas_call(
        halo_kernel,
        out_shape=(
            array((4, 4, 4, 64, 256), BF16),
            array((256, 256), BF16),
            array((32, 96, 64), BF16),
            array((32, 32, 64), BF16),
            array((32, 128, LANES), F32),
            array((256, 256), BF16),
            array((256, 128), BF16),
            array((16, 512), BF16),
            array((N_ROWS, 256), BF16),
            array((2, 32), jnp.int32),
            array((32,), jnp.int32),
        ),
        in_specs=[hbm] * 9 + [smem],
        out_specs=(any_,) + (vmem,) * 8 + (smem,) * 2,
        scratch_shapes=[
            pltpu.VMEM((4, 4, 4, 8, LANES), F32),
            spaces,
            pltpu.VMEM((2, 2, 2, 64, 256), BF16),
            pltpu.VMEM((1, 128), jnp.int32),
            pltpu.VMEM((1, 128), jnp.int32),
            pltpu.VMEM((256, 256), BF16),
            pltpu.VMEM((8, 256), BF16),
            pltpu.VMEM((1, 256), F32),
            pltpu.VMEM((256,), BF16),
            pltpu.VMEM((256, 256), BF16),
            pltpu.VMEM((256, 256), BF16),
            pltpu.SMEM((1, 2, 32), jnp.int32),
            pltpu.SMEM((3, 16), jnp.int32),
        ]
        + [dma((10,))] + [dma((N_BOX,))] * 4 + [dma((16,))] * 2,
        compiler_params=pltpu.CompilerParams(collective_id=0, has_side_effects=True, vmem_limit_bytes=16 * 1024 * 1024),
        name="halo",
    )(*(pltpu.with_memory_space_constraint(x, pltpu.HBM) for x in (pos_rows, atom_embed, move_slot, dest_row, block_list, embed_proj, radial_weight, latent_bias.reshape(1, 256), energy_weight)), block_count)
    fsum = pl.pallas_call(
        pair_kernel,
        out_shape=array((4, 4, 4, 8, LANES), F32),
        in_specs=[smem] * 3 + [vmem] * 7,
        out_specs=vmem,
        scratch_shapes=[
            pltpu.VMEM((32, 256, 128), BF16),
            pltpu.VMEM((64, 8, LANES), F32),
            pltpu.SMEM((MAXCH + WIDE_GROUP,), jnp.int32),
            pltpu.SMEM((MAXCH + WIDE_GROUP,), jnp.int32),
            pltpu.SMEM((40 + GROUP,), jnp.int32),
            pltpu.SMEM((40 + GROUP,), jnp.int32),
        ],
        compiler_params=pltpu.CompilerParams(vmem_limit_bytes=24 * 1024 * 1024),
        name="pairs",
    )(plan, block_count, tot, gemb.reshape(64, 64, 256), g1, g2, rc, projt, rb, w2)
    raw = pl.pallas_call(
        return_kernel,
        out_shape=(array((2, 2, 2, 8, LANES), F32), array((32, LANES), F32), array((256, 256), BF16)),
        in_specs=[vmem] + [hbm] * 2 + [vmem] * 2,
        out_specs=(vmem,) * 3,
        scratch_shapes=[spaces, spaces, pltpu.VMEM((N_BOX, 2, 2, 2, 8, LANES), F32), pltpu.VMEM((96, N_ROWS), F32)]
        + [pltpu.VMEM((256, LANES), BF16)] * 4
        + [pltpu.VMEM((256, 256), BF16)] * 2
        + [dma((2,))] + [dma((N_BOX,))] * 2 + [dma((16,))] * 2 + [dma((8,))] * 4,
        compiler_params=pltpu.CompilerParams(collective_id=1, has_side_effects=True, vmem_limit_bytes=16 * 1024 * 1024),
        name="give_back",
    )(fsum, *(pltpu.with_memory_space_constraint(x, pltpu.HBM) for x in (pos_rows, vel_rows)), held, places)
    forces, motion, embeds = pl.pallas_call(
        finish_kernel,
        out_shape=(array((2, 2, 3, 2, 64), F32), array((6, 2, 128), F32), array((128, 2, 256), BF16)),
        in_specs=[vmem] * 3,
        out_specs=(vmem,) * 3,
        compiler_params=pltpu.CompilerParams(vmem_limit_bytes=8 * 1024 * 1024),
        name="finish",
    )(*raw)
    return forces.transpose(0, 1, 3, 2, 4), motion.transpose(2, 1, 0), embeds


def solution(mesh):
    placed = (
        P("gx", "gy", "gz", None, None),
        P("gx", "gy", "gz", None, None),
        P("gx", "gy", "gz", None, None),
        P(),
        P(),
        P(),
        P(),
        P(("gx", "gy", "gz"), None, None),
        P(("gx", "gy", "gz")),
        P(("gx", "gy", "gz"), None),
        P(("gx", "gy", "gz"), None),
    )
    return jax.shard_map(
        per_device,
        mesh=mesh,
        in_specs=placed,
        out_specs=(
            P("gx", "gy", "gz", None, None),
            P(("gx", "gy", "gz"), None, None),
            P(("gx", "gy", "gz"), None, None),
        ),
        check_vma=False,
    )
```

```python
import functools

import jax
import jax.numpy as jnp
import numpy as np
from jax import lax
from jax.experimental import pallas as pl
from jax.experimental.pallas import tpu as pltpu
from jax.sharding import PartitionSpec as P

F32, BF16 = jnp.float32, jnp.bfloat16
MESH = pl.DeviceIdType.MESH
OFFSETS = np.array([[0, 0, 0], [1, 0, 0], [0, 1, 0], [0, 0, 1], [1, 1, 0], [1, 0, 1], [0, 1, 1], [1, 1, 1], [1, 1, -1], [1, -1, 1], [-1, 1, 1], [1, -1, 0], [1, 0, -1], [0, 1, -1]], np.int32)
LANES = 128
GROUP = 12
WIDE = 256
WIDE_GROUP = 7
MAXCH = 32 * 16
SIZES = (8, 4, 4)


def ghost_boxes():
    need = {}
    for a in np.ndindex(2, 2, 2):
        for o in OFFSETS:
            b = [int(x) for x in np.array(a) + o]
            s = tuple(-1 if x < 0 else (1 if x > 1 else 0) for x in b)
            if any(s):
                need.setdefault(s, []).append([x - 2 * y for x, y in zip(b, s)])
    boxes = []
    for s in sorted(need, key=lambda s: (len(set(map(tuple, need[s]))), s)):
        own = [(min(c[d] for c in need[s]), max(c[d] for c in need[s]) + 1) for d in range(3)]
        boxes.append((s, own, [(lo + 2 * s[d] + 1, hi + 2 * s[d] + 1) for d, (lo, hi) in enumerate(own)]))
    return boxes


BOXES = ghost_boxes()
N_BOX = len(BOXES)


def box(ref, ranges):
    return ref.at[tuple(pl.ds(lo, hi - lo) for lo, hi in ranges)]


def dot(a, b):
    return jnp.dot(a, b, preferred_element_type=F32)


def dot_nt(a, b):
    return lax.dot_general(a, b, (((1,), (1,)), ((), ())), preferred_element_type=F32)


def iota(shape, dim):
    return lax.broadcasted_iota(jnp.int32, shape, dim)


def position():
    return tuple(lax.axis_index(a) for a in ("gx", "gy", "gz"))


def shifted(me, s, sign):
    return tuple(lax.rem(m + sign * d + n, n) if d else m for m, d, n in zip(me, s, SIZES))


def greet(me, toward, line):
    barrier = pltpu.get_barrier_semaphore()
    for s, _, _ in BOXES:
        pl.semaphore_signal(barrier, inc=1, device_id=shifted(me, s, toward), device_id_type=MESH)
    for k in range(1, 16):
        pl.semaphore_signal(barrier, inc=1, device_id=plane_partner(me, k)[0], device_id_type=MESH)
    for k in range(1, 8 if line else 1):
        pl.semaphore_signal(barrier, inc=1, device_id=line_partner(me, k)[0], device_id_type=MESH)
    return N_BOX + 15 + (7 if line else 0)


def plane_partner(me, k):
    at = lax.rem(me[1] * 4 + me[2] + k, 16)
    return (me[0], at // 4, lax.rem(at, 4)), at


def line_partner(me, k):
    at = lax.rem(me[0] + k, 8)
    return (at, me[1], me[2]), at


def exchange(me, partner, count, rows, src, dst, send_sem, recv_sem):
    copies = []
    mine = me[0] if count == 8 else me[1] * 4 + me[2]
    here = pl.ds(pl.multiple_of(mine * rows, rows), rows)
    for k in range(1, count):
        device, at = partner(me, k)
        copy = pltpu.make_async_remote_copy(
            src_ref=src.at[pl.ds(pl.multiple_of(at * rows, rows), rows)],
            dst_ref=dst.at[here],
            send_sem=send_sem.at[k],
            recv_sem=recv_sem.at[k],
            device_id=device,
            device_id_type=MESH,
        )
        copy.start()
        copies.append(copy)
    dst[here] = src[here]
    return copies


def wait_all(copies):
    for copy in copies:
        copy.wait()


def leaving(dest, slot):
    dest_f = dest.astype(F32)
    row = jnp.broadcast_to(dest_f, (128, LANES))
    col = jnp.transpose(row)
    earlier = jnp.logical_and(col == row, iota((128, 128), 0) < iota((128, 128), 1))
    rank = jnp.sum(jnp.where(earlier, 1.0, 0.0), axis=0, keepdims=True)
    gx = jnp.floor(dest_f * (1.0 / 16.0))
    place = 2.0 * ((dest_f - 16.0 * gx) * 8.0 + gx) + rank
    sub = iota((8, LANES), 0)
    return jnp.where(sub == 4, slot.astype(F32), jnp.where(sub == 5, place, 0.0))


def places_of(rows):
    return jnp.where(iota((256, LANES), 0).astype(F32) == rows[5:6], 1.0, 0.0).astype(BF16)


def slots_of(rows, cells):
    at = iota((64, LANES), 0)
    hits = [(at + (c[0] * 4 + c[1] * 2 + c[2]) * 64).astype(F32) == rows[4:5] for c in cells]
    return jnp.where(jnp.concatenate(hits, axis=0), 1.0, 0.0).astype(BF16)


def cells_in(own):
    return [c for c in np.ndindex(2, 2, 2) if all(lo <= x < hi for x, (lo, hi) in zip(c, own))]


OWNERS = [((0, 0, 0), cells_in([(0, 2)] * 3))] + [(s, cells_in(own)) for s, own, _ in BOXES]
N_ROWS = 64 * sum(len(cells) for _, cells in OWNERS)


def turned(x, s):
    lane = iota(x.shape, 1)
    if s[0]:
        x = pltpu.roll(x, (16 * s[0]) % 128, 1)
    for size, step, at in ((s[1], 4, lane // 4 % 4), (s[2], 1, lane % 4)):
        if size:
            x = jnp.where(at == (0 if size > 0 else 3), pltpu.roll(x, (-3 * step * size) % 128, 1), pltpu.roll(x, (step * size) % 128, 1))
    return x


def shift_rows(offset, lanes):
    x, y, z = [(8 * v).astype(F32) for v in offset]
    row = iota((8, lanes), 0)
    return jnp.where(row == 0, x, jnp.where(row == 1, y, jnp.where(row == 2, z, 0.0)))


def halo_kernel(pos_in, emb, slot, dest, blk_in, proj, rw, bias, ew, cnt, gemb, held, g1, g2, rc, projt, rb, w2, ewc, places, plan, tot,
                pos, pos_v, emb_v, slot_v, dest_v, proj_v, rw_v, bias_v, ew_v, send1, recv1, blk, offs, loc, es, er, ps, pr, s1, r1):
    me = position()
    barrier = pltpu.get_barrier_semaphore()
    pos[...] = jnp.zeros_like(pos)
    for c, o in enumerate(OFFSETS):
        for d in range(3):
            offs[d, c] = int(o[d])
    partners = greet(me, 1, False)
    own = [(1, 3)] * 3
    local = []
    for i, (x, y) in enumerate(((pos_in, pos_v), (slot, slot_v), (dest, dest_v), (emb, emb_v), (blk_in, blk), (proj, proj_v), (rw, rw_v), (bias, bias_v), (ew, ew_v), (emb, box(gemb, own)))):
        local.append(pltpu.make_async_copy(x, y, loc.at[i]))
        local[-1].start()
    for copy in local[:3]:
        copy.wait()
    rows_out = leaving(dest_v[...], slot_v[...])
    for c in np.ndindex(2, 2, 2):
        pos[c[0] + 1, c[1] + 1, c[2] + 1] = rows_out
        pos[c[0] + 1, c[1] + 1, c[2] + 1, 0:3, 0:64] = pos_v[c[0], c[1], :, c[2], :]
    pl.semaphore_wait(barrier, partners)
    halo = []
    for a, b, x, y in ((pos, pos, ps, pr), (emb, gemb, es, er)):
        copies = []
        for i, (s, src, dst) in enumerate(BOXES):
            start = box(a, [(lo + 1, hi + 1) for lo, hi in src]) if a is pos else box(a, src)
            copies.append(pltpu.make_async_remote_copy(src_ref=start, dst_ref=box(b, dst), send_sem=x.at[i], recv_sem=y.at[i], device_id=shifted(me, s, -1), device_id_type=MESH))
            copies[-1].start()
        halo.append(copies)
    for copy in local[3:]:
        copy.wait()
    place = dot_nt(places_of(rows_out), slots_of(rows_out, OWNERS[0][1])).astype(BF16)
    send1[...] = dot(place, emb_v[...].reshape(512, 256)).astype(BF16)
    rows = exchange(me, plane_partner, 16, 16, send1, recv1, s1, r1)
    projt[...] = (0.5 * jnp.transpose(proj_v[...]).astype(F32)).astype(BF16)
    half = 0.5 * bias_v[...]
    b1 = half.astype(BF16).astype(F32)
    b2 = (half - b1).astype(BF16).astype(F32)
    row8 = iota((8, 256), 0)
    biases = jnp.where(row8 == 0, b1, jnp.where(row8 == 1, b2, jnp.where(row8 == 2, half - b1 - b2, 0.0)))
    rwf = rw_v[...].astype(F32)
    ewf = ew_v[...].astype(F32).reshape(1, 256)
    rb[...] = jnp.transpose(jnp.concatenate([0.5 * rwf, biases, jnp.zeros((112, 256), F32)], axis=0)).astype(BF16)
    z8 = jnp.zeros((8, 256), F32)
    w2[...] = jnp.concatenate([0.5 * rwf * ewf, z8], axis=0).astype(BF16)
    ewc[...] = jnp.transpose(jnp.broadcast_to(ewf, (LANES, 256)))

    jl = iota((64, 64), 1)
    il = iota((64, 64), 0)
    upper_b = jnp.where(il < jl, 1.0, 0.0).astype(BF16)
    lower_b = jnp.where(jl < il, 1.0, 0.0).astype(BF16)
    ones_b = jnp.ones((64, LANES), BF16)
    lane = iota((64, LANES), 1)

    def pos_at(c):
        return jnp.where(iota((8, 64), 0) < 3, pos[c // 16, c // 4 % 4, c % 4][:, :64], 0.0)

    def prepare(b):
        a, code = blk[0, 0, b], blk[0, 1, b]
        off = [offs[d, code] for d in range(3)]
        ca = ((a // 4 + 1) * 4 + (a // 2) % 2 + 1) * 4 + a % 2 + 1
        cb = ca + (off[0] * 4 + off[1]) * 4 + off[2]
        plan[0, b] = ca
        plan[1, b] = cb
        sh = shift_rows(off, 64)
        pa, pb = pos_at(ca), pos_at(cb)
        pbs = pb + sh
        pat = jnp.transpose(pa)
        d2 = None
        for c in range(3):
            df = pbs[c:c + 1, :] - pat[:, c:c + 1]
            d2 = df * df if d2 is None else d2 + df * df
        keep = jnp.logical_and(d2 + 0.25 < 36.001, jnp.logical_or(code != 0, il < jl))
        keep = jnp.where(jnp.logical_and(keep, b < cnt[0]), 1.0, 0.0)
        keep_b = keep.astype(BF16)
        counts = dot(keep_b, ones_b)
        prefix = dot(keep_b, upper_b)
        start = dot(lower_b, counts.astype(BF16))
        rc[b, 0:64] = start
        rc[b, 64:128] = start + counts
        local = jnp.where(keep > 0.5, prefix, 255.0)
        hi = jnp.floor(start * (1.0 / 64.0)) * 64.0
        side = jnp.where(lane == 64, hi, jnp.where(lane == 65, start - hi, 0.0))
        zt = jnp.transpose(jnp.concatenate([local, side[:, 64:]], axis=1))[:72]
        ah = pa.astype(BF16).astype(F32)
        bh = pb.astype(BF16).astype(F32)
        far = jnp.concatenate([sh, jnp.zeros_like(sh)], axis=0)
        g1[b] = jnp.concatenate([zt, ah, pa - ah, jnp.zeros((8, 64), F32)], axis=0).astype(BF16)
        g2[b] = jnp.concatenate([bh, pb - bh, far], axis=0).astype(BF16)
        tot[b] = jnp.sum(keep).astype(jnp.int32)
    wait_all(halo[0])

    def prep_group(g, c):
        for u in range(8):
            prepare(g * 8 + u)
        return c

    lax.fori_loop(0, 4, prep_group, 0)
    at = 0
    for i, (s, owned) in enumerate(OWNERS):
        first = tuple(x + 2 * d + 1 for x, d in zip(owned[0], s))
        rows_out = pos[first]
        size = 64 * len(owned)
        places[at:at + size] = dot_nt(slots_of(rows_out, owned), places_of(rows_out)).astype(BF16)
        at += size
    wait_all(rows)
    held[...] = recv1[...]
    wait_all(halo[1])


def sinpi_cospi(theta):
    m = jnp.round(theta)
    f = theta - m
    z = f * f
    sn = f * (3.14159265 + z * (-5.16771278 + z * (2.55016404 + z * (-0.599264529 + z * (0.0821458866 + z * -0.00737043094)))))
    cs = 1.0 + z * (-4.93480220 + z * (4.05871213 + z * (-1.33526277 + z * (0.235330630 + z * (-0.0258068913 + z * 0.00192957431)))))
    sign = 1.0 - 2.0 * (m - 2.0 * jnp.floor(0.5 * m))
    return sn * sign, cs * sign


def pair_kernel(plan, cnt, tot, gemb, g1, g2, rc, projt, rb, w2, ewc, out, wt, acc, tab_b, tab_k, rest_b, rest_k):
    def project(g, c):
        for u in range(0, 8, 2):
            four = [gemb[plan[d, g * 8 + v]] for v in (u, u + 1) for d in range(2)]
            both = dot_nt(projt[...], jnp.concatenate(four, axis=0)).astype(BF16)
            wt[g * 8 + u] = both[:, :LANES]
            wt[g * 8 + u + 1] = both[:, LANES:]
        return c

    lax.fori_loop(0, (cnt[0] + 7) // 8, project, 0)

    def fill_block(b, c):
        n, m = c
        wide_chunks = (tot[b] + WIDE - LANES - 1) // WIDE

        def put(t, n):
            tab_b[n] = b
            tab_k[n] = t * WIDE
            return n + 1

        rest_b[m] = b
        rest_k[m] = wide_chunks * WIDE
        return lax.fori_loop(0, wide_chunks, put, n), m + jnp.where(tot[b] > wide_chunks * WIDE, 1, 0)

    n, m = lax.fori_loop(0, cnt[0], fill_block, (0, 0))
    for u in range(WIDE_GROUP):
        tab_b[n + u] = 0
        tab_k[n + u] = 1 << 20
    for u in range(GROUP):
        rest_b[m + u] = 0
        rest_k[m + u] = 1 << 20

    acc[...] = jnp.zeros_like(acc)
    halves = iota((8, LANES), 1) < 64

    def run(chunk, group, tab_b, tab_k, count):
        kl = iota((1, chunk), 1)
        sub = iota((8, chunk), 0)
        order = (sub + 1).astype(F32)
        ones_rows = jnp.where(sub < 3, 1.0, 0.0)

        def wide(x):
            return jnp.concatenate([x] * (chunk // LANES), axis=1)

        def chunk_group(g, c):
            R = range(group)
            bs = [tab_b[g * group + u] for u in R]
            ks = [(kl + tab_k[g * group + u]).astype(F32) for u in R]
            oh_i = []
            for u in R:
                hit = jnp.logical_and(ks[u] >= wide(rc[bs[u], 0:64]), ks[u] < wide(rc[bs[u], 64:128]))
                oh_i.append(jnp.where(hit, 1.0, 0.0).astype(BF16))
            got = [dot(g1[bs[u]], oh_i[u]) for u in R]
            oh_j = []
            for u in R:
                want = ks[u] - got[u][64:65] - got[u][65:66]
                oh_j.append(jnp.where(got[u][:64] == want, 1.0, 0.0).astype(BF16))
            gotb = [dot(g2[bs[u]], oh_j[u]) for u in R]
            info = []
            xs = []
            for u in R:
                sep = (gotb[u][:8] + gotb[u][8:16] + gotb[u][16:24]) - (got[u][72:80] + got[u][80:88])
                sq = sep * sep
                d2 = sq[0:1] + sq[1:2] + sq[2:3]
                s = jnp.sqrt(jnp.broadcast_to(d2, (8, chunk)) + 0.25) * (1.0 / 6.0)
                sn, cs = sinpi_cospi(order * s)
                e = jnp.where(s < 1.0, 1.0 - s * s, 0.0)
                info.append((sep, s, e, cs * order))
                x2 = jnp.concatenate([sn, ones_rows], axis=0).astype(BF16)
                xs.append(jnp.concatenate([oh_i[u], oh_j[u], x2, jnp.zeros((112, chunk), BF16)], axis=0))
            qs = [dot(jnp.concatenate([wt[bs[u]], rb[...]], axis=1), xs[u]) for u in R]
            hd = []
            us = []
            for u in R:
                q = qs[u]
                t = jnp.tanh(q)
                h = q + q * t
                d = (1.0 + t) + h * (1.0 - t)
                hd.append(d.astype(BF16))
                us.append(jnp.sum((h * wide(ewc[...])).reshape(32, 8, chunk), axis=0))
            rs = []
            for u in range(0, group, 2 if chunk == LANES else 1):
                both = dot(w2[...], jnp.concatenate(hd[u:u + 2], axis=1) if chunk == LANES else hd[u])
                rs += [both[:, :LANES], both[:, LANES:]] if chunk == LANES else [both]
            fs = []
            for u in R:
                sep, s, e, cn = info[u]
                terms = rs[u][:8] * cn * (np.pi * e * e) + us[u] * (-4.0 * s * e)
                ct = jnp.sum(terms, axis=0, keepdims=True)
                f = sep * (ct / (36.0 * s))
                fh = f.astype(BF16).astype(F32)
                fs.append(jnp.concatenate([fh, f - fh], axis=0).astype(BF16))
            for u in R:
                both = dot_nt(fs[u], xs[u][:128])
                part = both[:8] + both[8:]
                acc[plan[0, bs[u]]] += jnp.where(halves, part, 0.0)
                acc[plan[1, bs[u]]] += jnp.where(halves, 0.0, part)
            return c

        lax.fori_loop(0, (count + group - 1) // group, chunk_group, 0)

    run(WIDE, WIDE_GROUP, tab_b, tab_k, n)
    run(LANES, GROUP, rest_b, rest_k, m)
    out[...] = (acc[...] - jnp.roll(acc[...], 64, axis=2)).reshape(4, 4, 4, 8, LANES)


def return_kernel(fsum, pos_in, vel_in, held, places, forces, moved, embeds, pos_v, vel_v, landed, lhs, send1, recv1, send2, recv2, esend, erecv, loc, fs, fr, s1, r1, s2, r2, s3, r3):
    me = position()
    barrier = pltpu.get_barrier_semaphore()
    partners = greet(me, -1, True)
    local = []
    for i, (x, y) in enumerate(((pos_in, pos_v), (vel_in, vel_v))):
        local.append(pltpu.make_async_copy(x, y, loc.at[i]))
        local[-1].start()
    lhs[...] = jnp.zeros_like(lhs)
    at = 0
    for i, (s, owned) in enumerate(OWNERS):
        for c in owned:
            part = fsum[tuple(x + 2 * d + 1 for x, d in zip(c, s))]
            if i % 2:
                part = pltpu.roll(part, 4, 0)
            lhs[8 * (i // 2):8 * (i // 2) + 8, at:at + 64] = part[:, :64]
            at += 64
    wait_all(local)
    for j, c in enumerate(OWNERS[0][1]):
        velocity = vel_v[c[0], c[1], :, c[2], :]
        lhs[80:83, 64 * j:64 * j + 64] = pos_v[c[0], c[1], :, c[2], :] + 0.5 * velocity
        lhs[84:87, 64 * j:64 * j + 64] = velocity
    rows = dot(lhs[...].astype(BF16), places[...])
    send1[...] = jnp.transpose(jnp.concatenate([rows, jnp.zeros((32, 256), F32)], axis=0)).astype(BF16)
    pl.semaphore_wait(barrier, partners)
    first = exchange(me, plane_partner, 16, 16, send1, recv1, s1, r1)
    back = []
    for i, (s, own, ghost) in enumerate(BOXES):
        copy = pltpu.make_async_remote_copy(src_ref=box(fsum, ghost), dst_ref=box(landed.at[i], own), send_sem=fs.at[i], recv_sem=fr.at[i], device_id=shifted(me, s, 1), device_id_type=MESH)
        copy.start()
        back.append(copy)
    out = iota((256, 256), 0)
    source = iota((256, 256), 1)
    want = ((out // 2) % 16) * 16 + (out // 32) * 2 + out % 2
    perm2 = jnp.where(source == want, 1.0, 0.0).astype(BF16)
    esend[...] = dot(perm2, held[...]).astype(BF16)
    rows_sent = exchange(me, line_partner, 8, 32, esend, erecv, s3, r3)
    want = (out % 16) * 16 + (out // 32) * 2 + (out // 16) % 2
    perm = jnp.where(source == want, 1.0, 0.0).astype(BF16)
    wait_all(first)
    send2[...] = dot(perm, recv1[...]).astype(BF16)
    last = exchange(me, line_partner, 8, 32, send2, recv2, s2, r2)
    wait_all(back)
    for c in np.ndindex(2, 2, 2):
        total = fsum[c[0] + 1, c[1] + 1, c[2] + 1]
        for i, (s, own, ghost) in enumerate(BOXES):
            if all(lo <= x < hi for x, (lo, hi) in zip(c, own)):
                total = total + landed[i, c[0], c[1], c[2]]
        forces[c[0], c[1], c[2]] = total
    wait_all(rows_sent)
    embeds[...] = erecv[...]
    wait_all(last)
    for h in range(2):
        by_source = jnp.concatenate([recv2[32 * g + 16 * h:32 * g + 16 * h + 16] for g in range(8)], axis=0)
        by_source = jnp.transpose(by_source.astype(F32))
        sums = [None, None]
        for i, (s, _) in enumerate(OWNERS):
            part = turned(by_source[8 * (i // 2):8 * (i // 2) + 8], s)
            sums[i % 2] = part if sums[i % 2] is None else sums[i % 2] + part
        total = sums[0] + pltpu.roll(sums[1], 4, 0)
        base = by_source[80:88]
        moved[16 * h:16 * h + 8] = base + 0.25 * total
        moved[16 * h + 8:16 * h + 16] = pltpu.roll(base, 4, 0) + 0.5 * total


def finish_kernel(forces, moved, embeds, forces_out, motion_out, embeds_out):
    for c in np.ndindex(2, 2, 2):
        forces_out[c[0], c[1], :, c[2], :] = forces[c[0], c[1], c[2]][:3, :64]
    for v in range(6):
        for h in range(2):
            at = 16 * h + 8 * (v // 3) + v % 3
            motion_out[v, h:h + 1, :] = moved[at:at + 1, :]
    embeds_out[...] = embeds[...].reshape(128, 2, 256)


def per_device(positions, velocity, atom_embed, embed_proj, radial_weight, latent_bias, energy_weight, block_list, block_count, move_slot, move_dest):
    any_, vmem, smem, hbm = (pl.BlockSpec(memory_space=m) for m in (pl.ANY, pltpu.VMEM, pltpu.SMEM, pltpu.HBM))
    dma = pltpu.SemaphoreType.DMA
    array = jax.ShapeDtypeStruct
    pos_rows, vel_rows = (x.transpose(0, 1, 3, 2, 4) for x in (positions, velocity))
    dest_row = move_dest.reshape(1, 128)
    spaces = pltpu.VMEM((2, 2, 3, 2, 64), F32)
    gemb, held, g1, g2, rc, projt, rb, w2, ewc, places, plan, tot = pl.pallas_call(
        halo_kernel,
        out_shape=(
            array((4, 4, 4, 64, 256), BF16),
            array((256, 256), BF16),
            array((32, 96, 64), BF16),
            array((32, 32, 64), BF16),
            array((32, 128, LANES), F32),
            array((256, 256), BF16),
            array((256, 128), BF16),
            array((16, 256), BF16),
            array((256, LANES), F32),
            array((N_ROWS, 256), BF16),
            array((2, 32), jnp.int32),
            array((32,), jnp.int32),
        ),
        in_specs=[hbm] * 9 + [smem],
        out_specs=(any_,) + (vmem,) * 9 + (smem,) * 2,
        scratch_shapes=[
            pltpu.VMEM((4, 4, 4, 8, LANES), F32),
            spaces,
            pltpu.VMEM((2, 2, 2, 64, 256), BF16),
            pltpu.VMEM((1, 128), jnp.int32),
            pltpu.VMEM((1, 128), jnp.int32),
            pltpu.VMEM((256, 256), BF16),
            pltpu.VMEM((8, 256), BF16),
            pltpu.VMEM((1, 256), F32),
            pltpu.VMEM((256,), BF16),
            pltpu.VMEM((256, 256), BF16),
            pltpu.VMEM((256, 256), BF16),
            pltpu.SMEM((1, 2, 32), jnp.int32),
            pltpu.SMEM((3, 16), jnp.int32),
        ]
        + [dma((10,))] + [dma((N_BOX,))] * 4 + [dma((16,))] * 2,
        compiler_params=pltpu.CompilerParams(collective_id=0, has_side_effects=True, vmem_limit_bytes=16 * 1024 * 1024),
        name="halo",
    )(*(pltpu.with_memory_space_constraint(x, pltpu.HBM) for x in (pos_rows, atom_embed, move_slot, dest_row, block_list, embed_proj, radial_weight, latent_bias.reshape(1, 256), energy_weight)), block_count)
    fsum = pl.pallas_call(
        pair_kernel,
        out_shape=array((4, 4, 4, 8, LANES), F32),
        in_specs=[smem] * 3 + [vmem] * 8,
        out_specs=vmem,
        scratch_shapes=[
            pltpu.VMEM((32, 256, 128), BF16),
            pltpu.VMEM((64, 8, LANES), F32),
            pltpu.SMEM((MAXCH + WIDE_GROUP,), jnp.int32),
            pltpu.SMEM((MAXCH + WIDE_GROUP,), jnp.int32),
            pltpu.SMEM((40 + GROUP,), jnp.int32),
            pltpu.SMEM((40 + GROUP,), jnp.int32),
        ],
        compiler_params=pltpu.CompilerParams(vmem_limit_bytes=24 * 1024 * 1024),
        name="pairs",
    )(plan, block_count, tot, gemb.reshape(64, 64, 256), g1, g2, rc, projt, rb, w2, ewc)
    raw = pl.pallas_call(
        return_kernel,
        out_shape=(array((2, 2, 2, 8, LANES), F32), array((32, LANES), F32), array((256, 256), BF16)),
        in_specs=[vmem] + [hbm] * 2 + [vmem] * 2,
        out_specs=(vmem,) * 3,
        scratch_shapes=[spaces, spaces, pltpu.VMEM((N_BOX, 2, 2, 2, 8, LANES), F32), pltpu.VMEM((96, N_ROWS), F32)]
        + [pltpu.VMEM((256, LANES), BF16)] * 4
        + [pltpu.VMEM((256, 256), BF16)] * 2
        + [dma((2,))] + [dma((N_BOX,))] * 2 + [dma((16,))] * 2 + [dma((8,))] * 4,
        compiler_params=pltpu.CompilerParams(collective_id=1, has_side_effects=True, vmem_limit_bytes=16 * 1024 * 1024),
        name="give_back",
    )(fsum, *(pltpu.with_memory_space_constraint(x, pltpu.HBM) for x in (pos_rows, vel_rows)), held, places)
    forces, motion, embeds = pl.pallas_call(
        finish_kernel,
        out_shape=(array((2, 2, 3, 2, 64), F32), array((6, 2, 128), F32), array((128, 2, 256), BF16)),
        in_specs=[vmem] * 3,
        out_specs=(vmem,) * 3,
        compiler_params=pltpu.CompilerParams(vmem_limit_bytes=8 * 1024 * 1024),
        name="finish",
    )(*raw)
    return forces.transpose(0, 1, 3, 2, 4), motion.transpose(2, 1, 0), embeds


def solution(mesh):
    placed = (
        P("gx", "gy", "gz", None, None),
        P("gx", "gy", "gz", None, None),
        P("gx", "gy", "gz", None, None),
        P(),
        P(),
        P(),
        P(),
        P(("gx", "gy", "gz"), None, None),
        P(("gx", "gy", "gz")),
        P(("gx", "gy", "gz"), None),
        P(("gx", "gy", "gz"), None),
    )
    return jax.shard_map(
        per_device,
        mesh=mesh,
        in_specs=placed,
        out_specs=(
            P("gx", "gy", "gz", None, None),
            P(("gx", "gy", "gz"), None, None),
            P(("gx", "gy", "gz"), None, None),
        ),
        check_vma=False,
    )
```

```python
import functools

import jax
import jax.numpy as jnp
import numpy as np
from jax import lax
from jax.experimental import pallas as pl
from jax.experimental.pallas import tpu as pltpu
from jax.sharding import PartitionSpec as P

F32, BF16 = jnp.float32, jnp.bfloat16
MESH = pl.DeviceIdType.MESH
OFFSETS = np.array([[0, 0, 0], [1, 0, 0], [0, 1, 0], [0, 0, 1], [1, 1, 0], [1, 0, 1], [0, 1, 1], [1, 1, 1], [1, 1, -1], [1, -1, 1], [-1, 1, 1], [1, -1, 0], [1, 0, -1], [0, 1, -1]], np.int32)
LANES = 128
GROUP = 16
WIDE = 256
WIDE_GROUP = 7
MAXCH = 32 * 16
SIZES = (8, 4, 4)


def ghost_boxes():
    need = {}
    for a in np.ndindex(2, 2, 2):
        for o in OFFSETS:
            b = [int(x) for x in np.array(a) + o]
            s = tuple(-1 if x < 0 else (1 if x > 1 else 0) for x in b)
            if any(s):
                need.setdefault(s, []).append([x - 2 * y for x, y in zip(b, s)])
    boxes = []
    for s in sorted(need, key=lambda s: (len(set(map(tuple, need[s]))), s)):
        own = [(min(c[d] for c in need[s]), max(c[d] for c in need[s]) + 1) for d in range(3)]
        boxes.append((s, own, [(lo + 2 * s[d] + 1, hi + 2 * s[d] + 1) for d, (lo, hi) in enumerate(own)]))
    return boxes


BOXES = ghost_boxes()
N_BOX = len(BOXES)


def box(ref, ranges):
    return ref.at[tuple(pl.ds(lo, hi - lo) for lo, hi in ranges)]


def dot(a, b):
    return jnp.dot(a, b, preferred_element_type=F32)


def dot_nt(a, b):
    return lax.dot_general(a, b, (((1,), (1,)), ((), ())), preferred_element_type=F32)


def iota(shape, dim):
    return lax.broadcasted_iota(jnp.int32, shape, dim)


def position():
    return tuple(lax.axis_index(a) for a in ("gx", "gy", "gz"))


def shifted(me, s, sign):
    return tuple(lax.rem(m + sign * d + n, n) if d else m for m, d, n in zip(me, s, SIZES))


def greet(me, toward, line):
    barrier = pltpu.get_barrier_semaphore()
    for s, _, _ in BOXES:
        pl.semaphore_signal(barrier, inc=1, device_id=shifted(me, s, toward), device_id_type=MESH)
    for k in range(1, 16):
        pl.semaphore_signal(barrier, inc=1, device_id=plane_partner(me, k)[0], device_id_type=MESH)
    for k in range(1, 8 if line else 1):
        pl.semaphore_signal(barrier, inc=1, device_id=line_partner(me, k)[0], device_id_type=MESH)
    return N_BOX + 15 + (7 if line else 0)


def plane_partner(me, k):
    at = lax.rem(me[1] * 4 + me[2] + k, 16)
    return (me[0], at // 4, lax.rem(at, 4)), at


def line_partner(me, k):
    at = lax.rem(me[0] + k, 8)
    return (at, me[1], me[2]), at


def exchange(me, partner, count, rows, src, dst, send_sem, recv_sem):
    copies = []
    mine = me[0] if count == 8 else me[1] * 4 + me[2]
    here = pl.ds(pl.multiple_of(mine * rows, rows), rows)
    for k in range(1, count):
        device, at = partner(me, k)
        copy = pltpu.make_async_remote_copy(
            src_ref=src.at[pl.ds(pl.multiple_of(at * rows, rows), rows)],
            dst_ref=dst.at[here],
            send_sem=send_sem.at[k],
            recv_sem=recv_sem.at[k],
            device_id=device,
            device_id_type=MESH,
        )
        copy.start()
        copies.append(copy)
    dst[here] = src[here]
    return copies


def wait_all(copies):
    for copy in copies:
        copy.wait()


def leaving(dest, slot):
    dest_f = dest.astype(F32)
    row = jnp.broadcast_to(dest_f, (128, LANES))
    col = jnp.transpose(row)
    earlier = jnp.logical_and(col == row, iota((128, 128), 0) < iota((128, 128), 1))
    rank = jnp.sum(jnp.where(earlier, 1.0, 0.0), axis=0, keepdims=True)
    gx = jnp.floor(dest_f * (1.0 / 16.0))
    place = 2.0 * ((dest_f - 16.0 * gx) * 8.0 + gx) + rank
    sub = iota((8, LANES), 0)
    return jnp.where(sub == 4, slot.astype(F32), jnp.where(sub == 5, place, 0.0))


def places_of(rows):
    return jnp.where(iota((256, LANES), 0).astype(F32) == rows[5:6], 1.0, 0.0).astype(BF16)


def slots_of(rows, cells):
    at = iota((64, LANES), 0)
    hits = [(at + (c[0] * 4 + c[1] * 2 + c[2]) * 64).astype(F32) == rows[4:5] for c in cells]
    return jnp.where(jnp.concatenate(hits, axis=0), 1.0, 0.0).astype(BF16)


def cells_in(own):
    return [c for c in np.ndindex(2, 2, 2) if all(lo <= x < hi for x, (lo, hi) in zip(c, own))]


OWNERS = [((0, 0, 0), cells_in([(0, 2)] * 3))] + [(s, cells_in(own)) for s, own, _ in BOXES]
N_ROWS = 64 * sum(len(cells) for _, cells in OWNERS)


def turned(x, s):
    lane = iota(x.shape, 1)
    if s[0]:
        x = pltpu.roll(x, (16 * s[0]) % 128, 1)
    for size, step, at in ((s[1], 4, lane // 4 % 4), (s[2], 1, lane % 4)):
        if size:
            x = jnp.where(at == (0 if size > 0 else 3), pltpu.roll(x, (-3 * step * size) % 128, 1), pltpu.roll(x, (step * size) % 128, 1))
    return x


def shift_rows(offset, lanes):
    x, y, z = [(8 * v).astype(F32) for v in offset]
    row = iota((8, lanes), 0)
    return jnp.where(row == 0, x, jnp.where(row == 1, y, jnp.where(row == 2, z, 0.0)))


def halo_kernel(pos_in, emb, slot, dest, blk_in, proj, rw, bias, ew, cnt, gemb, held, g1, g2, rc, projt, rb, w2, ewc, places, plan, tot,
                pos, pos_v, emb_v, slot_v, dest_v, proj_v, rw_v, bias_v, ew_v, send1, recv1, blk, offs, loc, es, er, ps, pr, s1, r1):
    me = position()
    barrier = pltpu.get_barrier_semaphore()
    pos[...] = jnp.zeros_like(pos)
    for c, o in enumerate(OFFSETS):
        for d in range(3):
            offs[d, c] = int(o[d])
    partners = greet(me, 1, False)
    own = [(1, 3)] * 3
    local = []
    for i, (x, y) in enumerate(((pos_in, pos_v), (slot, slot_v), (dest, dest_v), (emb, emb_v), (blk_in, blk), (proj, proj_v), (rw, rw_v), (bias, bias_v), (ew, ew_v), (emb, box(gemb, own)))):
        local.append(pltpu.make_async_copy(x, y, loc.at[i]))
        local[-1].start()
    for copy in local[:3]:
        copy.wait()
    rows_out = leaving(dest_v[...], slot_v[...])
    for c in np.ndindex(2, 2, 2):
        pos[c[0] + 1, c[1] + 1, c[2] + 1] = rows_out
        pos[c[0] + 1, c[1] + 1, c[2] + 1, 0:3, 0:64] = pos_v[c[0], c[1], :, c[2], :]
    pl.semaphore_wait(barrier, partners)
    halo = []
    for a, b, x, y in ((pos, pos, ps, pr), (emb, gemb, es, er)):
        copies = []
        for i, (s, src, dst) in enumerate(BOXES):
            start = box(a, [(lo + 1, hi + 1) for lo, hi in src]) if a is pos else box(a, src)
            copies.append(pltpu.make_async_remote_copy(src_ref=start, dst_ref=box(b, dst), send_sem=x.at[i], recv_sem=y.at[i], device_id=shifted(me, s, -1), device_id_type=MESH))
            copies[-1].start()
        halo.append(copies)
    for copy in local[3:]:
        copy.wait()
    place = dot_nt(places_of(rows_out), slots_of(rows_out, OWNERS[0][1])).astype(BF16)
    send1[...] = dot(place, emb_v[...].reshape(512, 256)).astype(BF16)
    rows = exchange(me, plane_partner, 16, 16, send1, recv1, s1, r1)
    projt[...] = (0.5 * jnp.transpose(proj_v[...]).astype(F32)).astype(BF16)
    half = 0.5 * bias_v[...]
    b1 = half.astype(BF16).astype(F32)
    b2 = (half - b1).astype(BF16).astype(F32)
    row8 = iota((8, 256), 0)
    biases = jnp.where(row8 == 0, b1, jnp.where(row8 == 1, b2, jnp.where(row8 == 2, half - b1 - b2, 0.0)))
    rwf = rw_v[...].astype(F32)
    ewf = ew_v[...].astype(F32).reshape(1, 256)
    rb[...] = jnp.transpose(jnp.concatenate([0.5 * rwf, biases, jnp.zeros((112, 256), F32)], axis=0)).astype(BF16)
    z8 = jnp.zeros((8, 256), F32)
    w2[...] = jnp.concatenate([0.5 * rwf * ewf, z8], axis=0).astype(BF16)
    ewc[...] = jnp.transpose(jnp.broadcast_to(ewf, (LANES, 256)))

    jl = iota((64, 64), 1)
    il = iota((64, 64), 0)
    upper_b = jnp.where(il < jl, 1.0, 0.0).astype(BF16)
    lower_b = jnp.where(jl < il, 1.0, 0.0).astype(BF16)
    ones_b = jnp.ones((64, LANES), BF16)
    lane = iota((64, LANES), 1)

    def pos_at(c):
        return jnp.where(iota((8, 64), 0) < 3, pos[c // 16, c // 4 % 4, c % 4][:, :64], 0.0)

    def prepare(b):
        a, code = blk[0, 0, b], blk[0, 1, b]
        off = [offs[d, code] for d in range(3)]
        ca = ((a // 4 + 1) * 4 + (a // 2) % 2 + 1) * 4 + a % 2 + 1
        cb = ca + (off[0] * 4 + off[1]) * 4 + off[2]
        plan[0, b] = ca
        plan[1, b] = cb
        sh = shift_rows(off, 64)
        pa, pb = pos_at(ca), pos_at(cb)
        pbs = pb + sh
        pat = jnp.transpose(pa)
        d2 = None
        for c in range(3):
            df = pbs[c:c + 1, :] - pat[:, c:c + 1]
            d2 = df * df if d2 is None else d2 + df * df
        keep = jnp.logical_and(d2 + 0.25 < 36.001, jnp.logical_or(code != 0, il < jl))
        keep = jnp.where(jnp.logical_and(keep, b < cnt[0]), 1.0, 0.0)
        keep_b = keep.astype(BF16)
        counts = dot(keep_b, ones_b)
        prefix = dot(keep_b, upper_b)
        start = dot(lower_b, counts.astype(BF16))
        rc[b, 0:64] = start
        rc[b, 64:128] = start + counts
        local = jnp.where(keep > 0.5, prefix, 255.0)
        hi = jnp.floor(start * (1.0 / 64.0)) * 64.0
        side = jnp.where(lane == 64, hi, jnp.where(lane == 65, start - hi, 0.0))
        zt = jnp.transpose(jnp.concatenate([local, side[:, 64:]], axis=1))[:72]
        ah = pa.astype(BF16).astype(F32)
        bh = pb.astype(BF16).astype(F32)
        far = jnp.concatenate([sh, jnp.zeros_like(sh)], axis=0)
        g1[b] = jnp.concatenate([zt, ah, pa - ah, jnp.zeros((8, 64), F32)], axis=0).astype(BF16)
        g2[b] = jnp.concatenate([bh, pb - bh, far], axis=0).astype(BF16)
        tot[b] = jnp.sum(keep).astype(jnp.int32)
    wait_all(halo[0])

    def prep_group(g, c):
        for u in range(8):
            prepare(g * 8 + u)
        return c

    lax.fori_loop(0, 4, prep_group, 0)
    at = 0
    for i, (s, owned) in enumerate(OWNERS):
        first = tuple(x + 2 * d + 1 for x, d in zip(owned[0], s))
        rows_out = pos[first]
        size = 64 * len(owned)
        places[at:at + size] = dot_nt(slots_of(rows_out, owned), places_of(rows_out)).astype(BF16)
        at += size
    wait_all(rows)
    held[...] = recv1[...]
    wait_all(halo[1])


def sinpi_cospi(theta):
    m = jnp.round(theta)
    f = theta - m
    z = f * f
    sn = f * (3.14159265 + z * (-5.16771278 + z * (2.55016404 + z * (-0.599264529 + z * (0.0821458866 + z * -0.00737043094)))))
    cs = 1.0 + z * (-4.93480220 + z * (4.05871213 + z * (-1.33526277 + z * (0.235330630 + z * (-0.0258068913 + z * 0.00192957431)))))
    sign = 1.0 - 2.0 * (m - 2.0 * jnp.floor(0.5 * m))
    return sn * sign, cs * sign


def pair_kernel(plan, cnt, tot, gemb, g1, g2, rc, projt, rb, w2, ewc, out, wt, acc, tab_b, tab_k, rest_b, rest_k):
    def project(g, c):
        for u in range(0, 8, 2):
            four = [gemb[plan[d, g * 8 + v]] for v in (u, u + 1) for d in range(2)]
            both = dot_nt(projt[...], jnp.concatenate(four, axis=0)).astype(BF16)
            wt[g * 8 + u] = both[:, :LANES]
            wt[g * 8 + u + 1] = both[:, LANES:]
        return c

    lax.fori_loop(0, (cnt[0] + 7) // 8, project, 0)

    def fill_block(b, c):
        n, m = c
        wide_chunks = (tot[b] + WIDE - LANES - 1) // WIDE

        def put(t, n):
            tab_b[n] = b
            tab_k[n] = t * WIDE
            return n + 1

        rest_b[m] = b
        rest_k[m] = wide_chunks * WIDE
        return lax.fori_loop(0, wide_chunks, put, n), m + jnp.where(tot[b] > wide_chunks * WIDE, 1, 0)

    n, m = lax.fori_loop(0, cnt[0], fill_block, (0, 0))
    for u in range(WIDE_GROUP):
        tab_b[n + u] = 0
        tab_k[n + u] = 1 << 20
    for u in range(GROUP):
        rest_b[m + u] = 0
        rest_k[m + u] = 1 << 20

    acc[...] = jnp.zeros_like(acc)
    halves = iota((8, LANES), 1) < 64

    def run(chunk, group, tab_b, tab_k, count):
        kl = iota((1, chunk), 1)
        sub = iota((8, chunk), 0)
        order = (sub + 1).astype(F32)
        ones_rows = jnp.where(sub < 3, 1.0, 0.0)

        def wide(x):
            return jnp.concatenate([x] * (chunk // LANES), axis=1)

        def chunk_group(g, c):
            R = range(group)
            bs = [tab_b[g * group + u] for u in R]
            ks = [(kl + tab_k[g * group + u]).astype(F32) for u in R]
            oh_i = []
            for u in R:
                hit = jnp.logical_and(ks[u] >= wide(rc[bs[u], 0:64]), ks[u] < wide(rc[bs[u], 64:128]))
                oh_i.append(jnp.where(hit, 1.0, 0.0).astype(BF16))
            got = [dot(g1[bs[u]], oh_i[u]) for u in R]
            oh_j = []
            for u in R:
                want = ks[u] - got[u][64:65] - got[u][65:66]
                oh_j.append(jnp.where(got[u][:64] == want, 1.0, 0.0).astype(BF16))
            gotb = [dot(g2[bs[u]], oh_j[u]) for u in R]
            info = []
            xs = []
            for u in R:
                sep = (gotb[u][:8] + gotb[u][8:16] + gotb[u][16:24]) - (got[u][72:80] + got[u][80:88])
                sq = sep * sep
                d2 = sq[0:1] + sq[1:2] + sq[2:3]
                s = jnp.sqrt(jnp.broadcast_to(d2, (8, chunk)) + 0.25) * (1.0 / 6.0)
                sn, cs = sinpi_cospi(order * s)
                e = jnp.where(s < 1.0, 1.0 - s * s, 0.0)
                info.append((sep, s, e, cs * order))
                x2 = jnp.concatenate([sn, ones_rows], axis=0).astype(BF16)
                xs.append(jnp.concatenate([oh_i[u], oh_j[u], x2, jnp.zeros((112, chunk), BF16)], axis=0))
            qs = [dot(jnp.concatenate([wt[bs[u]], rb[...]], axis=1), xs[u]) for u in R]
            hd = []
            us = []
            for u in R:
                q = qs[u]
                t = jnp.tanh(q)
                h = q + q * t
                d = (1.0 + t) + h * (1.0 - t)
                hd.append(d.astype(BF16))
                us.append(jnp.sum((h * wide(ewc[...])).reshape(32, 8, chunk), axis=0))
            rs = []
            for u in range(0, group, 2 if chunk == LANES else 1):
                both = dot(w2[...], jnp.concatenate(hd[u:u + 2], axis=1) if chunk == LANES else hd[u])
                rs += [both[:, :LANES], both[:, LANES:]] if chunk == LANES else [both]
            fs = []
            for u in R:
                sep, s, e, cn = info[u]
                terms = rs[u][:8] * cn * (np.pi * e * e) + us[u] * (-4.0 * s * e)
                ct = jnp.sum(terms, axis=0, keepdims=True)
                f = sep * (ct / (36.0 * s))
                fh = f.astype(BF16).astype(F32)
                fs.append(jnp.concatenate([fh, f - fh], axis=0).astype(BF16))
            for u in R:
                both = dot_nt(fs[u], xs[u][:128])
                part = both[:8] + both[8:]
                acc[plan[0, bs[u]]] += jnp.where(halves, part, 0.0)
                acc[plan[1, bs[u]]] += jnp.where(halves, 0.0, part)
            return c

        lax.fori_loop(0, (count + group - 1) // group, chunk_group, 0)

    run(WIDE, WIDE_GROUP, tab_b, tab_k, n)
    run(LANES, GROUP, rest_b, rest_k, m)
    out[...] = (acc[...] - jnp.roll(acc[...], 64, axis=2)).reshape(4, 4, 4, 8, LANES)


def return_kernel(fsum, pos_in, vel_in, held, places, forces, moved, embeds, pos_v, vel_v, landed, lhs, send1, recv1, send2, recv2, esend, erecv, loc, fs, fr, s1, r1, s2, r2, s3, r3):
    me = position()
    barrier = pltpu.get_barrier_semaphore()
    partners = greet(me, -1, True)
    local = []
    for i, (x, y) in enumerate(((pos_in, pos_v), (vel_in, vel_v))):
        local.append(pltpu.make_async_copy(x, y, loc.at[i]))
        local[-1].start()
    lhs[...] = jnp.zeros_like(lhs)
    at = 0
    for i, (s, owned) in enumerate(OWNERS):
        for c in owned:
            part = fsum[tuple(x + 2 * d + 1 for x, d in zip(c, s))]
            if i % 2:
                part = pltpu.roll(part, 4, 0)
            lhs[8 * (i // 2):8 * (i // 2) + 8, at:at + 64] = part[:, :64]
            at += 64
    wait_all(local)
    for j, c in enumerate(OWNERS[0][1]):
        velocity = vel_v[c[0], c[1], :, c[2], :]
        lhs[80:83, 64 * j:64 * j + 64] = pos_v[c[0], c[1], :, c[2], :] + 0.5 * velocity
        lhs[84:87, 64 * j:64 * j + 64] = velocity
    rows = dot(lhs[...].astype(BF16), places[...])
    send1[...] = jnp.transpose(jnp.concatenate([rows, jnp.zeros((32, 256), F32)], axis=0)).astype(BF16)
    pl.semaphore_wait(barrier, partners)
    first = exchange(me, plane_partner, 16, 16, send1, recv1, s1, r1)
    back = []
    for i, (s, own, ghost) in enumerate(BOXES):
        copy = pltpu.make_async_remote_copy(src_ref=box(fsum, ghost), dst_ref=box(landed.at[i], own), send_sem=fs.at[i], recv_sem=fr.at[i], device_id=shifted(me, s, 1), device_id_type=MESH)
        copy.start()
        back.append(copy)
    out = iota((256, 256), 0)
    source = iota((256, 256), 1)
    want = ((out // 2) % 16) * 16 + (out // 32) * 2 + out % 2
    perm2 = jnp.where(source == want, 1.0, 0.0).astype(BF16)
    esend[...] = dot(perm2, held[...]).astype(BF16)
    rows_sent = exchange(me, line_partner, 8, 32, esend, erecv, s3, r3)
    want = (out % 16) * 16 + (out // 32) * 2 + (out // 16) % 2
    perm = jnp.where(source == want, 1.0, 0.0).astype(BF16)
    wait_all(first)
    send2[...] = dot(perm, recv1[...]).astype(BF16)
    last = exchange(me, line_partner, 8, 32, send2, recv2, s2, r2)
    wait_all(back)
    for c in np.ndindex(2, 2, 2):
        total = fsum[c[0] + 1, c[1] + 1, c[2] + 1]
        for i, (s, own, ghost) in enumerate(BOXES):
            if all(lo <= x < hi for x, (lo, hi) in zip(c, own)):
                total = total + landed[i, c[0], c[1], c[2]]
        forces[c[0], c[1], c[2]] = total
    wait_all(rows_sent)
    embeds[...] = erecv[...]
    wait_all(last)
    for h in range(2):
        by_source = jnp.concatenate([recv2[32 * g + 16 * h:32 * g + 16 * h + 16] for g in range(8)], axis=0)
        by_source = jnp.transpose(by_source.astype(F32))
        sums = [None, None]
        for i, (s, _) in enumerate(OWNERS):
            part = turned(by_source[8 * (i // 2):8 * (i // 2) + 8], s)
            sums[i % 2] = part if sums[i % 2] is None else sums[i % 2] + part
        total = sums[0] + pltpu.roll(sums[1], 4, 0)
        base = by_source[80:88]
        moved[16 * h:16 * h + 8] = base + 0.25 * total
        moved[16 * h + 8:16 * h + 16] = pltpu.roll(base, 4, 0) + 0.5 * total


def finish_kernel(forces, moved, embeds, forces_out, motion_out, embeds_out):
    for c in np.ndindex(2, 2, 2):
        forces_out[c[0], c[1], :, c[2], :] = forces[c[0], c[1], c[2]][:3, :64]
    for v in range(6):
        for h in range(2):
            at = 16 * h + 8 * (v // 3) + v % 3
            motion_out[v, h:h + 1, :] = moved[at:at + 1, :]
    embeds_out[...] = embeds[...].reshape(128, 2, 256)


def per_device(positions, velocity, atom_embed, embed_proj, radial_weight, latent_bias, energy_weight, block_list, block_count, move_slot, move_dest):
    any_, vmem, smem, hbm = (pl.BlockSpec(memory_space=m) for m in (pl.ANY, pltpu.VMEM, pltpu.SMEM, pltpu.HBM))
    dma = pltpu.SemaphoreType.DMA
    array = jax.ShapeDtypeStruct
    pos_rows, vel_rows = (x.transpose(0, 1, 3, 2, 4) for x in (positions, velocity))
    dest_row = move_dest.reshape(1, 128)
    spaces = pltpu.VMEM((2, 2, 3, 2, 64), F32)
    gemb, held, g1, g2, rc, projt, rb, w2, ewc, places, plan, tot = pl.pallas_call(
        halo_kernel,
        out_shape=(
            array((4, 4, 4, 64, 256), BF16),
            array((256, 256), BF16),
            array((32, 96, 64), BF16),
            array((32, 32, 64), BF16),
            array((32, 128, LANES), F32),
            array((256, 256), BF16),
            array((256, 128), BF16),
            array((16, 256), BF16),
            array((256, LANES), F32),
            array((N_ROWS, 256), BF16),
            array((2, 32), jnp.int32),
            array((32,), jnp.int32),
        ),
        in_specs=[hbm] * 9 + [smem],
        out_specs=(any_,) + (vmem,) * 9 + (smem,) * 2,
        scratch_shapes=[
            pltpu.VMEM((4, 4, 4, 8, LANES), F32),
            spaces,
            pltpu.VMEM((2, 2, 2, 64, 256), BF16),
            pltpu.VMEM((1, 128), jnp.int32),
            pltpu.VMEM((1, 128), jnp.int32),
            pltpu.VMEM((256, 256), BF16),
            pltpu.VMEM((8, 256), BF16),
            pltpu.VMEM((1, 256), F32),
            pltpu.VMEM((256,), BF16),
            pltpu.VMEM((256, 256), BF16),
            pltpu.VMEM((256, 256), BF16),
            pltpu.SMEM((1, 2, 32), jnp.int32),
            pltpu.SMEM((3, 16), jnp.int32),
        ]
        + [dma((10,))] + [dma((N_BOX,))] * 4 + [dma((16,))] * 2,
        compiler_params=pltpu.CompilerParams(collective_id=0, has_side_effects=True, vmem_limit_bytes=16 * 1024 * 1024),
        name="halo",
    )(*(pltpu.with_memory_space_constraint(x, pltpu.HBM) for x in (pos_rows, atom_embed, move_slot, dest_row, block_list, embed_proj, radial_weight, latent_bias.reshape(1, 256), energy_weight)), block_count)
    fsum = pl.pallas_call(
        pair_kernel,
        out_shape=array((4, 4, 4, 8, LANES), F32),
        in_specs=[smem] * 3 + [vmem] * 8,
        out_specs=vmem,
        scratch_shapes=[
            pltpu.VMEM((32, 256, 128), BF16),
            pltpu.VMEM((64, 8, LANES), F32),
            pltpu.SMEM((MAXCH + WIDE_GROUP,), jnp.int32),
            pltpu.SMEM((MAXCH + WIDE_GROUP,), jnp.int32),
            pltpu.SMEM((40 + GROUP,), jnp.int32),
            pltpu.SMEM((40 + GROUP,), jnp.int32),
        ],
        compiler_params=pltpu.CompilerParams(vmem_limit_bytes=24 * 1024 * 1024),
        name="pairs",
    )(plan, block_count, tot, gemb.reshape(64, 64, 256), g1, g2, rc, projt, rb, w2, ewc)
    raw = pl.pallas_call(
        return_kernel,
        out_shape=(array((2, 2, 2, 8, LANES), F32), array((32, LANES), F32), array((256, 256), BF16)),
        in_specs=[vmem] + [hbm] * 2 + [vmem] * 2,
        out_specs=(vmem,) * 3,
        scratch_shapes=[spaces, spaces, pltpu.VMEM((N_BOX, 2, 2, 2, 8, LANES), F32), pltpu.VMEM((96, N_ROWS), F32)]
        + [pltpu.VMEM((256, LANES), BF16)] * 4
        + [pltpu.VMEM((256, 256), BF16)] * 2
        + [dma((2,))] + [dma((N_BOX,))] * 2 + [dma((16,))] * 2 + [dma((8,))] * 4,
        compiler_params=pltpu.CompilerParams(collective_id=1, has_side_effects=True, vmem_limit_bytes=16 * 1024 * 1024),
        name="give_back",
    )(fsum, *(pltpu.with_memory_space_constraint(x, pltpu.HBM) for x in (pos_rows, vel_rows)), held, places)
    forces, motion, embeds = pl.pallas_call(
        finish_kernel,
        out_shape=(array((2, 2, 3, 2, 64), F32), array((6, 2, 128), F32), array((128, 2, 256), BF16)),
        in_specs=[vmem] * 3,
        out_specs=(vmem,) * 3,
        compiler_params=pltpu.CompilerParams(vmem_limit_bytes=8 * 1024 * 1024),
        name="finish",
    )(*raw)
    return forces.transpose(0, 1, 3, 2, 4), motion.transpose(2, 1, 0), embeds


def solution(mesh):
    placed = (
        P("gx", "gy", "gz", None, None),
        P("gx", "gy", "gz", None, None),
        P("gx", "gy", "gz", None, None),
        P(),
        P(),
        P(),
        P(),
        P(("gx", "gy", "gz"), None, None),
        P(("gx", "gy", "gz")),
        P(("gx", "gy", "gz"), None),
        P(("gx", "gy", "gz"), None),
    )
    return jax.shard_map(
        per_device,
        mesh=mesh,
        in_specs=placed,
        out_specs=(
            P("gx", "gy", "gz", None, None),
            P(("gx", "gy", "gz"), None, None),
            P(("gx", "gy", "gz"), None, None),
        ),
        check_vma=False,
    )
```
